32 devices in a mesh: groups: 2 (over y), mesh: 4 (over z), band: 2 (over x), width: 2 (over core).
Axes of the slice: x: 2, y: 2, z: 4, core: 2. Of those that a mesh axis runs over, the one named last changes fastest.
Arguments:
- grid_latent: bfloat16 [8192, 512], P(('groups', 'mesh', 'band')), parts along dimension 0, may hold values from -6 to 6
- mesh_latent: bfloat16 [5120, 512], P(('groups', 'mesh', 'band')), parts along dimension 0, may hold values from -6 to 6
- grid_edge: bfloat16 [12288, 512], P(('groups', 'mesh', 'band')), parts along dimension 0, may hold values from -6 to 6
- mesh_edge: bfloat16 [12288, 512], P(('groups', 'mesh', 'band')), parts along dimension 0, may hold values from -6 to 6
- encoder_slot: int32 [12288], P(('groups', 'mesh', 'band')), parts along dimension 0, may hold values from 0 to 639, as said below
- encoder_target: int32 [12288], P(('groups', 'mesh', 'band')), parts along dimension 0, may hold values from 0 to 319
- halo_down: int32 [1024], P(('groups', 'mesh', 'band')), parts along dimension 0, may hold values from 0 to 511
- halo_up: int32 [1024], P(('groups', 'mesh', 'band')), parts along dimension 0, may hold values from 0 to 511
- send_lists: int32 [16, 8, 8], P(('groups', 'mesh', 'band')), parts along dimension 0, may hold values from -1 to 319, as said below
- mesh_slot: int32 [12288], P(('groups', 'mesh', 'band')), parts along dimension 0, may hold values from 0 to 63, as said below
- mesh_target: int32 [12288], P(('groups', 'mesh', 'band')), parts along dimension 0, may hold values from 0 to 319
- edge_mats: bfloat16 [3, 3, 512, 512], P(None, None, 'mesh', 'width'), may hold values from -0.15625 to 0.15625
- node_mats: bfloat16 [3, 2, 512, 512], P(None, None, 'mesh', 'width'), may hold values from -0.1875 to 0.1875
- edge_back: bfloat16 [3, 512, 512], P(None, 'width', 'mesh'), may hold values from -0.25 to 0.25
- node_back: bfloat16 [3, 512, 512], P(None, 'width', 'mesh'), may hold values from -0.25 to 0.25
Outputs:
- mesh_out: bfloat16 [5120, 512], P(('groups', 'mesh', 'band')), parts along dimension 0
The draws below stay inside these ranges and needn't reach their ends.
There are 2 independent parts, one for each index of `groups`. The reference program is written for one: setup_inputs(seed, part) draws one part's arguments, and reference() takes and returns one part's arrays. A program takes and returns all parts, laid end to end along the dimension named above; an argument that names none is the same for every part. Nothing has to cross between parts.
Inputs may be any that keep to these rules, and one draw needn't show every extreme that they name: `encoder_slot`: for an edge of device d (rows d * 768 to (d + 1) * 768 - 1): a value below 512 is one of d's own grid nodes; 512 + j with j < 64 names entry j of the halo_up list of device d - 1; 576 + j names entry j of the halo_down list of device d + 1. Device 0 names nothing of a lower and the last device nothing of an upper device; every entry of an existing neighbour's list is named by some edge of d. In each send_lists[p, q, :] the live entries (0 or more) come first, the rest are -1. Device p has 8 live entries for itself and for the four devices at most two indices away along mesh+band, counted around the loop, and between 2 and 4 for every other device. `mesh_slot`: for an edge of device q, slot s names entry s % 8 of send_lists[s // 8, q, :], which is always live; every live entry sent to q is named by some edge of q.
All inputs are finite; a program needn't handle non-finite values.
Results may differ from the reference program's by a relative error of at most 0.02.
Values may be sent and summed in bfloat16 or wider, within the bound.
No kernel may reach another device: no remote copies, remote signals or barrier semaphores. Data moves between devices by JAX's collectives and lax.ppermute only.
A program may use at most 64 MiB of HBM per device.

```python
import jax
import jax.numpy as jnp
from jax import lax

D = 512
HID = 512
MN_DEV = 320
GN_DEV = 512
HALO = 64
EG_DEV = 768
ME_DEV = 768
CAP = 8
LAYERS = 2
NPART = 8
HPART = 256
BLOCKS = 3
MESH_NODES = 2560
GRID_NODES = 4096
G2M_EDGES = 6144
M2M_EDGES = 6144
N_WIDTH = 2


def link_counts(key):
    key = jax.random.fold_in(key, 11)
    far_counts = jax.random.randint(key, (NPART, NPART), CAP // 4, CAP // 2 + 1)
    source = jnp.arange(NPART, dtype=jnp.int32)[:, None]
    target = jnp.arange(NPART, dtype=jnp.int32)[None, :]
    distance = jnp.abs(source - target)
    distance = jnp.minimum(distance, NPART - distance)
    return jnp.where(distance <= 2, CAP, far_counts).astype(jnp.int32)


def shuffled(key, values):
    row_count = values.shape[0]
    col_count = values.shape[1]
    scores = jax.random.randint(key, (row_count, col_count), 0, 2 ** 18) * col_count
    scores = scores + jnp.arange(col_count, dtype=jnp.int32)[None, :]
    ranking = jnp.argsort(scores, axis=1)
    return jnp.take_along_axis(values, ranking, axis=1)


def draw_send_lists(key, part):
    counts = link_counts(key)
    key = jax.random.fold_in(key, 3)
    node_pick = jax.random.randint(key, (NPART, NPART, CAP), 0, MN_DEV)
    slot_ids = jnp.arange(CAP, dtype=jnp.int32)[None, None, :]
    return jnp.where(slot_ids < counts[:, :, None], node_pick, -1).astype(jnp.int32)


def draw_mesh_slot(key, part):
    counts = link_counts(key)
    key = jax.random.fold_in(key, 5)
    first_key, second_key = jax.random.split(key)
    is_live = jnp.arange(CAP, dtype=jnp.int32)[None, None, :] < counts.T[:, :, None]
    flat_live = is_live.reshape(NPART, NPART * CAP).astype(jnp.int32)
    live_order = jnp.argsort(1 - flat_live, axis=1, stable=True).astype(jnp.int32)
    live_count = jnp.sum(flat_live, axis=1)
    extra_pick = jax.random.randint(first_key, (NPART, ME_DEV), 0, live_count[:, None])
    edge_pos = jnp.arange(ME_DEV, dtype=jnp.int32)[None, :]
    position = jnp.where(edge_pos < live_count[:, None], edge_pos, extra_pick)
    chosen = jnp.take_along_axis(live_order, position, axis=1)
    return shuffled(second_key, chosen).reshape(-1).astype(jnp.int32)


def draw_encoder_slot(key, part):
    key = jax.random.fold_in(key, 7)
    first_key, second_key = jax.random.split(key)
    device_id = jnp.arange(NPART, dtype=jnp.int32)[:, None]
    edge_pos = jnp.arange(EG_DEV, dtype=jnp.int32)[None, :]
    own_pick = jax.random.randint(first_key, (NPART, EG_DEV), 0, GN_DEV)
    halo_pick = GN_DEV + edge_pos
    from_lower = (edge_pos < HALO) & (device_id > 0)
    from_upper = (edge_pos >= HALO) & (edge_pos < 2 * HALO) & (device_id < NPART - 1)
    chosen = jnp.where(from_lower | from_upper, halo_pick, own_pick)
    return shuffled(second_key, chosen).reshape(-1).astype(jnp.int32)


def plant(values, own_key, low, high):
    dims = values.shape
    place = [jax.random.randint(jax.random.fold_in(own_key, axis), (), 0, dims[axis]) for axis in range(len(dims))]
    values = values.at[tuple(place)].set(low)
    longest = dims.index(max(dims))
    place[longest] = (place[longest] + 1) % dims[longest]
    return values.at[tuple(place)].set(high)


def level_of(stream_key, shape, shards, smallest, top_value):
    gain, own = 1.0, jax.random.fold_in(stream_key, 6)
    for dim, parts in shards:
        heights = jnp.exp(jax.random.uniform(jax.random.fold_in(own, dim), (parts,), jnp.float32, smallest / len(shards), top_value / len(shards)))
        gain = gain * jnp.repeat(heights, shape[dim] // parts).reshape([-1 if axis == dim else 1 for axis in range(len(shape))])
    return gain


def centred(rng, extent, deviation, reach, cuts=(), held_as=jnp.bfloat16):
    gain = level_of(rng, extent, cuts, -0.22, 0.18) if cuts else 1.0
    entries = jax.random.normal(rng, extent, jnp.float32) * deviation * gain
    return jnp.minimum(jnp.maximum(entries, -reach), reach).astype(held_as)


def setup_inputs(seed: int = 0, part: int = 0) -> dict:
    seeds = jax.random.split(jax.random.key(seed), 16)
    part_keys = jax.random.split(jax.random.fold_in(seeds[15], part), 16)
    return {
        "grid_latent": centred(part_keys[0], (GRID_NODES, D), 1.0, 6.0, ((0, 8),)),
        "mesh_latent": centred(part_keys[1], (MESH_NODES, D), 1.0, 6.0, ((0, 8),)),
        "grid_edge": centred(part_keys[2], (G2M_EDGES, D), 1.0, 6.0, ((0, 8),)),
        "mesh_edge": centred(part_keys[3], (M2M_EDGES, D), 1.0, 6.0, ((0, 8),)),
        "encoder_slot": draw_encoder_slot(jax.random.fold_in(jax.random.fold_in(seeds[15], part), 71), part),
        "encoder_target": plant(jax.random.randint(part_keys[5], (G2M_EDGES,), 0, MN_DEV), jax.random.fold_in(part_keys[5], 1), 0, MN_DEV - 1).astype(jnp.int32),
        "halo_down": plant(jax.random.randint(part_keys[6], (NPART * HALO,), 0, GN_DEV), jax.random.fold_in(part_keys[6], 1), 0, GN_DEV - 1).astype(jnp.int32),
        "halo_up": plant(jax.random.randint(part_keys[7], (NPART * HALO,), 0, GN_DEV), jax.random.fold_in(part_keys[7], 1), 0, GN_DEV - 1).astype(jnp.int32),
        "send_lists": draw_send_lists(jax.random.fold_in(jax.random.fold_in(seeds[15], part), 71), part),
        "mesh_slot": draw_mesh_slot(jax.random.fold_in(jax.random.fold_in(seeds[15], part), 71), part),
        "mesh_target": plant(jax.random.randint(part_keys[10], (M2M_EDGES,), 0, MN_DEV), jax.random.fold_in(part_keys[10], 1), 0, MN_DEV - 1).astype(jnp.int32),
        "edge_mats": centred(seeds[11], (BLOCKS, 3, D, HID), (3 * D) ** -0.5, 0.15625, ((2, 4), (3, 2))),
        "node_mats": centred(seeds[12], (BLOCKS, 2, D, HID), (2 * D) ** -0.5, 0.1875, ((2, 4), (3, 2))),
        "edge_back": centred(seeds[13], (BLOCKS, HID, D), HID ** -0.5, 0.25, ((1, 2), (2, 4))),
        "node_back": centred(seeds[14], (BLOCKS, HID, D), HID ** -0.5, 0.25, ((1, 2), (2, 4))),
    }


def normalize(total):
    row_mean = lax.optimization_barrier(jnp.mean(total, axis=1, keepdims=True))
    row_meansq = lax.optimization_barrier(jnp.mean(total * total, axis=1, keepdims=True))
    return (total - row_mean) * lax.rsqrt(row_meansq - row_mean * row_mean + 1e-05)

def grouped(hidden, back):
    total = jnp.zeros((hidden.shape[0], back.shape[1]), jnp.float32)
    for group_id in range(N_WIDTH):
        offset = group_id * HPART
        term = jnp.dot(hidden[:, offset:offset + HPART], back[offset:offset + HPART], preferred_element_type=jnp.float32)
        term = lax.optimization_barrier(term.astype(jnp.bfloat16))
        total = total + term.astype(jnp.float32)
    return total

def block(senders, node_rows, edge_rows, send_ids, target_ids, edge_mats, node_mats, edge_back, node_back):
    send_proj = jnp.dot(senders, edge_mats[0], preferred_element_type=jnp.float32).astype(jnp.bfloat16)
    recv_proj = jnp.dot(node_rows, edge_mats[1], preferred_element_type=jnp.float32)
    preact = jnp.dot(edge_rows, edge_mats[2], preferred_element_type=jnp.float32)
    preact = preact + send_proj[send_ids].astype(jnp.float32) + recv_proj[target_ids]
    edge_hidden = jax.nn.silu(preact).astype(jnp.bfloat16)
    edge_norm = normalize(grouped(edge_hidden, edge_back))
    message = edge_norm.astype(jnp.bfloat16)
    edge_next = (edge_rows.astype(jnp.float32) + edge_norm).astype(jnp.bfloat16)
    incoming = jax.ops.segment_sum(message.astype(jnp.float32), target_ids, num_segments=node_rows.shape[0])
    incoming = incoming.astype(jnp.bfloat16)
    node_pre = jnp.dot(node_rows, node_mats[0], preferred_element_type=jnp.float32)
    node_pre = node_pre + jnp.dot(incoming, node_mats[1], preferred_element_type=jnp.float32)
    node_hidden = jax.nn.silu(node_pre).astype(jnp.bfloat16)
    node_next = (node_rows.astype(jnp.float32) + normalize(grouped(node_hidden, node_back))).astype(jnp.bfloat16)
    return (node_next, edge_next)

def reference(grid_latent, mesh_latent, grid_edge, mesh_edge, encoder_slot, encoder_target, halo_down, halo_up, send_lists, mesh_slot, mesh_target, edge_mats, node_mats, edge_back, node_back):
    enc_ids = jnp.arange(G2M_EDGES, dtype=jnp.int32)
    device_id = enc_ids // EG_DEV
    lower_dev = jnp.maximum(device_id - 1, 0)
    upper_dev = jnp.minimum(device_id + 1, NPART - 1)
    own_rows = device_id * GN_DEV + jnp.minimum(encoder_slot, GN_DEV - 1)
    lower_pos = jnp.clip(lower_dev * HALO + encoder_slot - GN_DEV, 0, NPART * HALO - 1)
    upper_pos = jnp.clip(upper_dev * HALO + encoder_slot - GN_DEV - HALO, 0, NPART * HALO - 1)
    from_lower = lower_dev * GN_DEV + halo_up[lower_pos]
    from_upper = upper_dev * GN_DEV + halo_down[upper_pos]
    grid_send = jnp.where(encoder_slot < GN_DEV, own_rows, jnp.where(encoder_slot < GN_DEV + HALO, from_lower, from_upper)).astype(jnp.int32)
    grid_recv = (device_id * MN_DEV + encoder_target).astype(jnp.int32)
    mesh_ids = jnp.arange(M2M_EDGES, dtype=jnp.int32)
    holder = mesh_ids // ME_DEV
    source = mesh_slot // CAP
    mesh_send = (source * MN_DEV + send_lists[source, holder, mesh_slot % CAP]).astype(jnp.int32)
    mesh_recv = (holder * MN_DEV + mesh_target).astype(jnp.int32)
    node_rows, unused = block(grid_latent, mesh_latent, grid_edge, grid_send, grid_recv, edge_mats[0], node_mats[0], edge_back[0], node_back[0])
    edge_rows = mesh_edge
    for block_id in range(1, LAYERS + 1):
        node_rows, edge_rows = block(node_rows, node_rows, edge_rows, mesh_send, mesh_recv, edge_mats[block_id], node_mats[block_id], edge_back[block_id], node_back[block_id])
    return node_rows
```

```python
import functools

import jax
import jax.numpy as jnp
from jax import lax
from jax.experimental import pallas as pl
from jax.experimental.pallas import tpu as pltpu
from jax.sharding import PartitionSpec as P

BF = jnp.bfloat16
F32 = jnp.float32
ROWS = 256
SWAP = [(0, 1), (1, 0)]
PARAMS = pltpu.CompilerParams(vmem_limit_bytes=32 * 2**20)


def dot(a, b):
    return jnp.dot(a, b, preferred_element_type=F32)


def silu(v):
    return v / (1.0 + jnp.exp(-v))


def normalize(total):
    mean = jnp.mean(total, axis=1, keepdims=True)
    meansq = jnp.mean(total * total, axis=1, keepdims=True)
    return (total - mean) * lax.rsqrt(meansq - mean * mean + 1e-05)


def hot_columns(ids, count):
    spots = lax.broadcasted_iota(jnp.int32, (ids.shape[0], count), 1)
    return jnp.where(spots == ids, 1.0, 0.0).astype(BF)


def hot_rows(ids, count):
    spots = lax.broadcasted_iota(jnp.int32, (count, ids.shape[1]), 0)
    return jnp.where(spots == ids, 1.0, 0.0).astype(BF)


def call(body, outs, scratch, *args):
    return pl.pallas_call(
        body,
        out_shape=outs,
        scratch_shapes=scratch,
        compiler_params=PARAMS,
    )(*args)


def shaped(*dims):
    return jax.ShapeDtypeStruct(dims, BF)


def cut_body(plan, em, nm, eb, nb, *outs):
    index = {"quarter": 2 * lax.axis_index("groups") + lax.axis_index("band"), "x": lax.axis_index("band"), "y": lax.axis_index("groups")}
    for (block, kind, split, rows), out in zip(plan, outs):
        part = index[split]
        first = pl.ds(pl.multiple_of(part * rows, rows), rows)
        low = pl.ds(pl.multiple_of(part * 2 * rows, rows), rows)
        high = pl.ds(pl.multiple_of(part * 2 * rows + rows, rows), rows)
        spot = 0
        for letter, mats, back in (("e", em, eb), ("n", nm, nb)):
            if letter not in kind:
                continue
            for m in range(mats.shape[1]):
                out[spot] = mats[block, m, first, :]
                spot += 1
            width = back.shape[2]
            out[spot, :, 0:width] = back[block, low, :]
            out[spot, :, width:] = back[block, high, :]
            spot += 1


def put(src, zs, part, rows, half, kind, weights):
    for k, z in enumerate(zs):
        spot = 0
        for letter, mats, back in (("e", weights.get("em"), weights.get("eb")), ("n", weights.get("nm"), weights.get("nb"))):
            if letter not in kind:
                continue
            count = mats.shape[0] // mats.shape[1]
            depth = mats.shape[1]
            cols = src.shape[-1]
            lanes = cols // 2
            for m in range(count):
                at = pl.multiple_of(m * depth + z * lanes + part * rows, rows)
                mats[pl.ds(at, rows), half * cols : (half + 1) * cols] = src[k, spot]
                spot += 1
            for j in range(2):
                at = pl.multiple_of(half * cols + part * 2 * rows + j * rows, rows)
                back[pl.ds(at, rows), pl.ds(pl.multiple_of(z * lanes, lanes), lanes)] = src[
                    k, spot, :, j * lanes : (j + 1) * lanes
                ]
            spot += 1


def put_own(block, raws, half, kind, weights):
    z = lax.axis_index("mesh")
    for letter, mats, back in (("e", weights.get("em"), weights.get("eb")), ("n", weights.get("nm"), weights.get("nb"))):
        if letter not in kind:
            continue
        raw_mats, raw_back = raws[letter]
        depth, cols = raw_mats.shape[2:]
        for m in range(raw_mats.shape[1]):
            at = pl.multiple_of(m * mats.shape[1] + z * depth, depth)
            mats[pl.ds(at, depth), half * cols : (half + 1) * cols] = raw_mats[block, m]
        back[half * cols : (half + 1) * cols, pl.ds(pl.multiple_of(z * depth, depth), depth)] = raw_back[block]


def assemble(block, kind, split, rows, refs, weights):
    count = lax.axis_size("mesh")
    z = lax.axis_index("mesh")
    zs = [lax.rem(z + count - k, count) for k in range(1, count)]
    x, y = lax.axis_index("band"), lax.axis_index("groups")
    parts = {
        "quarter": [2 * y + x, 2 * y + 1 - x, 2 * (1 - y) + x, 2 * (1 - y) + 1 - x],
        "x": [x, 1 - x],
        "y": [y, 1 - y],
    }[split]
    for half, (raws, arrays) in enumerate(refs):
        put_own(block, raws, half, kind, weights)
        for part, src in zip(parts, arrays):
            put(src, zs, part, rows, half, kind, weights)


class Parts:
    def __init__(self, block, kind, split, rows, own, other, arrays, swapped):
        self.block, self.kind, self.split, self.rows = block, kind, split, rows
        self.operands = []
        for raws, got in ((own, arrays), (other, swapped)):
            for letter in kind:
                self.operands += list(raws[letter])
            self.operands += got

    def scratch(self, hidden, depth):
        found = []
        if "e" in self.kind:
            found += [pltpu.VMEM((3 * depth, hidden), BF), pltpu.VMEM((hidden, depth), BF)]
        if "n" in self.kind:
            found += [pltpu.VMEM((2 * depth, hidden), BF), pltpu.VMEM((hidden, depth), BF)]
        return found

    def load(self, operands, scratch):
        weights = dict(zip([name for letter in self.kind for name in (letter + "m", letter + "b")], scratch))
        each = len(operands) // 2
        refs = []
        for half in range(2):
            mine = list(operands[half * each : (half + 1) * each])
            raws = {}
            for letter in self.kind:
                raws[letter] = (mine.pop(0), mine.pop(0))
            refs.append((raws, mine))
        assemble(self.block, self.kind, self.split, self.rows, refs, weights)
        return weights


class Whole:
    def __init__(self, kind, arrays):
        self.kind = kind
        self.operands = arrays

    def scratch(self, hidden, depth):
        return []

    def load(self, operands, scratch):
        return dict(zip([name for letter in self.kind for name in (letter + "m", letter + "b")], operands))


def pack_body(rows, ids, out):
    out[...] = dot(hot_columns(ids[...], rows.shape[0]), rows[...]).astype(BF)


def sender_body(grid, low, high, nodes, slots, targets, out):
    table = jnp.concatenate([grid[...], low[...], high[...]], axis=0)
    depth = grid.shape[1]
    for at in range(0, out.shape[0], ROWS):
        rows = slice(at, at + ROWS)
        out[rows, 0:depth] = dot(hot_columns(slots[rows, :], table.shape[0]), table).astype(BF)
        out[rows, depth:] = dot(hot_columns(targets[rows, :], nodes.shape[0]), nodes[...]).astype(BF)


def edge_tail(pre, back, message, rows):
    total = dot(silu(pre).astype(BF), back[...])
    normed = normalize(total)
    message[rows, :] = normed.astype(BF)
    return normed


def node_tail(nodes, incoming, weights):
    depth = nodes.shape[1]
    pre = dot(nodes[...], weights["nm"][0:depth, :]) + dot(incoming, weights["nm"][depth:, :])
    total = dot(silu(pre).astype(BF), weights["nb"][...])
    return (nodes[...].astype(F32) + normalize(total)).astype(BF)


def first_edges_body(pack, count, gathered, edges, ids, *refs):
    operands, rest = refs[:count], refs[count:]
    out, message, scratch = rest[0], rest[1], rest[2:]
    weights = pack.load(operands, scratch)
    both = gathered.shape[1]
    for at in range(0, edges.shape[0], ROWS):
        rows = slice(at, at + ROWS)
        pre = dot(gathered[rows, :], weights["em"][0:both, :]) + dot(edges[rows, :], weights["em"][both:, :])
        edge_tail(pre, weights["eb"], message, rows)
    out[...] = dot(hot_rows(ids[...], out.shape[0]), message[...]).astype(BF)


def nodes_body(pack, count, nodes, incoming, lists, *refs):
    operands, rest = refs[:count], refs[count:]
    out, packed, scratch = rest[0], rest[1], rest[2:]
    weights = pack.load(operands, scratch)
    out[...] = node_tail(nodes, incoming[...], weights)
    packed[...] = dot(hot_columns(lists[...], nodes.shape[0]), out[...]).astype(BF)


def block_body(pack, count, last, senders, nodes, edges, slots, targets, ids, lists, *refs):
    operands, rest = refs[:count], refs[count:]
    if last:
        out, rest = rest[0], rest[1:]
    else:
        out, packed, edge_next, rest = rest[0], rest[1], rest[2], rest[3:]
    message, table, scratch = rest[0], rest[1], rest[2:]
    weights = pack.load(operands, scratch)
    depth = nodes.shape[1]
    sent = senders.shape[0]
    em = weights["em"]
    table[0:sent, :] = dot(senders[...], em[0:depth, :]).astype(BF)
    table[sent:, :] = dot(nodes[...], em[depth : 2 * depth, :]).astype(BF)
    for at in range(0, edges.shape[0], ROWS):
        rows = slice(at, at + ROWS)
        pre = dot(edges[rows, :], em[2 * depth :, :])
        pre = pre + dot(hot_columns(slots[rows, :], sent), table[0:sent, :])
        pre = pre + dot(hot_columns(targets[rows, :], nodes.shape[0]), table[sent:, :])
        normed = edge_tail(pre, weights["eb"], message, rows)
        if not last:
            edge_next[rows, :] = (edges[rows, :].astype(F32) + normed).astype(BF)
    incoming = dot(hot_rows(ids[...], nodes.shape[0]), message[...]).astype(BF)
    out[...] = node_tail(nodes, incoming, weights)
    if not last:
        packed[...] = dot(hot_columns(lists[...], nodes.shape[0]), out[...]).astype(BF)


def spread(chunk, split):
    count = lax.axis_size("mesh")
    turned = [lax.ppermute(chunk, "mesh", [(i, (i + k) % count) for i in range(count)]) for k in range(1, count)]
    own = jnp.stack(turned)
    if split == "x":
        return [own, lax.ppermute(own, "band", SWAP)]
    if split == "y":
        return [own, lax.ppermute(own, "groups", SWAP)]
    return [
        own,
        lax.ppermute(own, "band", SWAP),
        lax.ppermute(own, "groups", SWAP),
        lax.ppermute(own, ("groups", "band"), [(0, 3), (3, 0), (1, 2), (2, 1)]),
    ]


def swap_width(array):
    return lax.ppermute(array, "width", SWAP)


def weights_by_parts(edge_mats, node_mats, edge_back, node_back):
    depth = edge_mats.shape[2]
    quarter, halved = depth // 4, depth // 2
    plan = [(0, "e", "quarter", quarter), (0, "n", "quarter", quarter), (1, "en", "x", halved), (2, "en", "y", halved)]
    counts = {"e": 4, "n": 3, "en": 7}
    chunks = call(
        functools.partial(cut_body, plan),
        [shaped(counts[kind], rows, edge_mats.shape[3]) for _, kind, _, rows in plan],
        [],
        edge_mats,
        node_mats,
        edge_back,
        node_back,
    )
    own = {"e": (edge_mats, edge_back), "n": (node_mats, node_back)}
    other = {letter: tuple(swap_width(a) for a in pair) for letter, pair in own.items()}
    found = []
    for (block, kind, split, rows), chunk in zip(plan, chunks):
        arrays = spread(chunk, split)
        found.append(Parts(block, kind, split, rows, own, other, arrays, [swap_width(a) for a in arrays]))
    return found


def weights_whole(edge_mats, node_mats, edge_back, node_back):
    def joined(array, rows, cols):
        axis = {rows: array.ndim - 2, cols: array.ndim - 1}
        for name in ("mesh", "width"):
            array = lax.all_gather(array, name, axis=axis[name], tiled=True)
        return array

    em, nm = joined(edge_mats, "mesh", "width"), joined(node_mats, "mesh", "width")
    eb, nb = joined(edge_back, "width", "mesh"), joined(node_back, "width", "mesh")
    em = em.reshape(em.shape[0], -1, em.shape[3])
    nm = nm.reshape(nm.shape[0], -1, nm.shape[3])
    found = [Whole("e", [em[0], eb[0]]), Whole("n", [nm[0], nb[0]])]
    for block in range(1, em.shape[0]):
        found.append(Whole("en", [em[block], eb[block], nm[block], nb[block]]))
    return found


def on_device(
    grid_latent,
    mesh_latent,
    grid_edge,
    mesh_edge,
    encoder_slot,
    encoder_target,
    halo_down,
    halo_up,
    send_lists,
    mesh_slot,
    mesh_target,
    edge_mats,
    node_mats,
    edge_back,
    node_back,
):
    depth = grid_latent.shape[1]
    hidden = edge_mats.shape[3] * lax.axis_size("width")
    nodes = mesh_latent.shape[0]
    sizes = [lax.axis_size(name) for name in ("groups", "mesh", "band", "width")]
    by_parts = sizes == [2, 4, 2, 2] and edge_mats.shape[0] == 3
    halo = halo_down.shape[0]
    line = sizes[1] * sizes[2]
    packs = (weights_by_parts if by_parts else weights_whole)(edge_mats, node_mats, edge_back, node_back)

    lent = call(pack_body, shaped(2 * halo, depth), [], grid_latent, jnp.concatenate([halo_down, halo_up])[:, None])
    from_upper = lax.ppermute(lent[:halo], ("mesh", "band"), [((i + 1) % line, i) for i in range(line)])
    from_lower = lax.ppermute(lent[halo:], ("mesh", "band"), [(i, (i + 1) % line) for i in range(line)])
    gathered = call(
        sender_body,
        shaped(grid_edge.shape[0], 2 * depth),
        [],
        grid_latent,
        from_lower,
        from_upper,
        mesh_latent,
        encoder_slot[:, None],
        encoder_target[:, None],
    )
    pack = packs[0]
    incoming = call(
        functools.partial(first_edges_body, pack, len(pack.operands)),
        shaped(nodes, depth),
        [pltpu.VMEM(grid_edge.shape, BF)] + pack.scratch(hidden, depth),
        gathered,
        grid_edge,
        encoder_target[None, :],
        *pack.operands,
    )
    pack = packs[1]
    lists = send_lists.reshape(-1, 1)
    rows, packed = call(
        functools.partial(nodes_body, pack, len(pack.operands)),
        [shaped(nodes, depth), shaped(lists.shape[0], depth)],
        pack.scratch(hidden, depth),
        mesh_latent,
        incoming,
        lists,
        *pack.operands,
    )
    edges = mesh_edge
    slots, targets, ids = mesh_slot[:, None], mesh_target[:, None], mesh_target[None, :]
    for pack in packs[2:]:
        last = pack is packs[-1]
        cut = packed.reshape(send_lists.shape[1:] + (depth,))
        senders = lax.all_to_all(cut, ("mesh", "band"), split_axis=0, concat_axis=0, tiled=True).reshape(-1, depth)
        outs = [shaped(nodes, depth)]
        if not last:
            outs += [shaped(lists.shape[0], depth), shaped(*edges.shape)]
        got = call(
            functools.partial(block_body, pack, len(pack.operands), last),
            outs,
            [pltpu.VMEM(edges.shape, BF), pltpu.VMEM((senders.shape[0] + nodes, hidden), BF)] + pack.scratch(hidden, depth),
            senders,
            rows,
            edges,
            slots,
            targets,
            ids,
            lists,
            *pack.operands,
        )
        if last:
            rows = got[0]
        else:
            rows, packed, edges = got
    return rows


def solution(mesh):
    return jax.shard_map(
        on_device,
        mesh=mesh,
        in_specs=(
            P(("groups", "mesh", "band"), None),
            P(("groups", "mesh", "band"), None),
            P(("groups", "mesh", "band"), None),
            P(("groups", "mesh", "band"), None),
            P(("groups", "mesh", "band")),
            P(("groups", "mesh", "band")),
            P(("groups", "mesh", "band")),
            P(("groups", "mesh", "band")),
            P(("groups", "mesh", "band"), None, None),
            P(("groups", "mesh", "band")),
            P(("groups", "mesh", "band")),
            P(None, None, "mesh", "width"),
            P(None, None, "mesh", "width"),
            P(None, "width", "mesh"),
            P(None, "width", "mesh"),
        ),
        out_specs=P(("groups", "mesh", "band"), None),
        check_vma=False,
    )
```

```python
import functools

import jax
import jax.numpy as jnp
from jax import lax
from jax.experimental import pallas as pl
from jax.experimental.pallas import tpu as pltpu
from jax.sharding import PartitionSpec as P

BF = jnp.bfloat16
F32 = jnp.float32
ROWS = 256
SWAP = [(0, 1), (1, 0)]
DIAGONAL = [(0, 3), (3, 0), (1, 2), (2, 1)]
LIMIT = 28 * 2**20


def dot(a, b):
    return jnp.dot(a, b, preferred_element_type=F32)


def silu(v):
    return v / (1.0 + jnp.exp(-v))


def normalize(total):
    mean = jnp.mean(total, axis=1, keepdims=True)
    meansq = jnp.mean(total * total, axis=1, keepdims=True)
    return (total - mean) * lax.rsqrt(meansq - mean * mean + 1e-05)


def columns_of(ids):
    return jnp.broadcast_to(ids, (128, ids.shape[1])).T


def one_hot(ids, count):
    spread_ids = columns_of(ids)
    pieces = []
    for at in range(0, count, 128):
        width = min(128, count - at)
        spots = lax.broadcasted_iota(jnp.int32, (ids.shape[1], width), 1) + at
        pieces.append(jnp.where(spots == spread_ids[:, :width], 1.0, 0.0).astype(BF))
    return jnp.concatenate(pieces, axis=1) if len(pieces) > 1 else pieces[0]


def one_hot_rows(ids, count):
    spots = lax.broadcasted_iota(jnp.int32, (count, ids.shape[1]), 0)
    return jnp.where(spots == ids, 1.0, 0.0).astype(BF)


def call(body, outs, scratch, fast, slow=(), cost=0.5, far=0, keep=True):
    many = isinstance(outs, list)
    full = [(o if isinstance(o[1], tuple) or not isinstance(o[0], int) else (o, BF)) for o in (outs if many else [outs])]
    places = [pltpu.VMEM] * (len(full) - far) + [pltpu.HBM] * far
    shapes = [(place if keep else jax.ShapeDtypeStruct)(shape, dtype) for place, (shape, dtype) in zip(places, full)]
    operands = [pltpu.with_memory_space_constraint(a, pltpu.VMEM) for a in fast]
    operands += [pltpu.with_memory_space_constraint(a, pltpu.HBM) for a in slow]
    specs = [pl.BlockSpec(memory_space=pltpu.VMEM)] * len(fast) + [pl.BlockSpec(memory_space=pltpu.HBM)] * len(slow)
    return pl.pallas_call(
        body,
        out_shape=shapes if many else shapes[0],
        in_specs=specs,
        out_specs=[pl.BlockSpec(memory_space=place) for place in places] if many else pl.BlockSpec(memory_space=places[0]),
        scratch_shapes=scratch,
        compiler_params=pltpu.CompilerParams(vmem_limit_bytes=LIMIT),
        cost_estimate=pl.CostEstimate(flops=int(cost * 1e9), bytes_accessed=0, transcendentals=0),
    )(*operands)


def after(array, *others):
    return lax.optimization_barrier((array,) + others)[0]


MATS = {"e": 3, "n": 2}


def arrays_in(kind):
    return sum(MATS[letter] + 1 for letter in kind)


def weight_shapes(kind, hidden, depth):
    found = []
    for letter in kind:
        found += [(MATS[letter] * depth, hidden), (hidden, depth)]
    return found


def named(kind, refs):
    return dict(zip([letter + name for letter in kind for name in "mb"], refs))


def cut_body(plan, *refs):
    raws = (refs[0], refs[1]), (refs[2], refs[3])
    outs, sem = refs[4:-1], refs[-1]
    part = {"quarter": 2 * lax.axis_index("groups") + lax.axis_index("band"), "whole": 0}
    copies = []
    for (blocks, split, rows), out in zip(plan, outs):
        spot = 0
        for block in blocks:
            for mats, back in raws:
                lanes, count = back.shape[2], mats.shape[1]
                first = pl.ds(pl.multiple_of(part[split] * rows, rows), rows)
                copies.append((mats.at[block, :, first, :], out.at[spot : spot + count]))
                spot += count
                for j in range(2):
                    at = pl.ds(pl.multiple_of(part[split] * 2 * rows + j * rows, rows), rows)
                    copies.append((back.at[block, at, :], out.at[spot, :, j * lanes : (j + 1) * lanes]))
                spot += 1
    started = [pltpu.make_async_copy(src, dst, sem.at[i]) for i, (src, dst) in enumerate(copies)]
    for copy in started:
        copy.start()
    for copy in started:
        copy.wait()


def cut(plan, raws):
    shapes = [(arrays_in("en") * len(blocks), rows, raws[0].shape[3]) for blocks, _, rows in plan]
    copies = sum(6 * len(blocks) for blocks, _, _ in plan)
    return call(functools.partial(cut_body, plan), shapes, [pltpu.SemaphoreType.DMA((copies,))], [], raws)


def put(src, zs, part, half, kind, weights):
    def piece(k, spot):
        return src.at[spot] if len(src.shape) == 3 else src.at[k, spot]

    rows, cols = src.shape[-2:]
    lanes = cols // 2
    spot = 0
    for letter in "en":
        if letter in kind:
            mats, back = weights[letter + "m"], weights[letter + "b"]
            depth = back.shape[1]
            for k, z in enumerate(zs):
                for m in range(MATS[letter]):
                    at = pl.multiple_of(m * depth + z * lanes + part * rows, rows)
                    mats[pl.ds(at, rows), half * cols : (half + 1) * cols] = piece(k, spot + m)[...]
                for j in range(2):
                    at = pl.multiple_of(half * cols + part * 2 * rows + j * rows, rows)
                    into = pl.ds(pl.multiple_of(z * lanes, lanes), lanes)
                    back[pl.ds(at, rows), into] = piece(k, spot + MATS[letter])[:, j * lanes : (j + 1) * lanes]
        spot += MATS[letter] + 1


class Parts:
    def __init__(self, kind, sides, far):
        self.kind, self.sides, self.far = kind, len(sides), far
        self.operands = [array for side in sides for array in side]

    def scratch(self, hidden, depth):
        found = [pltpu.VMEM(shape, BF) for shape in weight_shapes(self.kind, hidden, depth)]
        if self.far:
            found += [pltpu.VMEM(array.shape, BF) for array in self.operands]
            found += [pltpu.SemaphoreType.DMA((len(self.operands),))]
        return found

    def start(self, operands, scratch):
        if not self.far:
            return []
        *places, sems = scratch[2 * len(self.kind) :]
        copies = [pltpu.make_async_copy(src, dst, sems.at[i]) for i, (src, dst) in enumerate(zip(operands, places))]
        for copy in copies:
            copy.start()
        return copies

    def finish(self, operands, scratch, copies):
        weights = named(self.kind, scratch)
        if self.far:
            operands = scratch[2 * len(self.kind) : -1]
        count = lax.axis_size("mesh")
        z = lax.axis_index("mesh")
        x, y = lax.axis_index("band"), lax.axis_index("groups")
        quarters = [2 * y + x, 2 * y + 1 - x, 2 * (1 - y) + x, 2 * (1 - y) + 1 - x]
        each = len(operands) // self.sides
        for half in range(self.sides):
            for copy in copies[half * each : (half + 1) * each]:
                copy.wait()
            own, *arrays = operands[half * each : (half + 1) * each]
            put(own, [z], 0, half, self.kind, weights)
            for part, src in zip(quarters, arrays):
                put(src, [z ^ k for k in range(1, count)], part, half, self.kind, weights)
        return weights


class Whole:
    far = False

    def __init__(self, kind, arrays):
        self.kind, self.operands = kind, arrays

    def scratch(self, hidden, depth):
        return []

    def start(self, operands, scratch):
        return []

    def finish(self, operands, scratch, copies):
        return named(self.kind, operands)


def join_body(*refs):
    blocks = [ref for ref in refs if len(ref.shape) == 4]
    for k, ref in enumerate(refs[: -len(blocks)]):
        for i, block in enumerate(blocks):
            block[k] = ref[i * block.shape[1] : (i + 1) * block.shape[1]]


def join(arrays, blocks):
    count, rows, cols = arrays[0].shape
    return call(join_body, [(len(arrays), count // blocks, rows, cols)] * blocks, [], arrays)


def lend_body(grid, down, up, low, high):
    low[...] = dot(one_hot(down[...], grid.shape[0]), grid[...]).astype(BF)
    high[...] = dot(one_hot(up[...], grid.shape[0]), grid[...]).astype(BF)


def gather_body(grid, low, high, nodes, slots, targets, out):
    table = jnp.concatenate([grid[...], low[...], high[...]], axis=0)
    depth = grid.shape[1]
    for at in range(0, out.shape[0], ROWS):
        rows = slice(at, at + ROWS)
        out[rows, 0:depth] = dot(one_hot(slots[:, rows], table.shape[0]), table).astype(BF)
        out[rows, depth:] = dot(one_hot(targets[:, rows], nodes.shape[0]), nodes[...]).astype(BF)


def edge_tail(weights, pre):
    return normalize(dot(silu(pre).astype(BF), weights["eb"][...]))


def node_pre(weights, nodes, incoming):
    depth = nodes.shape[1]
    return dot(nodes, weights["nm"][0:depth, :]) + dot(incoming, weights["nm"][depth:, :])


def node_tail(weights, nodes, incoming):
    pre = node_pre(weights, nodes, incoming)
    return (nodes.astype(F32) + normalize(dot(silu(pre).astype(BF), weights["nb"][...]))).astype(BF)


def sum_of(terms, rows=slice(None)):
    total = terms[0][rows, :].astype(F32)
    for term in terms[1:]:
        total = total + term[rows, :].astype(F32)
    return total


def first_edges_body(pack, gathered, *refs):
    count = len(pack.operands)
    edges, out, buffer, sem, scratch = refs[count], refs[count + 1], refs[count + 2], refs[count + 3], refs[count + 4 :]
    fetch = pltpu.make_async_copy(edges, buffer, sem)
    fetch.start()
    weights = pack.finish(refs[:count], scratch, [])
    for at in range(0, edges.shape[0], ROWS):
        rows = slice(at, at + ROWS)
        both = gathered.shape[1]
        pre = dot(gathered[rows, :], weights["em"][0:both, :])
        if at == 0:
            fetch.wait()
        pre = pre + dot(buffer[rows, :], weights["em"][both:, :])
        out[rows, :] = dot(silu(pre).astype(BF), weights["eb"][...]).astype(BF)


def first_sums_body(targets, *refs):
    terms, out, message = refs[:-2], refs[-2], refs[-1]
    for at in range(0, message.shape[0], ROWS):
        rows = slice(at, at + ROWS)
        message[rows, :] = normalize(sum_of(terms, rows)).astype(BF)
    out[...] = dot(one_hot_rows(targets[...], out.shape[0]), message[...]).astype(BF)


def first_nodes_body(pack, nodes, incoming, *refs):
    count = len(pack.operands)
    out, scratch = refs[count], refs[count + 1 :]
    weights = pack.finish(refs[:count], scratch, [])
    pre = node_pre(weights, nodes[...], incoming[...])
    out[...] = dot(silu(pre).astype(BF), weights["nb"][...]).astype(BF)


def first_next_body(nodes, lists, *refs):
    terms, packed, out, buffer, sem = refs[:-4], refs[-4], refs[-3], refs[-2], refs[-1]
    buffer[...] = (nodes[...].astype(F32) + normalize(sum_of(terms))).astype(BF)
    save = pltpu.make_async_copy(buffer, out, sem)
    save.start()
    packed[...] = dot(one_hot(lists[...], nodes.shape[0]), buffer[...]).astype(BF)
    save.wait()


def block_body(pack, last, sent, slots, targets, lists, *refs):
    count = len(pack.operands)
    refs, operands = refs[count:], refs[:count]
    if pack.far:
        nodes, edges, operands, refs = operands[0], operands[1], operands[2:] + refs[:2], refs[2:]
    else:
        nodes, edges, refs = refs[0], refs[1], refs[2:]
    if last:
        (out, *refs) = refs
    else:
        (packed, saved, edges_saved, *refs) = refs
    message, sent_table, node_table, node_buffer, edge_buffer, sems, *scratch = refs
    get_nodes = pltpu.make_async_copy(nodes, node_buffer, sems.at[0])
    get_edges = pltpu.make_async_copy(edges, edge_buffer, sems.at[1])
    get_nodes.start()
    get_edges.start()
    weights = pack.finish(operands, scratch, pack.start(operands, scratch))
    em, depth = weights["em"], sent.shape[1]
    sent_table[...] = dot(sent[...], em[0:depth, :]).astype(BF)
    get_nodes.wait()
    node_table[...] = dot(node_buffer[...], em[depth : 2 * depth, :]).astype(BF)
    get_edges.wait()
    for at in range(0, message.shape[0], ROWS):
        rows = slice(at, at + ROWS)
        pre = dot(edge_buffer[rows, :], em[2 * depth :, :])
        pre = pre + dot(one_hot(targets[:, rows], nodes.shape[0]), node_table[...])
        pre = pre + dot(one_hot(slots[:, rows], sent.shape[0]), sent_table[...])
        normed = edge_tail(weights, pre)
        message[rows, :] = normed.astype(BF)
        if not last:
            edge_buffer[rows, :] = (edge_buffer[rows, :].astype(F32) + normed).astype(BF)
    if not last:
        save_edges = pltpu.make_async_copy(edge_buffer, edges_saved, sems.at[2])
        save_edges.start()
    incoming = dot(one_hot_rows(targets[...], nodes.shape[0]), message[...]).astype(BF)
    new = node_tail(weights, node_buffer[...], incoming)
    if last:
        out[...] = new
        return
    node_buffer[...] = new
    save_nodes = pltpu.make_async_copy(node_buffer, saved, sems.at[3])
    save_nodes.start()
    packed[...] = dot(one_hot(lists[...], nodes.shape[0]), new).astype(BF)
    save_edges.wait()
    save_nodes.wait()


def over_slices(chunk):
    count = lax.axis_size("mesh")
    return [lax.ppermute(chunk, "mesh", [(i, i ^ k) for i in range(count)]) for k in range(1, count)]


def over_plane(own):
    return [
        lax.ppermute(own, "band", SWAP),
        lax.ppermute(own, "groups", SWAP),
        lax.ppermute(own, ("groups", "band"), DIAGONAL),
    ]


def swap_width(array):
    return lax.ppermute(array, "width", SWAP)


def weights_whole(edge_mats, node_mats, edge_back, node_back):
    def joined(array, rows, cols):
        axis = {rows: array.ndim - 2, cols: array.ndim - 1}
        for name in ("mesh", "width"):
            array = lax.all_gather(array, name, axis=axis[name], tiled=True)
        return array

    em, nm = joined(edge_mats, "mesh", "width"), joined(node_mats, "mesh", "width")
    eb, nb = joined(edge_back, "width", "mesh"), joined(node_back, "width", "mesh")
    em = em.reshape(em.shape[0], -1, em.shape[3])
    nm = nm.reshape(nm.shape[0], -1, nm.shape[3])
    found = []
    cols = edge_mats.shape[3]
    at = lax.axis_index("width") * cols
    for kind, mats, back in (("e", em[0], eb[0]), ("n", nm[0], nb[0])):
        mine = [lax.dynamic_slice_in_dim(mats, at, cols, 1), lax.dynamic_slice_in_dim(back, at, cols, 0)]
        found.append(Whole(kind, mine))
    for block in range(1, em.shape[0]):
        found.append(Whole("en", [em[block], eb[block], nm[block], nb[block]]))
    return found


def on_device(
    grid_latent,
    mesh_latent,
    grid_edge,
    mesh_edge,
    encoder_slot,
    encoder_target,
    halo_down,
    halo_up,
    send_lists,
    mesh_slot,
    mesh_target,
    edge_mats,
    node_mats,
    edge_back,
    node_back,
):
    depth = grid_latent.shape[1]
    nodes = mesh_latent.shape[0]
    grid_edges, mesh_edges = grid_edge.shape[0], mesh_edge.shape[0]
    sizes = [lax.axis_size(name) for name in ("groups", "mesh", "band", "width")]
    by_parts = sizes == [2, 4, 2, 2] and edge_mats.shape[0] == 3
    halo = halo_down.shape[0]
    line = sizes[1] * sizes[2]
    sent_rows = send_lists.shape[1] * send_lists.shape[2]
    hidden = edge_mats.shape[3] * sizes[3]
    lists = send_lists.reshape(1, -1)
    node_buffer, edge_buffer = pltpu.VMEM((nodes, depth), BF), pltpu.VMEM((mesh_edges, depth), BF)

    lent_down, lent_up = call(
        lend_body, [(halo, depth), (halo, depth)], [], [grid_latent, halo_down[None, :], halo_up[None, :]]
    )
    if by_parts:
        raws = [edge_mats, edge_back, node_mats, node_back]
        slab = edge_mats.shape[2]
        quarter = slab // 4
        [cut0] = cut([((0,), "quarter", quarter)], raws)
        cut12, own0, own1, own2 = cut([((1, 2), "quarter", quarter)] + [((block,), "whole", slab) for block in range(3)], raws)
        turned0 = over_slices(cut0)
        lent_down, lent_up = after(lent_down, turned0[0]), after(lent_up, turned0[0])
    from_upper = lax.ppermute(lent_down, ("mesh", "band"), [(i + 1, i) for i in range(line - 1)])
    from_lower = lax.ppermute(lent_up, ("mesh", "band"), [(i, i + 1) for i in range(line - 1)])
    if by_parts:
        [joined0] = join(turned0[:-1] + [after(turned0[-1], from_upper, from_lower, cut12)], 1)
        plane0 = over_plane(joined0)
        side0 = [own0, joined0] + plane0
        packs = [Parts("e", [side0], False), Parts("n", [side0], False), None, None]
        joined1, joined2 = join(over_slices(after(cut12, joined0)), 2)
        from_lower = after(from_lower, joined1)
    else:
        packs = weights_whole(edge_mats, node_mats, edge_back, node_back)
    gathered = call(
        gather_body,
        (grid_edges, 2 * depth),
        [],
        [grid_latent, from_lower, from_upper, mesh_latent, encoder_slot[None, :], encoder_target[None, :]],
        cost=1.2,
    )
    pack = packs[0]
    term = call(
        functools.partial(first_edges_body, pack),
        (grid_edges, depth),
        [pltpu.VMEM((grid_edges, depth), BF), pltpu.SemaphoreType.DMA(())] + pack.scratch(hidden // 2, depth),
        [gathered] + pack.operands,
        [grid_edge],
        cost=3.0,
    )
    if by_parts:
        plane1 = over_plane(after(joined1, term))
    incoming = call(
        first_sums_body,
        (nodes, depth),
        [pltpu.VMEM((grid_edges, depth), BF)],
        [encoder_target[None, :], term, swap_width(term)],
        cost=0.8,
    )
    pack = packs[1]
    term = call(
        functools.partial(first_nodes_body, pack),
        (nodes, depth),
        pack.scratch(hidden // 2, depth),
        [mesh_latent, incoming] + pack.operands,
        cost=0.8,
    )
    packed, rows = call(
        first_next_body,
        [(sent_rows, depth), (nodes, depth)],
        [node_buffer, pltpu.SemaphoreType.DMA(())],
        [mesh_latent, lists, term, swap_width(term)],
        cost=1.6,
        far=1,
    )
    edges = mesh_edge
    slots, targets = mesh_slot[None, :], mesh_target[None, :]
    early = incoming
    for block in range(1, edge_mats.shape[0]):
        last = block == edge_mats.shape[0] - 1
        pack = packs[block + 1]
        cut_rows = packed.reshape(send_lists.shape[1:] + (depth,))
        sent = lax.all_to_all(cut_rows, ("mesh", "band"), split_axis=0, concat_axis=0, tiled=True).reshape(-1, depth)
        if by_parts:
            if not last:
                plane2 = over_plane(after(joined2, sent, *plane1))
                side = [own1, joined1] + plane1
            else:
                side = [own2, joined2] + plane2
            other = [swap_width(after(a, early)) for a in side[:2]] + [swap_width(after(a, sent)) for a in side[2:]]
            pack = Parts("en", [side, other], True)
            early = sent
        near = [sent, slots, targets, lists]
        got = call(
            functools.partial(block_body, pack, last),
            (nodes, depth) if last else [(sent_rows, depth), (nodes, depth), (mesh_edges, depth)],
            [edge_buffer, pltpu.VMEM((sent_rows, hidden), BF), pltpu.VMEM((nodes, hidden), BF), node_buffer, edge_buffer]
            + [pltpu.SemaphoreType.DMA((4,))]
            + pack.scratch(hidden, depth),
            near if pack.far else near + pack.operands,
            [rows, edges] + (pack.operands if pack.far else []),
            cost=6.5,
            far=0 if last else 2,
            keep=not last,
        )
        if last:
            rows = got
        else:
            packed, rows, edges = got
    return rows


def solution(mesh):
    return jax.shard_map(
        on_device,
        mesh=mesh,
        in_specs=(
            P(("groups", "mesh", "band"), None),
            P(("groups", "mesh", "band"), None),
            P(("groups", "mesh", "band"), None),
            P(("groups", "mesh", "band"), None),
            P(("groups", "mesh", "band")),
            P(("groups", "mesh", "band")),
            P(("groups", "mesh", "band")),
            P(("groups", "mesh", "band")),
            P(("groups", "mesh", "band"), None, None),
            P(("groups", "mesh", "band")),
            P(("groups", "mesh", "band")),
            P(None, None, "mesh", "width"),
            P(None, None, "mesh", "width"),
            P(None, "width", "mesh"),
            P(None, "width", "mesh"),
        ),
        out_specs=P(("groups", "mesh", "band"), None),
        check_vma=False,
    )
```

```python
import functools

import jax
import jax.numpy as jnp
from jax import lax
from jax.experimental import pallas as pl
from jax.experimental.pallas import tpu as pltpu
from jax.sharding import PartitionSpec as P

BF = jnp.bfloat16
F32 = jnp.float32
ROWS = 384
SWAP = [(0, 1), (1, 0)]
DIAGONAL = [(0, 3), (3, 0), (1, 2), (2, 1)]
LIMIT = 28 * 2**20


def dot(a, b):
    return jnp.dot(a, b, preferred_element_type=F32)


def silu(v):
    return v * (0.5 * jnp.tanh(0.5 * v) + 0.5)


def normalize(total):
    mean = jnp.mean(total, axis=1, keepdims=True)
    meansq = jnp.mean(total * total, axis=1, keepdims=True)
    return (total - mean) * lax.rsqrt(meansq - mean * mean + 1e-05)


def columns_of(ids):
    return jnp.broadcast_to(ids, (128, ids.shape[1])).T


def one_hot(ids, count):
    spread_ids = columns_of(ids)
    pieces = []
    for at in range(0, count, 128):
        width = min(128, count - at)
        spots = lax.broadcasted_iota(jnp.int32, (ids.shape[1], width), 1) + at
        pieces.append(jnp.where(spots == spread_ids[:, :width], 1.0, 0.0).astype(BF))
    return jnp.concatenate(pieces, axis=1) if len(pieces) > 1 else pieces[0]


def one_hot_rows(ids, count):
    spots = lax.broadcasted_iota(jnp.int32, (count, ids.shape[1]), 0)
    return jnp.where(spots == ids, 1.0, 0.0).astype(BF)


def call(body, outs, scratch, fast, slow=(), cost=0.5, far=0, keep=True):
    many = isinstance(outs, list)
    full = [(o if isinstance(o[1], tuple) or not isinstance(o[0], int) else (o, BF)) for o in (outs if many else [outs])]
    places = [pltpu.VMEM] * (len(full) - far) + [pltpu.HBM] * far
    shapes = [(place if keep else jax.ShapeDtypeStruct)(shape, dtype) for place, (shape, dtype) in zip(places, full)]
    operands = [pltpu.with_memory_space_constraint(a, pltpu.VMEM) for a in fast]
    operands += [pltpu.with_memory_space_constraint(a, pltpu.HBM) for a in slow]
    specs = [pl.BlockSpec(memory_space=pltpu.VMEM)] * len(fast) + [pl.BlockSpec(memory_space=pltpu.HBM)] * len(slow)
    return pl.pallas_call(
        body,
        out_shape=shapes if many else shapes[0],
        in_specs=specs,
        out_specs=[pl.BlockSpec(memory_space=place) for place in places] if many else pl.BlockSpec(memory_space=places[0]),
        scratch_shapes=scratch,
        compiler_params=pltpu.CompilerParams(vmem_limit_bytes=LIMIT),
        cost_estimate=pl.CostEstimate(flops=int(cost * 1e9), bytes_accessed=0, transcendentals=0),
    )(*operands)


def after(array, *others):
    return lax.optimization_barrier((array,) + others)[0]


MATS = {"e": 3, "n": 2}


def arrays_in(kind):
    return sum(MATS[letter] + 1 for letter in kind)


def weight_shapes(kind, hidden, depth):
    found = []
    for letter in kind:
        found += [(MATS[letter] * depth, hidden), (hidden, depth)]
    return found


def named(kind, refs):
    return dict(zip([letter + name for letter in kind for name in "mb"], refs))


def cut_body(plan, *refs):
    raws = (refs[0], refs[1]), (refs[2], refs[3])
    outs, sem = refs[4:-1], refs[-1]
    part = {"quarter": 2 * lax.axis_index("groups") + lax.axis_index("band"), "whole": 0}
    copies = []
    for (blocks, split, rows), out in zip(plan, outs):
        spot = 0
        for block in blocks:
            for mats, back in raws:
                lanes, count = back.shape[2], mats.shape[1]
                first = pl.ds(pl.multiple_of(part[split] * rows, rows), rows)
                copies.append((mats.at[block, :, first, :], out.at[spot : spot + count]))
                spot += count
                for j in range(2):
                    at = pl.ds(pl.multiple_of(part[split] * 2 * rows + j * rows, rows), rows)
                    copies.append((back.at[block, at, :], out.at[spot, :, j * lanes : (j + 1) * lanes]))
                spot += 1
    started = [pltpu.make_async_copy(src, dst, sem.at[i]) for i, (src, dst) in enumerate(copies)]
    for copy in started:
        copy.start()
    for copy in started:
        copy.wait()


def cut(plan, raws):
    shapes = [(arrays_in("en") * len(blocks), rows, raws[0].shape[3]) for blocks, _, rows in plan]
    copies = sum(6 * len(blocks) for blocks, _, _ in plan)
    return call(functools.partial(cut_body, plan), shapes, [pltpu.SemaphoreType.DMA((copies,))], [], raws)


def put(src, zs, part, half, kind, weights):
    def piece(k, spot):
        return src.at[spot] if len(src.shape) == 3 else src.at[k, spot]

    rows, cols = src.shape[-2:]
    lanes = cols // 2
    spot = 0
    for letter in "en":
        if letter in kind:
            mats, back = weights[letter + "m"], weights[letter + "b"]
            depth = back.shape[1]
            for k, z in enumerate(zs):
                for m in range(MATS[letter]):
                    at = pl.multiple_of(m * depth + z * lanes + part * rows, rows)
                    mats[pl.ds(at, rows), half * cols : (half + 1) * cols] = piece(k, spot + m)[...]
                for j in range(2):
                    at = pl.multiple_of(half * cols + part * 2 * rows + j * rows, rows)
                    into = pl.ds(pl.multiple_of(z * lanes, lanes), lanes)
                    back[pl.ds(at, rows), into] = piece(k, spot + MATS[letter])[:, j * lanes : (j + 1) * lanes]
        spot += MATS[letter] + 1


class Parts:
    def __init__(self, sides, far, kind="en"):
        arrays = [array for side in sides for array in side]
        self.kind, self.sides = kind, len(sides)
        self.far = [i in far for i in range(len(arrays))]
        self.near_operands = [array for array, far in zip(arrays, self.far) if not far]
        self.far_operands = [array for array, far in zip(arrays, self.far) if far]

    def scratch(self, hidden, depth):
        found = [pltpu.VMEM(shape, BF) for shape in weight_shapes(self.kind, hidden, depth)]
        found += [pltpu.VMEM(array.shape, BF) for array in self.far_operands]
        return found + [pltpu.SemaphoreType.DMA((max(len(self.far_operands), 1),))]

    def load(self, near, far, scratch):
        weights, sems = named(self.kind, scratch), scratch[-1]
        staged = scratch[2 * len(self.kind) : -1]
        copies = [pltpu.make_async_copy(src, dst, sems.at[i]) for i, (src, dst) in enumerate(zip(far, staged))]
        for copy in copies:
            copy.start()
        sources, near, staged, waits = [], list(near), list(staged), list(copies)
        for is_far in self.far:
            sources.append((staged.pop(0), waits.pop(0)) if is_far else (near.pop(0), None))
        count = lax.axis_size("mesh")
        z = lax.axis_index("mesh")
        x, y = lax.axis_index("band"), lax.axis_index("groups")
        quarters = [2 * y + x, 2 * y + 1 - x, 2 * (1 - y) + x, 2 * (1 - y) + 1 - x]
        each = len(sources) // self.sides

        def place(kind):
            for wanted in (False, True):
                for i, (src, wait) in enumerate(sources):
                    if self.far[i] != wanted:
                        continue
                    if wait is not None and kind == "e":
                        wait.wait()
                    spot = i % each
                    if spot == 0:
                        put(src, [z], 0, i // each, kind, weights)
                    else:
                        put(src, [z ^ k for k in range(1, count)], quarters[spot - 1], i // each, kind, weights)

        return weights, place


class Whole:
    def __init__(self, arrays, kind="en"):
        self.near_operands, self.far_operands, self.kind = arrays, [], kind

    def scratch(self, hidden, depth):
        return []

    def load(self, near, far, scratch):
        return named(self.kind, near), lambda kind: None


def join_body(*refs):
    blocks = [ref for ref in refs if len(ref.shape) == 4]
    for k, ref in enumerate(refs[: -len(blocks)]):
        for i, block in enumerate(blocks):
            block[k] = ref[i * block.shape[1] : (i + 1) * block.shape[1]]


def join(arrays, blocks):
    count, rows, cols = arrays[0].shape
    return call(join_body, [(len(arrays), count // blocks, rows, cols)] * blocks, [], arrays)


def lend_body(grid, down, up, low, high):
    low[...] = dot(one_hot(down[...], grid.shape[0]), grid[...]).astype(BF)
    high[...] = dot(one_hot(up[...], grid.shape[0]), grid[...]).astype(BF)


def gather_body(grid, low, high, nodes, slots, targets, out):
    table = jnp.concatenate([grid[...], low[...], high[...]], axis=0)
    depth = grid.shape[1]
    for at in range(0, out.shape[0], ROWS):
        rows = slice(at, at + ROWS)
        out[rows, 0:depth] = dot(one_hot(slots[:, rows], table.shape[0]), table).astype(BF)
        out[rows, depth:] = dot(one_hot(targets[:, rows], nodes.shape[0]), nodes[...]).astype(BF)


def edges_to_nodes(weights, inputs, table, edge_buffer, targets, message, keep):
    for at in range(0, message.shape[0], ROWS):
        rows = slice(at, at + ROWS)
        pre = dot(inputs(rows), table[...])
        normed = normalize(dot(silu(pre).astype(BF), weights["eb"][...]))
        message[rows, :] = normed.astype(BF)
        if keep:
            edge_buffer[rows, :] = (edge_buffer[rows, :].astype(F32) + normed).astype(BF)


def nodes_after(weights, nodes, incoming):
    pre = dot(jnp.concatenate([nodes, incoming], axis=1), weights["nm"][...])
    return (nodes.astype(F32) + normalize(dot(silu(pre).astype(BF), weights["nb"][...]))).astype(BF)


def sum_of(terms, rows=slice(None)):
    total = terms[0][rows, :].astype(F32)
    for term in terms[1:]:
        total = total + term[rows, :].astype(F32)
    return total


def half_edges_body(pack, gathered, *refs):
    count = len(pack.near_operands)
    edges, out, buffer, sem, *scratch = refs[count:]
    fetch = pltpu.make_async_copy(edges, buffer, sem)
    fetch.start()
    weights, place = pack.load(refs[:count], (), scratch)
    place("e")
    fetch.wait()
    for at in range(0, edges.shape[0], ROWS):
        rows = slice(at, at + ROWS)
        pre = dot(jnp.concatenate([gathered[rows, :], buffer[rows, :]], axis=1), weights["em"][...])
        out[rows, :] = dot(silu(pre).astype(BF), weights["eb"][...]).astype(BF)


def half_nodes_body(pack, targets, nodes, mine, other, *refs):
    count = len(pack.near_operands)
    out, message, *scratch = refs[count:]
    weights, place = pack.load(refs[:count], (), scratch)
    place("n")
    for at in range(0, message.shape[0], ROWS):
        rows = slice(at, at + ROWS)
        message[rows, :] = normalize(sum_of((mine, other), rows)).astype(BF)
    incoming = dot(one_hot_rows(targets[...], nodes.shape[0]), message[...]).astype(BF)
    pre = dot(jnp.concatenate([nodes[...], incoming], axis=1), weights["nm"][...])
    out[...] = dot(silu(pre).astype(BF), weights["nb"][...]).astype(BF)


def first_next_body(nodes, lists, mine, other, packed, out, buffer, sem):
    buffer[...] = (nodes[...].astype(F32) + normalize(sum_of((mine, other)))).astype(BF)
    save = pltpu.make_async_copy(buffer, out, sem)
    save.start()
    packed[...] = dot(one_hot(lists[...], nodes.shape[0]), buffer[...]).astype(BF)
    save.wait()


def block_body(pack, last, sent, slots, targets, lists, *refs):
    near, far = len(pack.near_operands), len(pack.far_operands)
    near, refs = refs[:near], refs[near:]
    nodes, edges, far, refs = refs[0], refs[1], refs[2 : 2 + far], refs[2 + far :]
    if last:
        (out, *refs) = refs
    else:
        (packed, saved, edges_saved, *refs) = refs
    message, table, node_buffer, edge_buffer, sems, *scratch = refs
    get_nodes = pltpu.make_async_copy(nodes, node_buffer, sems.at[0])
    get_edges = pltpu.make_async_copy(edges, edge_buffer, sems.at[1])
    get_nodes.start()
    get_edges.start()
    weights, place = pack.load(near, far, scratch)
    place("e")
    em, depth, count = weights["em"], sent.shape[1], nodes.shape[0]
    table[0:depth, :] = em[2 * depth :, :]
    get_nodes.wait()
    table[depth : depth + count, :] = dot(node_buffer[...], em[depth : 2 * depth, :]).astype(BF)
    table[depth + count :, :] = dot(sent[...], em[0:depth, :]).astype(BF)
    get_edges.wait()

    def inputs(rows):
        picks = [one_hot(targets[:, rows], count), one_hot(slots[:, rows], sent.shape[0])]
        return jnp.concatenate([edge_buffer[rows, :]] + picks, axis=1)

    edges_to_nodes(weights, inputs, table, edge_buffer, targets, message, not last)
    if not last:
        save_edges = pltpu.make_async_copy(edge_buffer, edges_saved, sems.at[2])
        save_edges.start()
    place("n")
    incoming = dot(one_hot_rows(targets[...], count), message[...]).astype(BF)
    new = nodes_after(weights, node_buffer[...], incoming)
    if last:
        out[...] = new
        return
    node_buffer[...] = new
    save_nodes = pltpu.make_async_copy(node_buffer, saved, sems.at[3])
    save_nodes.start()
    packed[...] = dot(one_hot(lists[...], count), new).astype(BF)
    save_edges.wait()
    save_nodes.wait()


def over_slices(chunk):
    count = lax.axis_size("mesh")
    return [lax.ppermute(chunk, "mesh", [(i, i ^ k) for i in range(count)]) for k in range(1, count)]


def over_plane(own):
    return [
        lax.ppermute(own, "band", SWAP),
        lax.ppermute(own, "groups", SWAP),
        lax.ppermute(own, ("groups", "band"), DIAGONAL),
    ]


def swap_width(array):
    return lax.ppermute(array, "width", SWAP)


def weights_whole(edge_mats, node_mats, edge_back, node_back):
    def joined(array, rows, cols):
        axis = {rows: array.ndim - 2, cols: array.ndim - 1}
        for name in ("mesh", "width"):
            array = lax.all_gather(array, name, axis=axis[name], tiled=True)
        return array

    em, nm = joined(edge_mats, "mesh", "width"), joined(node_mats, "mesh", "width")
    eb, nb = joined(edge_back, "width", "mesh"), joined(node_back, "width", "mesh")
    em = em.reshape(em.shape[0], -1, em.shape[3])
    nm = nm.reshape(nm.shape[0], -1, nm.shape[3])
    cols = edge_mats.shape[3]
    at = lax.axis_index("width") * cols
    found = []
    for kind, mats, back in (("e", em[0], eb[0]), ("n", nm[0], nb[0])):
        found.append(Whole([lax.dynamic_slice_in_dim(mats, at, cols, 1), lax.dynamic_slice_in_dim(back, at, cols, 0)], kind))
    return found + [Whole([em[block], eb[block], nm[block], nb[block]]) for block in range(1, em.shape[0])]


def on_device(
    grid_latent,
    mesh_latent,
    grid_edge,
    mesh_edge,
    encoder_slot,
    encoder_target,
    halo_down,
    halo_up,
    send_lists,
    mesh_slot,
    mesh_target,
    edge_mats,
    node_mats,
    edge_back,
    node_back,
):
    depth = grid_latent.shape[1]
    nodes = mesh_latent.shape[0]
    grid_edges, mesh_edges = grid_edge.shape[0], mesh_edge.shape[0]
    sizes = [lax.axis_size(name) for name in ("groups", "mesh", "band", "width")]
    by_parts = sizes == [2, 4, 2, 2] and edge_mats.shape[0] == 3
    halo = halo_down.shape[0]
    line = sizes[1] * sizes[2]
    sent_rows = send_lists.shape[1] * send_lists.shape[2]
    hidden = edge_mats.shape[3] * sizes[3]
    lists = send_lists.reshape(1, -1)
    node_buffer, edge_buffer = pltpu.VMEM((nodes, depth), BF), pltpu.VMEM((mesh_edges, depth), BF)

    lent_down, lent_up = call(
        lend_body, [(halo, depth), (halo, depth)], [], [grid_latent, halo_down[None, :], halo_up[None, :]]
    )
    if by_parts:
        raws = [edge_mats, edge_back, node_mats, node_back]
        slab = edge_mats.shape[2]
        quarter = slab // 4
        [cut0] = cut([((0,), "quarter", quarter)], raws)
        cut12, own0, own1, own2 = cut([((1, 2), "quarter", quarter)] + [((block,), "whole", slab) for block in range(3)], raws)
        turned0 = over_slices(cut0)
        lent_down, lent_up = after(lent_down, turned0[0]), after(lent_up, turned0[0])
    from_upper = lax.ppermute(lent_down, ("mesh", "band"), [(i + 1, i) for i in range(line - 1)])
    from_lower = lax.ppermute(lent_up, ("mesh", "band"), [(i, i + 1) for i in range(line - 1)])
    if by_parts:
        [joined0] = join(turned0[:-1] + [after(turned0[-1], from_upper, from_lower, cut12)], 1)
        plane0 = over_plane(joined0)
        side0 = [own0, joined0] + plane0
        joined1, joined2 = join(over_slices(after(cut12, joined0)), 2)
        from_lower = after(from_lower, joined1)
    else:
        packs = weights_whole(edge_mats, node_mats, edge_back, node_back)
    gathered = call(
        gather_body,
        (grid_edges, 2 * depth),
        [],
        [grid_latent, from_lower, from_upper, mesh_latent, encoder_slot[None, :], encoder_target[None, :]],
        cost=1.2,
    )
    if by_parts:
        packs = [Parts([side0], [], "e"), Parts([side0], [], "n")]
    term = call(
        functools.partial(half_edges_body, packs[0]),
        (grid_edges, depth),
        [pltpu.VMEM((grid_edges, depth), BF), pltpu.SemaphoreType.DMA(())] + packs[0].scratch(hidden // 2, depth),
        [gathered] + packs[0].near_operands,
        [grid_edge],
        cost=3.0,
    )
    if by_parts:
        plane1 = over_plane(after(joined1, term))
    before = term
    term = call(
        functools.partial(half_nodes_body, packs[1]),
        (nodes, depth),
        [pltpu.VMEM((grid_edges, depth), BF)] + packs[1].scratch(hidden // 2, depth),
        [encoder_target[None, :], mesh_latent, term, swap_width(term)] + packs[1].near_operands,
        cost=1.6,
    )
    packed, rows = call(
        first_next_body,
        [(sent_rows, depth), (nodes, depth)],
        [node_buffer, pltpu.SemaphoreType.DMA(())],
        [mesh_latent, lists, term, swap_width(term)],
        cost=1.6,
        far=1,
    )
    edges = mesh_edge
    slots, targets = mesh_slot[None, :], mesh_target[None, :]
    for block in range(1, edge_mats.shape[0]):
        last = block == edge_mats.shape[0] - 1
        cut_rows = packed.reshape(send_lists.shape[1:] + (depth,))
        sent = lax.all_to_all(cut_rows, ("mesh", "band"), split_axis=0, concat_axis=0, tiled=True).reshape(-1, depth)
        if by_parts:
            if not last:
                plane2 = over_plane(after(joined2, sent))
                side = [own1, joined1] + plane1
            else:
                side = [own2, joined2] + plane2
            other = [swap_width(after(a, before)) for a in side[:2]] + [swap_width(after(a, sent)) for a in side[2:]]
            pack = Parts([side, other], range(7))
            before = sent
        else:
            pack = packs[block + 1]
        table = pltpu.VMEM((depth + nodes + sent_rows, hidden), BF)
        got = call(
            functools.partial(block_body, pack, last),
            (nodes, depth) if last else [(sent_rows, depth), (nodes, depth), (mesh_edges, depth)],
            [edge_buffer, table, node_buffer, edge_buffer, pltpu.SemaphoreType.DMA((4,))] + pack.scratch(hidden, depth),
            [sent, slots, targets, lists] + pack.near_operands,
            [rows, edges] + pack.far_operands,
            cost=6.5,
            far=0 if last else 2,
            keep=not last,
        )
        if last:
            rows = got
        else:
            packed, rows, edges = got
    return rows


def solution(mesh):
    return jax.shard_map(
        on_device,
        mesh=mesh,
        in_specs=(
            P(("groups", "mesh", "band"), None),
            P(("groups", "mesh", "band"), None),
            P(("groups", "mesh", "band"), None),
            P(("groups", "mesh", "band"), None),
            P(("groups", "mesh", "band")),
            P(("groups", "mesh", "band")),
            P(("groups", "mesh", "band")),
            P(("groups", "mesh", "band")),
            P(("groups", "mesh", "band"), None, None),
            P(("groups", "mesh", "band")),
            P(("groups", "mesh", "band")),
            P(None, None, "mesh", "width"),
            P(None, None, "mesh", "width"),
            P(None, "width", "mesh"),
            P(None, "width", "mesh"),
        ),
        out_specs=P(("groups", "mesh", "band"), None),
        check_vma=False,
    )
```

```python
import functools

import jax
import jax.numpy as jnp
from jax import lax
from jax.experimental import pallas as pl
from jax.experimental.pallas import tpu as pltpu
from jax.sharding import PartitionSpec as P

BF = jnp.bfloat16
F32 = jnp.float32
ROWS = 384
SWAP = [(0, 1), (1, 0)]
DIAGONAL = [(0, 3), (3, 0), (1, 2), (2, 1)]
LIMIT = 28 * 2**20


def dot(a, b):
    return jnp.dot(a, b, preferred_element_type=F32)


def silu(v):
    return v * (0.5 * jnp.tanh(0.5 * v) + 0.5)


def normalize(total):
    mean = jnp.mean(total, axis=1, keepdims=True)
    meansq = jnp.mean(total * total, axis=1, keepdims=True)
    return (total - mean) * lax.rsqrt(meansq - mean * mean + 1e-05)


def columns_of(ids):
    return jnp.broadcast_to(ids, (128, ids.shape[1])).T


def one_hot(ids, count):
    spread_ids = columns_of(ids)
    pieces = []
    for at in range(0, count, 128):
        width = min(128, count - at)
        spots = lax.broadcasted_iota(jnp.int32, (ids.shape[1], width), 1) + at
        pieces.append(jnp.where(spots == spread_ids[:, :width], 1.0, 0.0).astype(BF))
    return jnp.concatenate(pieces, axis=1) if len(pieces) > 1 else pieces[0]


def one_hot_rows(ids, count):
    spots = lax.broadcasted_iota(jnp.int32, (count, ids.shape[1]), 0)
    return jnp.where(spots == ids, 1.0, 0.0).astype(BF)


def call(body, outs, scratch, fast, slow=(), cost=0.5, far=0, keep=True):
    many = isinstance(outs, list)
    full = [(o if isinstance(o[1], tuple) or not isinstance(o[0], int) else (o, BF)) for o in (outs if many else [outs])]
    places = [pltpu.VMEM] * (len(full) - far) + [pltpu.HBM] * far
    shapes = [(place if keep else jax.ShapeDtypeStruct)(shape, dtype) for place, (shape, dtype) in zip(places, full)]
    operands = [pltpu.with_memory_space_constraint(a, pltpu.VMEM) for a in fast]
    operands += [pltpu.with_memory_space_constraint(a, pltpu.HBM) for a in slow]
    specs = [pl.BlockSpec(memory_space=pltpu.VMEM)] * len(fast) + [pl.BlockSpec(memory_space=pltpu.HBM)] * len(slow)
    return pl.pallas_call(
        body,
        out_shape=shapes if many else shapes[0],
        in_specs=specs,
        out_specs=[pl.BlockSpec(memory_space=place) for place in places] if many else pl.BlockSpec(memory_space=places[0]),
        scratch_shapes=scratch,
        compiler_params=pltpu.CompilerParams(vmem_limit_bytes=LIMIT),
        cost_estimate=pl.CostEstimate(flops=int(cost * 1e9), bytes_accessed=0, transcendentals=0),
    )(*operands)


def after(array, *others):
    return lax.optimization_barrier((array,) + others)[0]


MATS = {"e": 3, "n": 2}


def arrays_in(kind):
    return sum(MATS[letter] + 1 for letter in kind)


def weight_shapes(kind, hidden, depth):
    found = []
    for letter in kind:
        found += [(MATS[letter] * depth, hidden), (hidden, depth)]
    return found


def named(kind, refs):
    return dict(zip([letter + name for letter in kind for name in "mb"], refs))


def cut_body(plan, *refs):
    raws = (refs[0], refs[1]), (refs[2], refs[3])
    outs, sem = refs[4:-1], refs[-1]
    part = {"quarter": 2 * lax.axis_index("groups") + lax.axis_index("band"), "whole": 0}
    copies = []
    for (blocks, split, rows), out in zip(plan, outs):
        spot = 0
        for block in blocks:
            for mats, back in raws:
                lanes, count = back.shape[2], mats.shape[1]
                first = pl.ds(pl.multiple_of(part[split] * rows, rows), rows)
                copies.append((mats.at[block, :, first, :], out.at[spot : spot + count]))
                spot += count
                for j in range(2):
                    at = pl.ds(pl.multiple_of(part[split] * 2 * rows + j * rows, rows), rows)
                    copies.append((back.at[block, at, :], out.at[spot, :, j * lanes : (j + 1) * lanes]))
                spot += 1
    started = [pltpu.make_async_copy(src, dst, sem.at[i]) for i, (src, dst) in enumerate(copies)]
    for copy in started:
        copy.start()
    for copy in started:
        copy.wait()


def cut(plan, raws):
    shapes = [(arrays_in("en") * len(blocks), rows, raws[0].shape[3]) for blocks, _, rows in plan]
    copies = sum(6 * len(blocks) for blocks, _, _ in plan)
    return call(functools.partial(cut_body, plan), shapes, [pltpu.SemaphoreType.DMA((copies,))], [], raws)


def put(src, zs, part, half, kind, weights):
    def piece(k, spot):
        return src.at[spot] if len(src.shape) == 3 else src.at[k, spot]

    rows, cols = src.shape[-2:]
    lanes = cols // 2
    spot = 0
    for letter in "en":
        if letter in kind:
            mats, back = weights[letter + "m"], weights[letter + "b"]
            depth = back.shape[1]
            for k, z in enumerate(zs):
                for m in range(MATS[letter]):
                    at = pl.multiple_of(m * depth + z * lanes + part * rows, rows)
                    mats[pl.ds(at, rows), half * cols : (half + 1) * cols] = piece(k, spot + m)[...]
                for j in range(2):
                    at = pl.multiple_of(half * cols + part * 2 * rows + j * rows, rows)
                    into = pl.ds(pl.multiple_of(z * lanes, lanes), lanes)
                    back[pl.ds(at, rows), into] = piece(k, spot + MATS[letter])[:, j * lanes : (j + 1) * lanes]
        spot += MATS[letter] + 1


class Parts:
    def __init__(self, sides, far, kind="en"):
        arrays = [array for side in sides for array in side]
        self.kind, self.sides = kind, len(sides)
        self.far = [i in far for i in range(len(arrays))]
        self.near_operands = [array for array, far in zip(arrays, self.far) if not far]
        self.far_operands = [array for array, far in zip(arrays, self.far) if far]

    def scratch(self, hidden, depth):
        found = [pltpu.VMEM(shape, BF) for shape in weight_shapes(self.kind, hidden, depth)]
        found += [pltpu.VMEM(array.shape, BF) for array in self.far_operands]
        return found + [pltpu.SemaphoreType.DMA((max(len(self.far_operands), 1),))]

    def load(self, near, far, scratch):
        weights, sems = named(self.kind, scratch), scratch[-1]
        staged = scratch[2 * len(self.kind) : -1]
        copies = [pltpu.make_async_copy(src, dst, sems.at[i]) for i, (src, dst) in enumerate(zip(far, staged))]
        for copy in copies:
            copy.start()
        sources, near, staged, waits = [], list(near), list(staged), list(copies)
        for is_far in self.far:
            sources.append((staged.pop(0), waits.pop(0)) if is_far else (near.pop(0), None))
        count = lax.axis_size("mesh")
        z = lax.axis_index("mesh")
        x, y = lax.axis_index("band"), lax.axis_index("groups")
        quarters = [2 * y + x, 2 * y + 1 - x, 2 * (1 - y) + x, 2 * (1 - y) + 1 - x]
        each = len(sources) // self.sides

        def place(kind):
            for wanted in (False, True):
                for i, (src, wait) in enumerate(sources):
                    if self.far[i] != wanted:
                        continue
                    if wait is not None and kind == "e":
                        wait.wait()
                    spot = i % each
                    if spot == 0:
                        put(src, [z], 0, i // each, kind, weights)
                    else:
                        put(src, [z ^ k for k in range(1, count)], quarters[spot - 1], i // each, kind, weights)

        return weights, place


class Whole:
    def __init__(self, arrays, kind="en"):
        self.near_operands, self.far_operands, self.kind = arrays, [], kind

    def scratch(self, hidden, depth):
        return []

    def load(self, near, far, scratch):
        return named(self.kind, near), lambda kind: None


def join_body(*refs):
    blocks = [ref for ref in refs if len(ref.shape) == 4]
    for k, ref in enumerate(refs[: -len(blocks)]):
        for i, block in enumerate(blocks):
            block[k] = ref[i * block.shape[1] : (i + 1) * block.shape[1]]


def join(arrays, blocks, cost=0.5):
    count, rows, cols = arrays[0].shape
    return call(join_body, [(len(arrays), count // blocks, rows, cols)] * blocks, [], arrays, cost=cost)


def lend_body(grid, down, up, low, high):
    low[...] = dot(one_hot(down[...], grid.shape[0]), grid[...]).astype(BF)
    high[...] = dot(one_hot(up[...], grid.shape[0]), grid[...]).astype(BF)


def gather_body(grid, low, high, nodes, slots, targets, out):
    table = jnp.concatenate([grid[...], low[...], high[...]], axis=0)
    depth = grid.shape[1]
    for at in range(0, out.shape[0], ROWS):
        rows = slice(at, at + ROWS)
        out[rows, 0:depth] = dot(one_hot(slots[:, rows], table.shape[0]), table).astype(BF)
        out[rows, depth:] = dot(one_hot(targets[:, rows], nodes.shape[0]), nodes[...]).astype(BF)


def edges_to_nodes(weights, inputs, table, edge_buffer, targets, message, keep):
    for at in range(0, message.shape[0], ROWS):
        rows = slice(at, at + ROWS)
        pre = dot(inputs(rows), table[...])
        normed = normalize(dot(silu(pre).astype(BF), weights["eb"][...]))
        message[rows, :] = normed.astype(BF)
        if keep:
            edge_buffer[rows, :] = (edge_buffer[rows, :].astype(F32) + normed).astype(BF)


def nodes_after(weights, nodes, incoming):
    pre = dot(jnp.concatenate([nodes, incoming], axis=1), weights["nm"][...])
    return (nodes.astype(F32) + normalize(dot(silu(pre).astype(BF), weights["nb"][...]))).astype(BF)


def sum_of(terms, rows=slice(None)):
    total = terms[0][rows, :].astype(F32)
    for term in terms[1:]:
        total = total + term[rows, :].astype(F32)
    return total


def half_edges_body(pack, gathered, *refs):
    count = len(pack.near_operands)
    operands, edges, out, refs = refs[:count], refs[count], refs[count + 1], refs[count + 2 :]
    saved, refs = (refs[:2], refs[2:]) if len(pack.kind) == 2 else ((), refs)
    buffer, sems, *scratch = refs
    fetch = pltpu.make_async_copy(edges, buffer, sems.at[0])
    fetch.start()
    weights, place = pack.load(operands, (), scratch)
    saves = []
    if saved:
        place("n")
        saves = [pltpu.make_async_copy(weights[n], to, sems.at[1 + i]) for i, (n, to) in enumerate(zip(("nm", "nb"), saved))]
    for save in saves:
        save.start()
    place("e")
    fetch.wait()
    for at in range(0, edges.shape[0], ROWS):
        rows = slice(at, at + ROWS)
        pre = dot(jnp.concatenate([gathered[rows, :], buffer[rows, :]], axis=1), weights["em"][...])
        out[rows, :] = dot(silu(pre).astype(BF), weights["eb"][...]).astype(BF)
    for save in saves:
        save.wait()


def half_nodes_body(targets, mine, other, nodes_in, nm_in, nb_in, out, message, nodes, nm, nb, sems):
    pairs = ((nodes_in, nodes), (nm_in, nm), (nb_in, nb))
    fetches = [pltpu.make_async_copy(src, dst, sems.at[i]) for i, (src, dst) in enumerate(pairs)]
    for fetch in fetches:
        fetch.start()
    for at in range(0, message.shape[0], ROWS):
        rows = slice(at, at + ROWS)
        message[rows, :] = normalize(sum_of((mine, other), rows)).astype(BF)
    incoming = dot(one_hot_rows(targets[...], nodes.shape[0]), message[...]).astype(BF)
    for fetch in fetches:
        fetch.wait()
    pre = dot(jnp.concatenate([nodes[...], incoming], axis=1), nm[...])
    out[...] = dot(silu(pre).astype(BF), nb[...]).astype(BF)


def mark_body(source, out):
    out[...] = source[0 : out.shape[0], 0 : out.shape[1]]


def mark(source, cost):
    return call(mark_body, (16, 128), [], [source], cost=cost)


def first_next_body(nodes, lists, mine, other, piece, packed, out, buffer, sem):
    buffer[...] = (nodes[...].astype(F32) + normalize(sum_of((mine, other)))).astype(BF)
    save = pltpu.make_async_copy(buffer, out, sem)
    save.start()
    packed[...] = dot(one_hot(lists[...], nodes.shape[0]), buffer[...]).astype(BF)
    save.wait()


def block_body(pack, last, sent, slots, targets, lists, *refs):
    near, far = len(pack.near_operands), len(pack.far_operands)
    near, refs = refs[:near], refs[near:]
    nodes, edges, far, refs = refs[0], refs[1], refs[2 : 2 + far], refs[2 + far :]
    if last:
        (out, *refs) = refs
    else:
        (packed, saved, edges_saved, *refs) = refs
    message, table, node_buffer, edge_buffer, sems, *scratch = refs
    get_nodes = pltpu.make_async_copy(nodes, node_buffer, sems.at[0])
    get_edges = pltpu.make_async_copy(edges, edge_buffer, sems.at[1])
    get_nodes.start()
    get_edges.start()
    weights, place = pack.load(near, far, scratch)
    place("e")
    em, depth, count = weights["em"], sent.shape[1], nodes.shape[0]
    table[0:depth, :] = em[2 * depth :, :]
    get_nodes.wait()
    table[depth : depth + count, :] = dot(node_buffer[...], em[depth : 2 * depth, :]).astype(BF)
    table[depth + count :, :] = dot(sent[...], em[0:depth, :]).astype(BF)
    get_edges.wait()

    def inputs(rows):
        picks = [one_hot(targets[:, rows], count), one_hot(slots[:, rows], sent.shape[0])]
        return jnp.concatenate([edge_buffer[rows, :]] + picks, axis=1)

    edges_to_nodes(weights, inputs, table, edge_buffer, targets, message, not last)
    if not last:
        save_edges = pltpu.make_async_copy(edge_buffer, edges_saved, sems.at[2])
        save_edges.start()
    place("n")
    incoming = dot(one_hot_rows(targets[...], count), message[...]).astype(BF)
    new = nodes_after(weights, node_buffer[...], incoming)
    if last:
        out[...] = new
        return
    node_buffer[...] = new
    save_nodes = pltpu.make_async_copy(node_buffer, saved, sems.at[3])
    save_nodes.start()
    packed[...] = dot(one_hot(lists[...], count), new).astype(BF)
    save_edges.wait()
    save_nodes.wait()


def over_slices(chunk):
    count = lax.axis_size("mesh")
    return [lax.ppermute(chunk, "mesh", [(i, i ^ k) for i in range(count)]) for k in range(1, count)]


def over_plane(own):
    across = lax.ppermute(own, ("groups", "band"), DIAGONAL)
    along_y = lax.ppermute(own, "groups", SWAP)
    along_x = lax.ppermute(own, "band", SWAP)
    return [along_x, along_y, across]


def swap_width(array):
    return lax.ppermute(array, "width", SWAP)


def weights_whole(edge_mats, node_mats, edge_back, node_back):
    def joined(array, rows, cols):
        axis = {rows: array.ndim - 2, cols: array.ndim - 1}
        for name in ("mesh", "width"):
            array = lax.all_gather(array, name, axis=axis[name], tiled=True)
        return array

    em, nm = joined(edge_mats, "mesh", "width"), joined(node_mats, "mesh", "width")
    eb, nb = joined(edge_back, "width", "mesh"), joined(node_back, "width", "mesh")
    em = em.reshape(em.shape[0], -1, em.shape[3])
    nm = nm.reshape(nm.shape[0], -1, nm.shape[3])
    cols = edge_mats.shape[3]
    at = lax.axis_index("width") * cols
    found = []
    for kind, mats, back in (("e", em[0], eb[0]), ("n", nm[0], nb[0])):
        found.append(Whole([lax.dynamic_slice_in_dim(mats, at, cols, 1), lax.dynamic_slice_in_dim(back, at, cols, 0)], kind))
    return found + [Whole([em[block], eb[block], nm[block], nb[block]]) for block in range(1, em.shape[0])]


def on_device(
    grid_latent,
    mesh_latent,
    grid_edge,
    mesh_edge,
    encoder_slot,
    encoder_target,
    halo_down,
    halo_up,
    send_lists,
    mesh_slot,
    mesh_target,
    edge_mats,
    node_mats,
    edge_back,
    node_back,
):
    depth = grid_latent.shape[1]
    nodes = mesh_latent.shape[0]
    grid_edges, mesh_edges = grid_edge.shape[0], mesh_edge.shape[0]
    sizes = [lax.axis_size(name) for name in ("groups", "mesh", "band", "width")]
    by_parts = sizes == [2, 4, 2, 2] and edge_mats.shape[0] == 3
    halo = halo_down.shape[0]
    line = sizes[1] * sizes[2]
    sent_rows = send_lists.shape[1] * send_lists.shape[2]
    hidden = edge_mats.shape[3] * sizes[3]
    lists = send_lists.reshape(1, -1)
    node_buffer, edge_buffer = pltpu.VMEM((nodes, depth), BF), pltpu.VMEM((mesh_edges, depth), BF)

    lent_down, lent_up = call(
        lend_body, [(halo, depth), (halo, depth)], [], [grid_latent, halo_down[None, :], halo_up[None, :]]
    )
    if by_parts:
        raws = [edge_mats, edge_back, node_mats, node_back]
        slab = edge_mats.shape[2]
        quarter = slab // 4
        [cut0] = cut([((0,), "quarter", quarter)], raws)
        cut12, own0, own1, own2 = cut([((1, 2), "quarter", quarter)] + [((block,), "whole", slab) for block in range(3)], raws)
        turned0 = over_slices(cut0)
        lent_down, lent_up = after(lent_down, turned0[0]), after(lent_up, turned0[0])
    from_upper = lax.ppermute(lent_down, ("mesh", "band"), [(i + 1, i) for i in range(line - 1)])
    from_lower = lax.ppermute(lent_up, ("mesh", "band"), [(i, i + 1) for i in range(line - 1)])
    if by_parts:
        [joined0] = join(turned0[:-1] + [after(turned0[-1], from_upper, from_lower, cut12)], 1)
        plane0 = over_plane(joined0)
        side0 = [own0, joined0] + plane0
        joined1, joined2 = join(over_slices(after(cut12, joined0)), 2, 3.0)
    else:
        packs = weights_whole(edge_mats, node_mats, edge_back, node_back)
    gathered = call(
        gather_body,
        (grid_edges, 2 * depth),
        [],
        [grid_latent, from_lower, from_upper, mesh_latent, encoder_slot[None, :], encoder_target[None, :]],
        cost=1.2,
    )
    if by_parts:
        packs = [Parts([[after(own0, joined1)] + side0[1:]], [])]
    pack = packs[0]
    term, *node_weights = call(
        functools.partial(half_edges_body, pack),
        [((grid_edges, depth), BF)] + [(shape, BF) for shape in (weight_shapes("n", hidden // 2, depth) if by_parts else [])],
        [pltpu.VMEM((grid_edges, depth), BF), pltpu.SemaphoreType.DMA((3,))] + pack.scratch(hidden // 2, depth),
        [gathered] + pack.near_operands,
        [grid_edge],
        cost=3.0,
        far=2 if by_parts else 0,
    )
    if by_parts:
        plane1 = over_plane(after(joined1, term))
    else:
        node_weights = packs[1].near_operands
    before = term
    term = call(
        half_nodes_body,
        (nodes, depth),
        [pltpu.VMEM((grid_edges, depth), BF), node_buffer]
        + [pltpu.VMEM(shape, BF) for shape in weight_shapes("n", hidden // 2, depth)]
        + [pltpu.SemaphoreType.DMA((3,))],
        [encoder_target[None, :], term, swap_width(term)],
        [mesh_latent] + node_weights,
        cost=1.6,
    )
    packed, rows = call(
        first_next_body,
        [(sent_rows, depth), (nodes, depth)],
        [node_buffer, pltpu.SemaphoreType.DMA(())],
        [mesh_latent, lists, term, swap_width(term), mark(term, 5.0)],
        cost=1.6,
        far=1,
    )
    edges = mesh_edge
    slots, targets = mesh_slot[None, :], mesh_target[None, :]
    for block in range(1, edge_mats.shape[0]):
        last = block == edge_mats.shape[0] - 1
        cut_rows = packed.reshape(send_lists.shape[1:] + (depth,))
        sent = lax.all_to_all(cut_rows, ("mesh", "band"), split_axis=0, concat_axis=0, tiled=True).reshape(-1, depth)
        if by_parts:
            if not last:
                plane2 = over_plane(after(joined2, sent))
                side = [own1, joined1] + plane1
            else:
                side = [own2, joined2] + plane2
            other = [swap_width(after(a, before)) for a in side[:2]] + [swap_width(after(a, sent)) for a in side[2:]]
            pack = Parts([side, other], range(7))
            before = sent
        else:
            pack = packs[block + 1]
        table = pltpu.VMEM((depth + nodes + sent_rows, hidden), BF)
        got = call(
            functools.partial(block_body, pack, last),
            (nodes, depth) if last else [(sent_rows, depth), (nodes, depth), (mesh_edges, depth)],
            [edge_buffer, table, node_buffer, edge_buffer, pltpu.SemaphoreType.DMA((4,))] + pack.scratch(hidden, depth),
            [sent, slots, targets, lists] + pack.near_operands,
            [rows, edges] + pack.far_operands,
            cost=6.5,
            far=0 if last else 2,
            keep=not last,
        )
        if last:
            rows = got
        else:
            packed, rows, edges = got
    return rows


def solution(mesh):
    return jax.shard_map(
        on_device,
        mesh=mesh,
        in_specs=(
            P(("groups", "mesh", "band"), None),
            P(("groups", "mesh", "band"), None),
            P(("groups", "mesh", "band"), None),
            P(("groups", "mesh", "band"), None),
            P(("groups", "mesh", "band")),
            P(("groups", "mesh", "band")),
            P(("groups", "mesh", "band")),
            P(("groups", "mesh", "band")),
            P(("groups", "mesh", "band"), None, None),
            P(("groups", "mesh", "band")),
            P(("groups", "mesh", "band")),
            P(None, None, "mesh", "width"),
            P(None, None, "mesh", "width"),
            P(None, "width", "mesh"),
            P(None, "width", "mesh"),
        ),
        out_specs=P(("groups", "mesh", "band"), None),
        check_vma=False,
    )
```

```python
import functools

import jax
import jax.numpy as jnp
from jax import lax
from jax.experimental import pallas as pl
from jax.experimental.pallas import tpu as pltpu
from jax.sharding import PartitionSpec as P

BF = jnp.bfloat16
F32 = jnp.float32
ROWS = 384
SWAP = [(0, 1), (1, 0)]
DIAGONAL = [(0, 3), (3, 0), (1, 2), (2, 1)]
LIMIT = 28 * 2**20


def dot(a, b):
    return jnp.dot(a, b, preferred_element_type=F32)


def silu(v):
    return v * (0.5 * jnp.tanh(0.5 * v) + 0.5)


def normalize(total):
    mean = jnp.mean(total, axis=1, keepdims=True)
    meansq = jnp.mean(total * total, axis=1, keepdims=True)
    return (total - mean) * lax.rsqrt(meansq - mean * mean + 1e-05)


def columns_of(ids):
    return jnp.broadcast_to(ids, (128, ids.shape[1])).T


def one_hot(ids, count):
    spread_ids = columns_of(ids)
    pieces = []
    for at in range(0, count, 128):
        width = min(128, count - at)
        spots = lax.broadcasted_iota(jnp.int32, (ids.shape[1], width), 1) + at
        pieces.append(jnp.where(spots == spread_ids[:, :width], 1.0, 0.0).astype(BF))
    return jnp.concatenate(pieces, axis=1) if len(pieces) > 1 else pieces[0]


def one_hot_rows(ids, count):
    spots = lax.broadcasted_iota(jnp.int32, (count, ids.shape[1]), 0)
    return jnp.where(spots == ids, 1.0, 0.0).astype(BF)


def call(body, outs, scratch, fast, slow=(), cost=0.5, far=0, keep=True):
    many = isinstance(outs, list)
    full = [(o if isinstance(o[1], tuple) or not isinstance(o[0], int) else (o, BF)) for o in (outs if many else [outs])]
    places = [pltpu.VMEM] * (len(full) - far) + [pltpu.HBM] * far
    shapes = [(place if keep else jax.ShapeDtypeStruct)(shape, dtype) for place, (shape, dtype) in zip(places, full)]
    operands = [pltpu.with_memory_space_constraint(a, pltpu.VMEM) for a in fast]
    operands += [pltpu.with_memory_space_constraint(a, pltpu.HBM) for a in slow]
    specs = [pl.BlockSpec(memory_space=pltpu.VMEM)] * len(fast) + [pl.BlockSpec(memory_space=pltpu.HBM)] * len(slow)
    return pl.pallas_call(
        body,
        out_shape=shapes if many else shapes[0],
        in_specs=specs,
        out_specs=[pl.BlockSpec(memory_space=place) for place in places] if many else pl.BlockSpec(memory_space=places[0]),
        scratch_shapes=scratch,
        compiler_params=pltpu.CompilerParams(vmem_limit_bytes=LIMIT),
        cost_estimate=pl.CostEstimate(flops=int(cost * 1e9), bytes_accessed=0, transcendentals=0),
    )(*operands)


def after(array, *others):
    return lax.optimization_barrier((array,) + others)[0]


MATS = {"e": 3, "n": 2}


def arrays_in(kind):
    return sum(MATS[letter] + 1 for letter in kind)


def weight_shapes(kind, hidden, depth):
    found = []
    for letter in kind:
        found += [(MATS[letter] * depth, hidden), (hidden, depth)]
    return found


def named(kind, refs):
    return dict(zip([letter + name for letter in kind for name in "mb"], refs))


def cut_body(plan, *refs):
    raws = (refs[0], refs[1]), (refs[2], refs[3])
    outs, sem = refs[4:-1], refs[-1]
    part = {"quarter": 2 * lax.axis_index("groups") + lax.axis_index("band"), "whole": 0}
    copies = []
    for (blocks, split, rows), out in zip(plan, outs):
        spot = 0
        for block in blocks:
            for mats, back in raws:
                lanes, count = back.shape[2], mats.shape[1]
                first = pl.ds(pl.multiple_of(part[split] * rows, rows), rows)
                copies.append((mats.at[block, :, first, :], out.at[spot : spot + count]))
                spot += count
                for j in range(2):
                    at = pl.ds(pl.multiple_of(part[split] * 2 * rows + j * rows, rows), rows)
                    copies.append((back.at[block, at, :], out.at[spot, :, j * lanes : (j + 1) * lanes]))
                spot += 1
    started = [pltpu.make_async_copy(src, dst, sem.at[i]) for i, (src, dst) in enumerate(copies)]
    for copy in started:
        copy.start()
    for copy in started:
        copy.wait()


def cut(plan, raws):
    shapes = [(arrays_in("en") * len(blocks), rows, raws[0].shape[3]) for blocks, _, rows in plan]
    copies = sum(6 * len(blocks) for blocks, _, _ in plan)
    return call(functools.partial(cut_body, plan), shapes, [pltpu.SemaphoreType.DMA((copies,))], [], raws)


def put(src, zs, part, half, kind, weights):
    def piece(k, spot):
        return src.at[spot] if len(src.shape) == 3 else src.at[k, spot]

    rows, cols = src.shape[-2:]
    lanes = cols // 2
    spot = 0
    for letter in "en":
        if letter in kind:
            mats, back = weights[letter + "m"], weights[letter + "b"]
            depth = back.shape[1]
            for k, z in enumerate(zs):
                for m in range(MATS[letter]):
                    at = pl.multiple_of(m * depth + z * lanes + part * rows, rows)
                    mats[pl.ds(at, rows), half * cols : (half + 1) * cols] = piece(k, spot + m)[...]
                for j in range(2):
                    at = pl.multiple_of(half * cols + part * 2 * rows + j * rows, rows)
                    into = pl.ds(pl.multiple_of(z * lanes, lanes), lanes)
                    back[pl.ds(at, rows), into] = piece(k, spot + MATS[letter])[:, j * lanes : (j + 1) * lanes]
        spot += MATS[letter] + 1


class Parts:
    def __init__(self, sides, far, kind="en"):
        arrays = [array for side in sides for array in side]
        self.kind, self.sides = kind, len(sides)
        self.far = [i in far for i in range(len(arrays))]
        self.near_operands = [array for array, far in zip(arrays, self.far) if not far]
        self.far_operands = [array for array, far in zip(arrays, self.far) if far]

    def scratch(self, hidden, depth):
        found = [pltpu.VMEM(shape, BF) for shape in weight_shapes(self.kind, hidden, depth)]
        found += [pltpu.VMEM(array.shape, BF) for array in self.far_operands]
        return found + [pltpu.SemaphoreType.DMA((max(len(self.far_operands), 1),))]

    def load(self, near, far, scratch):
        weights, sems = named(self.kind, scratch), scratch[-1]
        staged = scratch[2 * len(self.kind) : -1]
        copies = [pltpu.make_async_copy(src, dst, sems.at[i]) for i, (src, dst) in enumerate(zip(far, staged))]
        for copy in copies:
            copy.start()
        sources, near, staged, waits = [], list(near), list(staged), list(copies)
        for is_far in self.far:
            sources.append((staged.pop(0), waits.pop(0)) if is_far else (near.pop(0), None))
        count = lax.axis_size("mesh")
        z = lax.axis_index("mesh")
        x, y = lax.axis_index("band"), lax.axis_index("groups")
        quarters = [2 * y + x, 2 * y + 1 - x, 2 * (1 - y) + x, 2 * (1 - y) + 1 - x]
        each = len(sources) // self.sides

        def place(kind):
            for wanted in (False, True):
                for i, (src, wait) in enumerate(sources):
                    if self.far[i] != wanted:
                        continue
                    if wait is not None and kind == "e":
                        wait.wait()
                    spot = i % each
                    if spot == 0:
                        put(src, [z], 0, i // each, kind, weights)
                    else:
                        put(src, [z ^ k for k in range(1, count)], quarters[spot - 1], i // each, kind, weights)

        return weights, place


class Whole:
    def __init__(self, arrays, kind="en"):
        self.near_operands, self.far_operands, self.kind = arrays, [], kind

    def scratch(self, hidden, depth):
        return []

    def load(self, near, far, scratch):
        return named(self.kind, near), lambda kind: None


def join_body(*refs):
    blocks = [ref for ref in refs if len(ref.shape) == 4]
    for k, ref in enumerate(refs[: -len(blocks)]):
        for i, block in enumerate(blocks):
            block[k] = ref[i * block.shape[1] : (i + 1) * block.shape[1]]


def join(arrays, blocks, cost=0.5):
    count, rows, cols = arrays[0].shape
    return call(join_body, [(len(arrays), count // blocks, rows, cols)] * blocks, [], arrays, cost=cost)


class Copies:
    def __init__(self, sems, at, *plans):
        self.each = []
        for src, dst, pieces in plans:
            rows = src.shape[0] // pieces
            cuts = [slice(i * rows, (i + 1) * rows) for i in range(pieces)]
            self.each.append([pltpu.make_async_copy(src.at[cut], dst.at[cut], sems.at[at + i]) for i, cut in enumerate(cuts)])
            at += pieces
        for copy in sum(self.each, []):
            copy.start()

    def wait(self, *which):
        for i in which:
            for copy in self.each[i]:
                copy.wait()


def lend_body(grid_in, down_in, up_in, low, high, grid, down, up, sems):
    copies = Copies(sems, 0, (down_in, down, 1), (up_in, up, 1), (grid_in, grid, 1))
    copies.wait(0, 1, 2)
    low[...] = dot(one_hot(down[...], grid.shape[0]), grid[...]).astype(BF)
    high[...] = dot(one_hot(up[...], grid.shape[0]), grid[...]).astype(BF)


def gather_body(grid, low, high, nodes, slots, targets, edges, out, sem):
    depth = grid.shape[1]
    beside = pltpu.make_async_copy(edges, out.at[:, 2 * depth :], sem)
    beside.start()
    table = jnp.concatenate([grid[...], low[...], high[...]], axis=0)
    for at in range(0, out.shape[0], ROWS):
        rows = slice(at, at + ROWS)
        out[rows, 0:depth] = dot(one_hot(slots[:, rows], table.shape[0]), table).astype(BF)
        out[rows, depth : 2 * depth] = dot(one_hot(targets[:, rows], nodes.shape[0]), nodes[...]).astype(BF)
    beside.wait()


def edges_to_nodes(weights, inputs, table, edge_buffer, targets, message, keep):
    for at in range(0, message.shape[0], ROWS):
        rows = slice(at, at + ROWS)
        pre = dot(inputs(rows), table[...])
        normed = normalize(dot(silu(pre).astype(BF), weights["eb"][...]))
        message[rows, :] = normed.astype(BF)
        if keep:
            edge_buffer[rows, :] = (edge_buffer[rows, :].astype(F32) + normed).astype(BF)


def nodes_after(weights, nodes, incoming):
    pre = dot(jnp.concatenate([nodes, incoming], axis=1), weights["nm"][...])
    return (nodes.astype(F32) + normalize(dot(silu(pre).astype(BF), weights["nb"][...]))).astype(BF)


def sum_of(terms, rows=slice(None)):
    total = terms[0][rows, :].astype(F32)
    for term in terms[1:]:
        total = total + term[rows, :].astype(F32)
    return total


def half_edges_body(pack, gathered, *refs):
    count = len(pack.near_operands)
    operands, out, refs = refs[:count], refs[count], refs[count + 1 :]
    saved, refs = (refs[:2], refs[2:]) if len(pack.kind) == 2 else ((), refs)
    sems, *scratch = refs
    weights, place = pack.load(operands, (), scratch)
    saves = []
    if saved:
        place("n")
        saves = [pltpu.make_async_copy(weights[n], to, sems.at[i]) for i, (n, to) in enumerate(zip(("nm", "nb"), saved))]
    for save in saves:
        save.start()
    place("e")
    for at in range(0, gathered.shape[0], ROWS):
        rows = slice(at, at + ROWS)
        pre = dot(gathered[rows, :], weights["em"][...])
        out[rows, :] = dot(silu(pre).astype(BF), weights["eb"][...]).astype(BF)
    for save in saves:
        save.wait()


def half_nodes_body(targets, mine, other, nodes_in, nm_in, nb_in, out, message, nodes, nm, nb, sems):
    pairs = ((nodes_in, nodes), (nm_in, nm), (nb_in, nb))
    fetches = [pltpu.make_async_copy(src, dst, sems.at[i]) for i, (src, dst) in enumerate(pairs)]
    for fetch in fetches:
        fetch.start()
    for at in range(0, message.shape[0], ROWS):
        rows = slice(at, at + ROWS)
        message[rows, :] = normalize(sum_of((mine, other), rows)).astype(BF)
    incoming = dot(one_hot_rows(targets[...], nodes.shape[0]), message[...]).astype(BF)
    for fetch in fetches:
        fetch.wait()
    pre = dot(jnp.concatenate([nodes[...], incoming], axis=1), nm[...])
    out[...] = dot(silu(pre).astype(BF), nb[...]).astype(BF)


def mark_body(source, out):
    out[...] = source[0 : out.shape[0], 0 : out.shape[1]]


def mark(source, cost):
    return call(mark_body, (16, 128), [], [source], cost=cost)


def first_next_body(nodes, lists, mine, other, piece, packed, out, buffer, sem):
    buffer[...] = (nodes[...].astype(F32) + normalize(sum_of((mine, other)))).astype(BF)
    save = pltpu.make_async_copy(buffer, out, sem)
    save.start()
    packed[...] = dot(one_hot(lists[...], nodes.shape[0]), buffer[...]).astype(BF)
    save.wait()


def block_body(pack, last, sent, slots, targets, lists, *refs):
    near, far = len(pack.near_operands), len(pack.far_operands)
    near, refs = refs[:near], refs[near:]
    nodes, edges, far, refs = refs[0], refs[1], refs[2 : 2 + far], refs[2 + far :]
    if last:
        (out, *refs) = refs
    else:
        (packed, saved, edges_saved, *refs) = refs
    message, table, node_buffer, edge_buffer, sems, *scratch = refs
    get_nodes = pltpu.make_async_copy(nodes, node_buffer, sems.at[0])
    get_edges = pltpu.make_async_copy(edges, edge_buffer, sems.at[1])
    get_nodes.start()
    get_edges.start()
    weights, place = pack.load(near, far, scratch)
    place("e")
    em, depth, count = weights["em"], sent.shape[1], nodes.shape[0]
    table[0:depth, :] = em[2 * depth :, :]
    get_nodes.wait()
    table[depth : depth + count, :] = dot(node_buffer[...], em[depth : 2 * depth, :]).astype(BF)
    table[depth + count :, :] = dot(sent[...], em[0:depth, :]).astype(BF)
    get_edges.wait()

    def inputs(rows):
        picks = [one_hot(targets[:, rows], count), one_hot(slots[:, rows], sent.shape[0])]
        return jnp.concatenate([edge_buffer[rows, :]] + picks, axis=1)

    edges_to_nodes(weights, inputs, table, edge_buffer, targets, message, not last)
    if not last:
        save_edges = pltpu.make_async_copy(edge_buffer, edges_saved, sems.at[2])
        save_edges.start()
    place("n")
    incoming = dot(one_hot_rows(targets[...], count), message[...]).astype(BF)
    new = nodes_after(weights, node_buffer[...], incoming)
    if last:
        out[...] = new
        return
    node_buffer[...] = new
    save_nodes = pltpu.make_async_copy(node_buffer, saved, sems.at[3])
    save_nodes.start()
    packed[...] = dot(one_hot(lists[...], count), new).astype(BF)
    save_edges.wait()
    save_nodes.wait()


def over_slices(chunk):
    count = lax.axis_size("mesh")
    return [lax.ppermute(chunk, "mesh", [(i, i ^ k) for i in range(count)]) for k in range(1, count)]


def over_plane(own):
    across = lax.ppermute(own, ("groups", "band"), DIAGONAL)
    along_y = lax.ppermute(own, "groups", SWAP)
    along_x = lax.ppermute(own, "band", SWAP)
    return [along_x, along_y, across]


def swap_width(array):
    return lax.ppermute(array, "width", SWAP)


def weights_whole(edge_mats, node_mats, edge_back, node_back):
    def joined(array, rows, cols):
        axis = {rows: array.ndim - 2, cols: array.ndim - 1}
        for name in ("mesh", "width"):
            array = lax.all_gather(array, name, axis=axis[name], tiled=True)
        return array

    em, nm = joined(edge_mats, "mesh", "width"), joined(node_mats, "mesh", "width")
    eb, nb = joined(edge_back, "width", "mesh"), joined(node_back, "width", "mesh")
    em = em.reshape(em.shape[0], -1, em.shape[3])
    nm = nm.reshape(nm.shape[0], -1, nm.shape[3])
    cols = edge_mats.shape[3]
    at = lax.axis_index("width") * cols
    found = []
    for kind, mats, back in (("e", em[0], eb[0]), ("n", nm[0], nb[0])):
        found.append(Whole([lax.dynamic_slice_in_dim(mats, at, cols, 1), lax.dynamic_slice_in_dim(back, at, cols, 0)], kind))
    return found + [Whole([em[block], eb[block], nm[block], nb[block]]) for block in range(1, em.shape[0])]


def on_device(
    grid_latent,
    mesh_latent,
    grid_edge,
    mesh_edge,
    encoder_slot,
    encoder_target,
    halo_down,
    halo_up,
    send_lists,
    mesh_slot,
    mesh_target,
    edge_mats,
    node_mats,
    edge_back,
    node_back,
):
    depth = grid_latent.shape[1]
    nodes = mesh_latent.shape[0]
    grid_edges, mesh_edges = grid_edge.shape[0], mesh_edge.shape[0]
    sizes = [lax.axis_size(name) for name in ("groups", "mesh", "band", "width")]
    by_parts = sizes == [2, 4, 2, 2] and edge_mats.shape[0] == 3
    halo = halo_down.shape[0]
    line = sizes[1] * sizes[2]
    sent_rows = send_lists.shape[1] * send_lists.shape[2]
    hidden = edge_mats.shape[3] * sizes[3]
    lists = send_lists.reshape(1, -1)
    lists_back = send_lists[:, ::-1].reshape(1, -1)
    node_buffer, edge_buffer = pltpu.VMEM((nodes, depth), BF), pltpu.VMEM((mesh_edges, depth), BF)

    lent_down, lent_up = call(
        lend_body,
        [(halo, depth), (halo, depth)],
        [pltpu.VMEM(grid_latent.shape, BF)] + [pltpu.VMEM((1, halo), jnp.int32)] * 2 + [pltpu.SemaphoreType.DMA((3,))],
        [],
        [grid_latent, halo_down[None, :], halo_up[None, :]],
    )
    if by_parts:
        raws = [edge_mats, edge_back, node_mats, node_back]
        slab = edge_mats.shape[2]
        quarter = slab // 4
        [cut0] = cut([((0,), "quarter", quarter)], raws)
        cut12, own0, own1, own2 = cut([((1, 2), "quarter", quarter)] + [((block,), "whole", slab) for block in range(3)], raws)
        turned0 = over_slices(cut0)
        lent_down, lent_up = after(lent_down, turned0[0]), after(lent_up, turned0[0])
    from_upper = lax.ppermute(lent_down, ("mesh", "band"), [(i + 1, i) for i in range(line - 1)])
    from_lower = lax.ppermute(lent_up, ("mesh", "band"), [(i, i + 1) for i in range(line - 1)])
    if by_parts:
        [joined0] = join(turned0[:-1] + [after(turned0[-1], from_upper, from_lower, cut12)], 1)
        plane0 = over_plane(joined0)
        side0 = [own0, joined0] + plane0
        joined1, joined2 = join(over_slices(after(cut12, joined0)), 2, 3.0)
    else:
        packs = weights_whole(edge_mats, node_mats, edge_back, node_back)
    gathered = call(
        gather_body,
        (grid_edges, 3 * depth),
        [pltpu.SemaphoreType.DMA(())],
        [grid_latent, from_lower, from_upper, mesh_latent, encoder_slot[None, :], encoder_target[None, :]],
        [grid_edge],
        cost=1.2,
    )
    if by_parts:
        packs = [Parts([[after(own0, joined1)] + side0[1:]], [])]
    pack = packs[0]
    term, *node_weights = call(
        functools.partial(half_edges_body, pack),
        [((grid_edges, depth), BF)] + [(shape, BF) for shape in (weight_shapes("n", hidden // 2, depth) if by_parts else [])],
        [pltpu.SemaphoreType.DMA((2,))] + pack.scratch(hidden // 2, depth),
        [gathered] + pack.near_operands,
        cost=3.0,
        far=2 if by_parts else 0,
    )
    if by_parts:
        plane1 = over_plane(after(joined1, term))
    else:
        node_weights = packs[1].near_operands
    before = term
    term = call(
        half_nodes_body,
        (nodes, depth),
        [pltpu.VMEM((grid_edges, depth), BF), node_buffer]
        + [pltpu.VMEM(shape, BF) for shape in weight_shapes("n", hidden // 2, depth)]
        + [pltpu.SemaphoreType.DMA((3,))],
        [encoder_target[None, :], term, swap_width(term)],
        [mesh_latent] + node_weights,
        cost=1.6,
    )
    packed, rows = call(
        first_next_body,
        [(sent_rows, depth), (nodes, depth)],
        [node_buffer, pltpu.SemaphoreType.DMA(())],
        [mesh_latent, lists_back, term, swap_width(term), mark(term, 5.0)],
        cost=1.6,
        far=1,
    )
    edges = mesh_edge
    slots, targets = mesh_slot[None, :], mesh_target[None, :]
    room = send_lists.shape[2]
    slots_back = ((line - 1 - mesh_slot // room) * room + mesh_slot % room)[None, :]
    for block in range(1, edge_mats.shape[0]):
        last = block == edge_mats.shape[0] - 1
        cut_rows = packed.reshape(send_lists.shape[1:] + (depth,))
        order = [list(reversed(range(line)))]
        sent = lax.all_to_all(
            cut_rows, ("mesh", "band"), split_axis=0, concat_axis=0, axis_index_groups=order, tiled=True
        ).reshape(-1, depth)
        if by_parts:
            if not last:
                plane2 = over_plane(after(joined2, sent))
                side = [own1, joined1] + plane1
            else:
                side = [own2, joined2] + plane2
            other = [swap_width(after(a, before)) for a in side[:2]] + [swap_width(after(a, sent)) for a in side[2:]]
            pack = Parts([side, other], range(7))
            before = sent
        else:
            pack = packs[block + 1]
        table = pltpu.VMEM((depth + nodes + sent_rows, hidden), BF)
        got = call(
            functools.partial(block_body, pack, last),
            (nodes, depth) if last else [(sent_rows, depth), (nodes, depth), (mesh_edges, depth)],
            [edge_buffer, table, node_buffer, edge_buffer, pltpu.SemaphoreType.DMA((4,))] + pack.scratch(hidden, depth),
            [sent, slots_back, targets, lists_back] + pack.near_operands,
            [rows, edges] + pack.far_operands,
            cost=6.5,
            far=0 if last else 2,
            keep=not last,
        )
        if last:
            rows = got
        else:
            packed, rows, edges = got
    return rows


def solution(mesh):
    return jax.shard_map(
        on_device,
        mesh=mesh,
        in_specs=(
            P(("groups", "mesh", "band"), None),
            P(("groups", "mesh", "band"), None),
            P(("groups", "mesh", "band"), None),
            P(("groups", "mesh", "band"), None),
            P(("groups", "mesh", "band")),
            P(("groups", "mesh", "band")),
            P(("groups", "mesh", "band")),
            P(("groups", "mesh", "band")),
            P(("groups", "mesh", "band"), None, None),
            P(("groups", "mesh", "band")),
            P(("groups", "mesh", "band")),
            P(None, None, "mesh", "width"),
            P(None, None, "mesh", "width"),
            P(None, "width", "mesh"),
            P(None, "width", "mesh"),
        ),
        out_specs=P(("groups", "mesh", "band"), None),
        check_vma=False,
    )
```

```python
import functools

import jax
import jax.numpy as jnp
from jax import lax
from jax.experimental import pallas as pl
from jax.experimental.pallas import tpu as pltpu
from jax.sharding import PartitionSpec as P

BF = jnp.bfloat16
F32 = jnp.float32
ROWS = 384
SWAP = [(0, 1), (1, 0)]
DIAGONAL = [(0, 3), (3, 0), (1, 2), (2, 1)]
LIMIT = 28 * 2**20


def dot(a, b):
    return jnp.dot(a, b, preferred_element_type=F32)


def silu(v):
    return v * (0.5 * jnp.tanh(0.5 * v) + 0.5)


def normalize(total):
    mean = jnp.mean(total, axis=1, keepdims=True)
    meansq = jnp.mean(total * total, axis=1, keepdims=True)
    return (total - mean) * lax.rsqrt(meansq - mean * mean + 1e-05)


def columns_of(ids):
    return jnp.broadcast_to(ids, (128, ids.shape[1])).T


def one_hot(ids, count):
    spread_ids = columns_of(ids)
    pieces = []
    for at in range(0, count, 128):
        width = min(128, count - at)
        spots = lax.broadcasted_iota(jnp.int32, (ids.shape[1], width), 1) + at
        pieces.append(jnp.where(spots == spread_ids[:, :width], 1.0, 0.0).astype(BF))
    return jnp.concatenate(pieces, axis=1) if len(pieces) > 1 else pieces[0]


def one_hot_rows(ids, count):
    spots = lax.broadcasted_iota(jnp.int32, (count, ids.shape[1]), 0)
    return jnp.where(spots == ids, 1.0, 0.0).astype(BF)


def call(body, outs, scratch, fast, slow=(), free=(), cost=0.5, far=0, keep=True):
    many = isinstance(outs, list)
    full = [(o if isinstance(o[1], tuple) or not isinstance(o[0], int) else (o, BF)) for o in (outs if many else [outs])]
    places = [pltpu.VMEM] * (len(full) - far) + [pltpu.HBM] * far
    shapes = [(place if keep else jax.ShapeDtypeStruct)(shape, dtype) for place, (shape, dtype) in zip(places, full)]
    operands = [pltpu.with_memory_space_constraint(a, pltpu.VMEM) for a in fast]
    operands += [pltpu.with_memory_space_constraint(a, pltpu.HBM) for a in slow]
    operands += list(free)
    specs = [pl.BlockSpec(memory_space=pltpu.VMEM)] * len(fast) + [pl.BlockSpec(memory_space=pltpu.HBM)] * len(slow)
    specs += [pl.BlockSpec(memory_space=pl.ANY)] * len(free)
    return pl.pallas_call(
        body,
        out_shape=shapes if many else shapes[0],
        in_specs=specs,
        out_specs=[pl.BlockSpec(memory_space=place) for place in places] if many else pl.BlockSpec(memory_space=places[0]),
        scratch_shapes=scratch,
        compiler_params=pltpu.CompilerParams(vmem_limit_bytes=LIMIT),
        cost_estimate=pl.CostEstimate(flops=int(cost * 1e9), bytes_accessed=0, transcendentals=0),
    )(*operands)


def after(array, *others):
    return lax.optimization_barrier((array,) + others)[0]


MATS = {"e": 3, "n": 2}


def arrays_in(kind):
    return sum(MATS[letter] + 1 for letter in kind)


def weight_shapes(kind, hidden, depth):
    found = []
    for letter in kind:
        found += [(MATS[letter] * depth, hidden), (hidden, depth)]
    return found


def named(kind, refs):
    return dict(zip([letter + name for letter in kind for name in "mb"], refs))


def cut_body(plan, *refs):
    raws = (refs[0], refs[1]), (refs[2], refs[3])
    outs, sem = refs[4:-1], refs[-1]
    part = {"quarter": 2 * lax.axis_index("groups") + lax.axis_index("band"), "whole": 0}
    copies = []
    for (blocks, split, rows), out in zip(plan, outs):
        spot = 0
        for block in blocks:
            for mats, back in raws:
                lanes, count = back.shape[2], mats.shape[1]
                first = pl.ds(pl.multiple_of(part[split] * rows, rows), rows)
                copies.append((mats.at[block, :, first, :], out.at[spot : spot + count]))
                spot += count
                for j in range(2):
                    at = pl.ds(pl.multiple_of(part[split] * 2 * rows + j * rows, rows), rows)
                    copies.append((back.at[block, at, :], out.at[spot, :, j * lanes : (j + 1) * lanes]))
                spot += 1
    started = [pltpu.make_async_copy(src, dst, sem.at[i]) for i, (src, dst) in enumerate(copies)]
    for copy in started:
        copy.start()
    for copy in started:
        copy.wait()


def cut(plan, raws):
    shapes = [(arrays_in("en") * len(blocks), rows, raws[0].shape[3]) for blocks, _, rows in plan]
    copies = sum(6 * len(blocks) for blocks, _, _ in plan)
    return call(functools.partial(cut_body, plan), shapes, [pltpu.SemaphoreType.DMA((copies,))], [], raws)


def put(src, zs, part, half, kind, weights):
    def piece(k, spot):
        return src.at[spot] if len(src.shape) == 3 else src.at[k, spot]

    rows, cols = src.shape[-2:]
    lanes = cols // 2
    spot = 0
    for letter in "en":
        if letter in kind:
            mats, back = weights[letter + "m"], weights[letter + "b"]
            depth = back.shape[1]
            for k, z in enumerate(zs):
                for m in range(MATS[letter]):
                    at = pl.multiple_of(m * depth + z * lanes + part * rows, rows)
                    mats[pl.ds(at, rows), half * cols : (half + 1) * cols] = piece(k, spot + m)[...]
                for j in range(2):
                    at = pl.multiple_of(half * cols + part * 2 * rows + j * rows, rows)
                    into = pl.ds(pl.multiple_of(z * lanes, lanes), lanes)
                    back[pl.ds(at, rows), into] = piece(k, spot + MATS[letter])[:, j * lanes : (j + 1) * lanes]
        spot += MATS[letter] + 1


class Parts:
    def __init__(self, sides, far, kind="en"):
        arrays = [array for side in sides for array in side]
        self.kind, self.sides = kind, len(sides)
        self.far = [i in far for i in range(len(arrays))]
        self.near_operands = [array for array, far in zip(arrays, self.far) if not far]
        self.far_operands = [array for array, far in zip(arrays, self.far) if far]

    def scratch(self, hidden, depth):
        found = [pltpu.VMEM(shape, BF) for shape in weight_shapes(self.kind, hidden, depth)]
        found += [pltpu.VMEM(array.shape, BF) for array in self.far_operands]
        return found + [pltpu.SemaphoreType.DMA((max(len(self.far_operands), 1),))]

    def load(self, near, far, scratch):
        weights, sems = named(self.kind, scratch), scratch[-1]
        staged = scratch[2 * len(self.kind) : -1]
        copies = [pltpu.make_async_copy(src, dst, sems.at[i]) for i, (src, dst) in enumerate(zip(far, staged))]
        for copy in copies:
            copy.start()
        sources, near, staged, waits = [], list(near), list(staged), list(copies)
        for is_far in self.far:
            sources.append((staged.pop(0), waits.pop(0)) if is_far else (near.pop(0), None))
        count = lax.axis_size("mesh")
        z = lax.axis_index("mesh")
        x, y = lax.axis_index("band"), lax.axis_index("groups")
        quarters = [2 * y + x, 2 * y + 1 - x, 2 * (1 - y) + x, 2 * (1 - y) + 1 - x]
        each = len(sources) // self.sides

        def place(kind):
            for wanted in (False, True):
                for i, (src, wait) in enumerate(sources):
                    if self.far[i] != wanted:
                        continue
                    if wait is not None and kind == "e":
                        wait.wait()
                    spot = i % each
                    if spot == 0:
                        put(src, [z], 0, i // each, kind, weights)
                    else:
                        put(src, [z ^ k for k in range(1, count)], quarters[spot - 1], i // each, kind, weights)

        return weights, place


class Whole:
    def __init__(self, arrays, kind="en"):
        self.near_operands, self.far_operands, self.kind = arrays, [], kind

    def scratch(self, hidden, depth):
        return []

    def load(self, near, far, scratch):
        return named(self.kind, near), lambda kind: None


def join_body(*refs):
    blocks = [ref for ref in refs if len(ref.shape) == 4]
    for k, ref in enumerate(refs[: -len(blocks)]):
        for i, block in enumerate(blocks):
            block[k] = ref[i * block.shape[1] : (i + 1) * block.shape[1]]


def join(arrays, blocks, cost=0.5):
    count, rows, cols = arrays[0].shape
    return call(join_body, [(len(arrays), count // blocks, rows, cols)] * blocks, [], arrays, cost=cost)


class Copies:
    def __init__(self, sems, at, *plans):
        self.each = []
        for src, dst, pieces in plans:
            rows = src.shape[0] // pieces
            cuts = [slice(i * rows, (i + 1) * rows) for i in range(pieces)]
            self.each.append([pltpu.make_async_copy(src.at[cut], dst.at[cut], sems.at[at + i]) for i, cut in enumerate(cuts)])
            at += pieces
        for copy in sum(self.each, []):
            copy.start()

    def wait(self, *which):
        for i in which:
            for copy in self.each[i]:
                copy.wait()


def lend_body(grid_in, down_in, up_in, low, high, grid, down, up, sems):
    copies = Copies(sems, 0, (down_in, down, 1), (up_in, up, 1), (grid_in, grid, 1))
    copies.wait(0, 1, 2)
    low[...] = dot(one_hot(down[...], grid.shape[0]), grid[...]).astype(BF)
    high[...] = dot(one_hot(up[...], grid.shape[0]), grid[...]).astype(BF)


def gather_body(grid, low, high, nodes, slots, targets, edges, out, sem):
    depth = grid.shape[1]
    beside = pltpu.make_async_copy(edges, out.at[:, 2 * depth :], sem)
    beside.start()
    table = jnp.concatenate([grid[...], low[...], high[...]], axis=0)
    for at in range(0, out.shape[0], ROWS):
        rows = slice(at, at + ROWS)
        out[rows, 0:depth] = dot(one_hot(slots[:, rows], table.shape[0]), table).astype(BF)
        out[rows, depth : 2 * depth] = dot(one_hot(targets[:, rows], nodes.shape[0]), nodes[...]).astype(BF)
    beside.wait()


def edges_to_nodes(weights, inputs, table, edge_buffer, targets, message, keep):
    for at in range(0, message.shape[0], ROWS):
        rows = slice(at, at + ROWS)
        pre = dot(inputs(rows), table[...])
        normed = normalize(dot(silu(pre).astype(BF), weights["eb"][...]))
        message[rows, :] = normed.astype(BF)
        if keep:
            edge_buffer[rows, :] = (edge_buffer[rows, :].astype(F32) + normed).astype(BF)


def nodes_after(weights, nodes, incoming):
    pre = dot(jnp.concatenate([nodes, incoming], axis=1), weights["nm"][...])
    return (nodes.astype(F32) + normalize(dot(silu(pre).astype(BF), weights["nb"][...]))).astype(BF)


def sum_of(terms, rows=slice(None)):
    total = terms[0][rows, :].astype(F32)
    for term in terms[1:]:
        total = total + term[rows, :].astype(F32)
    return total


def half_edges_body(pack, gathered, *refs):
    count = len(pack.near_operands)
    operands, out, refs = refs[:count], refs[count], refs[count + 1 :]
    saved, refs = (refs[:2], refs[2:]) if len(pack.kind) == 2 else ((), refs)
    sems, *scratch = refs
    weights, place = pack.load(operands, (), scratch)
    saves = []
    if saved:
        place("n")
        saves = [pltpu.make_async_copy(weights[n], to, sems.at[i]) for i, (n, to) in enumerate(zip(("nm", "nb"), saved))]
    for save in saves:
        save.start()
    place("e")
    pre = dot(gathered[...], weights["em"][...])
    out[...] = dot(silu(pre).astype(BF), weights["eb"][...]).astype(BF)
    for save in saves:
        save.wait()


def half_nodes_body(targets, mine, other, nodes_in, nm_in, nb_in, out, message, nodes, nm, nb, sems):
    pairs = ((nodes_in, nodes), (nm_in, nm), (nb_in, nb))
    fetches = [pltpu.make_async_copy(src, dst, sems.at[i]) for i, (src, dst) in enumerate(pairs)]
    for fetch in fetches:
        fetch.start()
    for at in range(0, message.shape[0], ROWS):
        rows = slice(at, at + ROWS)
        message[rows, :] = normalize(sum_of((mine, other), rows)).astype(BF)
    incoming = dot(one_hot_rows(targets[...], nodes.shape[0]), message[...]).astype(BF)
    for fetch in fetches:
        fetch.wait()
    pre = dot(jnp.concatenate([nodes[...], incoming], axis=1), nm[...])
    out[...] = dot(silu(pre).astype(BF), nb[...]).astype(BF)


def mark_body(source, out):
    out[...] = source[0 : out.shape[0], 0 : out.shape[1]]


def mark(source, cost):
    return call(mark_body, (16, 128), [], [source], cost=cost)


def first_next_body(nodes, lists, mine, other, piece, packed, out, buffer, sem):
    buffer[...] = (nodes[...].astype(F32) + normalize(sum_of((mine, other)))).astype(BF)
    save = pltpu.make_async_copy(buffer, out, sem)
    save.start()
    packed[...] = dot(one_hot(lists[...], nodes.shape[0]), buffer[...]).astype(BF)
    save.wait()


def block_body(pack, last, sent, slots, targets, lists, *refs):
    near, far = len(pack.near_operands), len(pack.far_operands)
    near, refs = refs[:near], refs[near:]
    nodes, edges, far, refs = refs[0], refs[1], refs[2 : 2 + far], refs[2 + far :]
    if last:
        (out, *refs) = refs
    else:
        (packed, saved, edges_saved, *refs) = refs
    message, table, node_buffer, edge_buffer, sems, *scratch = refs
    get_nodes = pltpu.make_async_copy(nodes, node_buffer, sems.at[0])
    get_edges = pltpu.make_async_copy(edges, edge_buffer, sems.at[1])
    get_nodes.start()
    get_edges.start()
    weights, place = pack.load(near, far, scratch)
    place("e")
    em, depth, count = weights["em"], sent.shape[1], nodes.shape[0]
    table[0:depth, :] = em[2 * depth :, :]
    get_nodes.wait()
    table[depth : depth + count, :] = dot(node_buffer[...], em[depth : 2 * depth, :]).astype(BF)
    table[depth + count :, :] = dot(sent[...], em[0:depth, :]).astype(BF)
    get_edges.wait()

    def inputs(rows):
        picks = [one_hot(targets[:, rows], count), one_hot(slots[:, rows], sent.shape[0])]
        return jnp.concatenate([edge_buffer[rows, :]] + picks, axis=1)

    edges_to_nodes(weights, inputs, table, edge_buffer, targets, message, not last)
    if not last:
        save_edges = pltpu.make_async_copy(edge_buffer, edges_saved, sems.at[2])
        save_edges.start()
    place("n")
    incoming = dot(one_hot_rows(targets[...], count), message[...]).astype(BF)
    new = nodes_after(weights, node_buffer[...], incoming)
    if last:
        out[...] = new
        return
    node_buffer[...] = new
    save_nodes = pltpu.make_async_copy(node_buffer, saved, sems.at[3])
    save_nodes.start()
    packed[...] = dot(one_hot(lists[...], count), new).astype(BF)
    save_edges.wait()
    save_nodes.wait()


def picks_of(targets, slots, rows, count, room):
    return [one_hot(targets[:, rows], count), one_hot(slots[:, rows], room)]


def fill_table(table, weights, nodes, sent):
    em, depth, count = weights["em"], sent.shape[1], nodes.shape[0]
    table[0:depth, :] = em[2 * depth :, :]
    table[depth : depth + count, :] = dot(nodes[...], em[depth : 2 * depth, :]).astype(BF)
    table[depth + count :, :] = dot(sent[...], em[0:depth, :]).astype(BF)


def own_half_body(pack, sent, slots, targets, nodes_in, edges_in, *refs):
    far, refs = refs[:7], refs[7:]
    total, nm, nb, own_there, joined_there, nodes, edges, table, sems, *scratch = refs
    pairs = ((nodes_in, nodes), (edges_in, edges), (far[5], own_there), (far[6], joined_there))
    copies = [pltpu.make_async_copy(src, dst, sems.at[i]) for i, (src, dst) in enumerate(pairs)]
    weights, place = pack.load((), far[:5], scratch)
    for copy in copies:
        copy.start()
    place("e")
    copies[0].wait()
    fill_table(table, weights, nodes, sent)
    copies[1].wait()
    for at in range(0, edges.shape[0], edges.shape[0]):
        rows = slice(at, at + edges.shape[0])
        picks = picks_of(targets, slots, rows, nodes.shape[0], sent.shape[0])
        pre = dot(jnp.concatenate([edges[rows, :]] + picks, axis=1), table[...])
        total[rows, :] = dot(silu(pre).astype(BF), weights["eb"][...])
    place("n")
    nm[...] = weights["nm"][...]
    nb[...] = weights["nb"][...]
    copies[2].wait()
    copies[3].wait()


def other_half_body(pack, sent, slots, targets, total, nm, nb, nodes, edges, *refs):
    near, out, message, table, scratch = refs[:5], refs[5], refs[6], refs[7], refs[8:]
    weights, place = pack.load(near, (), scratch)
    place("e")
    fill_table(table, weights, nodes, sent)
    for at in range(0, edges.shape[0], edges.shape[0]):
        rows = slice(at, at + edges.shape[0])
        picks = picks_of(targets, slots, rows, nodes.shape[0], sent.shape[0])
        pre = dot(jnp.concatenate([edges[rows, :]] + picks, axis=1), table[...])
        sums = total[rows, :] + dot(silu(pre).astype(BF), weights["eb"][...])
        message[rows, :] = normalize(sums).astype(BF)
    place("n")
    incoming = dot(one_hot_rows(targets[...], nodes.shape[0]), message[...]).astype(BF)
    both = jnp.concatenate([nodes[...], incoming], axis=1)
    sums = dot(silu(dot(both, nm[...])).astype(BF), nb[...])
    sums = sums + dot(silu(dot(both, weights["nm"][...])).astype(BF), weights["nb"][...])
    out[...] = (nodes[...].astype(F32) + normalize(sums)).astype(BF)


def over_slices(chunk):
    count = lax.axis_size("mesh")
    return [lax.ppermute(chunk, "mesh", [(i, i ^ k) for i in range(count)]) for k in range(1, count)]


def over_plane(own):
    across = lax.ppermute(own, ("groups", "band"), DIAGONAL)
    along_y = lax.ppermute(own, "groups", SWAP)
    along_x = lax.ppermute(own, "band", SWAP)
    return [along_x, along_y, across]


def swap_width(array):
    return lax.ppermute(array, "width", SWAP)


def weights_whole(edge_mats, node_mats, edge_back, node_back):
    def joined(array, rows, cols):
        axis = {rows: array.ndim - 2, cols: array.ndim - 1}
        for name in ("mesh", "width"):
            array = lax.all_gather(array, name, axis=axis[name], tiled=True)
        return array

    em, nm = joined(edge_mats, "mesh", "width"), joined(node_mats, "mesh", "width")
    eb, nb = joined(edge_back, "width", "mesh"), joined(node_back, "width", "mesh")
    em = em.reshape(em.shape[0], -1, em.shape[3])
    nm = nm.reshape(nm.shape[0], -1, nm.shape[3])
    cols = edge_mats.shape[3]
    at = lax.axis_index("width") * cols
    found = []
    for kind, mats, back in (("e", em[0], eb[0]), ("n", nm[0], nb[0])):
        found.append(Whole([lax.dynamic_slice_in_dim(mats, at, cols, 1), lax.dynamic_slice_in_dim(back, at, cols, 0)], kind))
    return found + [Whole([em[block], eb[block], nm[block], nb[block]]) for block in range(1, em.shape[0])]


def on_device(
    grid_latent,
    mesh_latent,
    grid_edge,
    mesh_edge,
    encoder_slot,
    encoder_target,
    halo_down,
    halo_up,
    send_lists,
    mesh_slot,
    mesh_target,
    edge_mats,
    node_mats,
    edge_back,
    node_back,
):
    depth = grid_latent.shape[1]
    nodes = mesh_latent.shape[0]
    grid_edges, mesh_edges = grid_edge.shape[0], mesh_edge.shape[0]
    sizes = [lax.axis_size(name) for name in ("groups", "mesh", "band", "width")]
    by_parts = sizes == [2, 4, 2, 2] and edge_mats.shape[0] == 3
    halo = halo_down.shape[0]
    line = sizes[1] * sizes[2]
    sent_rows = send_lists.shape[1] * send_lists.shape[2]
    hidden = edge_mats.shape[3] * sizes[3]
    lists = send_lists.reshape(1, -1)
    lists_back = send_lists[:, ::-1].reshape(1, -1)
    node_buffer, edge_buffer = pltpu.VMEM((nodes, depth), BF), pltpu.VMEM((mesh_edges, depth), BF)

    lent_down, lent_up = call(
        lend_body,
        [(halo, depth), (halo, depth)],
        [pltpu.VMEM(grid_latent.shape, BF)] + [pltpu.VMEM((1, halo), jnp.int32)] * 2 + [pltpu.SemaphoreType.DMA((3,))],
        [],
        [grid_latent, halo_down[None, :], halo_up[None, :]],
    )
    if by_parts:
        raws = [edge_mats, edge_back, node_mats, node_back]
        slab = edge_mats.shape[2]
        quarter = slab // 4
        [cut0] = cut([((0,), "quarter", quarter)], raws)
        cut12, own0, own1, own2 = cut([((1, 2), "quarter", quarter)] + [((block,), "whole", slab) for block in range(3)], raws)
        turned0 = over_slices(cut0)
        lent_down, lent_up = after(lent_down, turned0[0]), after(lent_up, turned0[0])
    from_upper = lax.ppermute(lent_down, ("mesh", "band"), [(i + 1, i) for i in range(line - 1)])
    from_lower = lax.ppermute(lent_up, ("mesh", "band"), [(i, i + 1) for i in range(line - 1)])
    if by_parts:
        [joined0] = join(turned0[:-1] + [after(turned0[-1], from_upper, from_lower, cut12)], 1)
        plane0 = over_plane(joined0)
        side0 = [own0, joined0] + plane0
        joined1, joined2 = join(over_slices(after(cut12, joined0)), 2, 3.0)
    else:
        packs = weights_whole(edge_mats, node_mats, edge_back, node_back)
    gathered = call(
        gather_body,
        (grid_edges, 3 * depth),
        [pltpu.SemaphoreType.DMA(())],
        [grid_latent, from_lower, from_upper, mesh_latent, encoder_slot[None, :], encoder_target[None, :]],
        [grid_edge],
        cost=1.2,
    )
    if by_parts:
        packs = [Parts([[after(own0, joined1)] + side0[1:]], [])]
    pack = packs[0]
    term, *node_weights = call(
        functools.partial(half_edges_body, pack),
        [((grid_edges, depth), BF)] + [(shape, BF) for shape in (weight_shapes("n", hidden // 2, depth) if by_parts else [])],
        [pltpu.SemaphoreType.DMA((2,))] + pack.scratch(hidden // 2, depth),
        [gathered] + pack.near_operands,
        cost=3.0,
        far=2 if by_parts else 0,
    )
    if by_parts:
        plane1 = over_plane(after(joined1, term))
    else:
        node_weights = packs[1].near_operands
    before = term
    term = call(
        half_nodes_body,
        (nodes, depth),
        [pltpu.VMEM((grid_edges, depth), BF), node_buffer]
        + [pltpu.VMEM(shape, BF) for shape in weight_shapes("n", hidden // 2, depth)]
        + [pltpu.SemaphoreType.DMA((3,))],
        [encoder_target[None, :], term, swap_width(term)],
        [mesh_latent] + node_weights,
        cost=1.6,
    )
    packed, rows = call(
        first_next_body,
        [(sent_rows, depth), (nodes, depth)],
        [node_buffer, pltpu.SemaphoreType.DMA(())],
        [mesh_latent, lists_back, term, swap_width(term), mark(term, 5.0)],
        cost=1.6,
        far=1,
    )
    edges = mesh_edge
    slots, targets = mesh_slot[None, :], mesh_target[None, :]
    room = send_lists.shape[2]
    slots_back = ((line - 1 - mesh_slot // room) * room + mesh_slot % room)[None, :]
    for block in range(1, edge_mats.shape[0]):
        last = block == edge_mats.shape[0] - 1
        cut_rows = packed.reshape(send_lists.shape[1:] + (depth,))
        order = [list(reversed(range(line)))]
        sent = lax.all_to_all(
            cut_rows, ("mesh", "band"), split_axis=0, concat_axis=0, axis_index_groups=order, tiled=True
        ).reshape(-1, depth)
        if by_parts:
            if not last:
                plane2 = over_plane(after(joined2, sent))
                side = [own1, joined1] + plane1
            else:
                side = [own2, joined2] + plane2
            other = [swap_width(after(a, before)) for a in side[:2]] + [swap_width(after(a, sent)) for a in side[2:]]
            pack = Parts([side, other], range(7))
            before = sent
        else:
            pack = packs[block + 1]
        if by_parts and last:
            half = hidden // 2
            mine, there = Parts([side], range(5)), Parts([other], [])
            table = pltpu.VMEM((depth + nodes + sent_rows, half), BF)
            total, *kept = call(
                functools.partial(own_half_body, mine),
                [((mesh_edges, depth), F32)]
                + [(shape, BF) for shape in weight_shapes("n", half, depth) + [other[0].shape, other[1].shape]]
                + [((nodes, depth), BF), ((mesh_edges, depth), BF)],
                [table, pltpu.SemaphoreType.DMA((4,))] + mine.scratch(half, depth),
                [sent, slots_back, targets],
                [rows, edges],
                side + other[:2],
                cost=3.5,
            )
            nm, nb, own_there, joined_there, node_rows, edge_rows = kept
            return call(
                functools.partial(other_half_body, there),
                (nodes, depth),
                [edge_buffer, table] + there.scratch(half, depth),
                [sent, slots_back, targets, total, nm, nb, node_rows, edge_rows, own_there, joined_there] + other[2:],
                cost=3.5,
                keep=False,
            )
        table = pltpu.VMEM((depth + nodes + sent_rows, hidden), BF)
        got = call(
            functools.partial(block_body, pack, last),
            (nodes, depth) if last else [(sent_rows, depth), (nodes, depth), (mesh_edges, depth)],
            [edge_buffer, table, node_buffer, edge_buffer, pltpu.SemaphoreType.DMA((4,))] + pack.scratch(hidden, depth),
            [sent, slots_back, targets, lists_back] + pack.near_operands,
            [rows, edges] + pack.far_operands,
            cost=6.5,
            far=0 if last else 2,
            keep=not last,
        )
        if last:
            rows = got
        else:
            packed, rows, edges = got
    return rows


def solution(mesh):
    return jax.shard_map(
        on_device,
        mesh=mesh,
        in_specs=(
            P(("groups", "mesh", "band"), None),
            P(("groups", "mesh", "band"), None),
            P(("groups", "mesh", "band"), None),
            P(("groups", "mesh", "band"), None),
            P(("groups", "mesh", "band")),
            P(("groups", "mesh", "band")),
            P(("groups", "mesh", "band")),
            P(("groups", "mesh", "band")),
            P(("groups", "mesh", "band"), None, None),
            P(("groups", "mesh", "band")),
            P(("groups", "mesh", "band")),
            P(None, None, "mesh", "width"),
            P(None, None, "mesh", "width"),
            P(None, "width", "mesh"),
            P(None, "width", "mesh"),
        ),
        out_specs=P(("groups", "mesh", "band"), None),
        check_vma=False,
    )
```

```python
import functools

import jax
import jax.numpy as jnp
from jax import lax
from jax.experimental import pallas as pl
from jax.experimental.pallas import tpu as pltpu
from jax.sharding import PartitionSpec as P

BF = jnp.bfloat16
F32 = jnp.float32
ROWS = 384
SWAP = [(0, 1), (1, 0)]
DIAGONAL = [(0, 3), (3, 0), (1, 2), (2, 1)]
LIMIT = 28 * 2**20


def dot(a, b):
    return jnp.dot(a, b, preferred_element_type=F32)


def silu(v):
    return v * (0.5 * jnp.tanh(0.5 * v) + 0.5)


def normalize(total):
    mean = jnp.mean(total, axis=1, keepdims=True)
    meansq = jnp.mean(total * total, axis=1, keepdims=True)
    return (total - mean) * lax.rsqrt(meansq - mean * mean + 1e-05)


def columns_of(ids):
    return jnp.broadcast_to(ids, (128, ids.shape[1])).T


def one_hot(ids, count):
    spread_ids = columns_of(ids)
    pieces = []
    for at in range(0, count, 128):
        width = min(128, count - at)
        spots = lax.broadcasted_iota(jnp.int32, (ids.shape[1], width), 1) + at
        pieces.append(jnp.where(spots == spread_ids[:, :width], 1.0, 0.0).astype(BF))
    return jnp.concatenate(pieces, axis=1) if len(pieces) > 1 else pieces[0]


def one_hot_rows(ids, count):
    spots = lax.broadcasted_iota(jnp.int32, (count, ids.shape[1]), 0)
    return jnp.where(spots == ids, 1.0, 0.0).astype(BF)


def call(body, outs, scratch, fast, slow=(), free=(), cost=0.5, far=0, keep=True):
    many = isinstance(outs, list)
    full = [(o if isinstance(o[1], tuple) or not isinstance(o[0], int) else (o, BF)) for o in (outs if many else [outs])]
    places = [pltpu.VMEM] * (len(full) - far) + [pltpu.HBM] * far
    shapes = [(place if keep else jax.ShapeDtypeStruct)(shape, dtype) for place, (shape, dtype) in zip(places, full)]
    operands = [pltpu.with_memory_space_constraint(a, pltpu.VMEM) for a in fast]
    operands += [pltpu.with_memory_space_constraint(a, pltpu.HBM) for a in slow]
    operands += list(free)
    specs = [pl.BlockSpec(memory_space=pltpu.VMEM)] * len(fast) + [pl.BlockSpec(memory_space=pltpu.HBM)] * len(slow)
    specs += [pl.BlockSpec(memory_space=pl.ANY)] * len(free)
    return pl.pallas_call(
        body,
        out_shape=shapes if many else shapes[0],
        in_specs=specs,
        out_specs=[pl.BlockSpec(memory_space=place) for place in places] if many else pl.BlockSpec(memory_space=places[0]),
        scratch_shapes=scratch,
        compiler_params=pltpu.CompilerParams(vmem_limit_bytes=LIMIT),
        cost_estimate=pl.CostEstimate(flops=int(cost * 1e9), bytes_accessed=0, transcendentals=0),
    )(*operands)


def after(array, *others):
    return lax.optimization_barrier((array,) + others)[0]


MATS = {"e": 3, "n": 2}


def arrays_in(kind):
    return sum(MATS[letter] + 1 for letter in kind)


def weight_shapes(kind, hidden, depth):
    found = []
    for letter in kind:
        found += [(MATS[letter] * depth, hidden), (hidden, depth)]
    return found


def named(kind, refs):
    return dict(zip([letter + name for letter in kind for name in "mb"], refs))


def cut_body(plan, *refs):
    raws = (refs[0], refs[1]), (refs[2], refs[3])
    outs, sem = refs[4:-1], refs[-1]
    part = {"quarter": 2 * lax.axis_index("groups") + lax.axis_index("band"), "whole": 0}
    copies = []
    for (blocks, split, rows), out in zip(plan, outs):
        spot = 0
        for block in blocks:
            for mats, back in raws:
                lanes, count = back.shape[2], mats.shape[1]
                first = pl.ds(pl.multiple_of(part[split] * rows, rows), rows)
                copies.append((mats.at[block, :, first, :], out.at[spot : spot + count]))
                spot += count
                for j in range(2):
                    at = pl.ds(pl.multiple_of(part[split] * 2 * rows + j * rows, rows), rows)
                    copies.append((back.at[block, at, :], out.at[spot, :, j * lanes : (j + 1) * lanes]))
                spot += 1
    started = [pltpu.make_async_copy(src, dst, sem.at[i]) for i, (src, dst) in enumerate(copies)]
    for copy in started:
        copy.start()
    for copy in started:
        copy.wait()


def cut(plan, raws):
    shapes = [(arrays_in("en") * len(blocks), rows, raws[0].shape[3]) for blocks, _, rows in plan]
    copies = sum(6 * len(blocks) for blocks, _, _ in plan)
    return call(functools.partial(cut_body, plan), shapes, [pltpu.SemaphoreType.DMA((copies,))], [], raws)


def put(src, zs, part, half, kind, weights):
    def piece(k, spot):
        return src.at[spot] if len(src.shape) == 3 else src.at[k, spot]

    rows, cols = src.shape[-2:]
    lanes = cols // 2
    spot = 0
    for letter in "en":
        if letter in kind:
            mats, back = weights[letter + "m"], weights[letter + "b"]
            depth = back.shape[1]
            for k, z in enumerate(zs):
                for m in range(MATS[letter]):
                    at = pl.multiple_of(m * depth + z * lanes + part * rows, rows)
                    mats[pl.ds(at, rows), half * cols : (half + 1) * cols] = piece(k, spot + m)[...]
                for j in range(2):
                    at = pl.multiple_of(half * cols + part * 2 * rows + j * rows, rows)
                    into = pl.ds(pl.multiple_of(z * lanes, lanes), lanes)
                    back[pl.ds(at, rows), into] = piece(k, spot + MATS[letter])[:, j * lanes : (j + 1) * lanes]
        spot += MATS[letter] + 1


class Parts:
    def __init__(self, sides, far, kind="en"):
        arrays = [array for side in sides for array in side]
        self.kind, self.sides = kind, len(sides)
        self.far = [i in far for i in range(len(arrays))]
        self.near_operands = [array for array, far in zip(arrays, self.far) if not far]
        self.far_operands = [array for array, far in zip(arrays, self.far) if far]

    def scratch(self, hidden, depth):
        found = [pltpu.VMEM(shape, BF) for shape in weight_shapes(self.kind, hidden, depth)]
        found += [pltpu.VMEM(array.shape, BF) for array in self.far_operands]
        return found + [pltpu.SemaphoreType.DMA((max(len(self.far_operands), 1),))]

    def load(self, near, far, scratch):
        weights, sems = named(self.kind, scratch), scratch[-1]
        staged = scratch[2 * len(self.kind) : -1]
        copies = [pltpu.make_async_copy(src, dst, sems.at[i]) for i, (src, dst) in enumerate(zip(far, staged))]
        for copy in copies:
            copy.start()
        sources, near, staged, waits = [], list(near), list(staged), list(copies)
        for is_far in self.far:
            sources.append((staged.pop(0), waits.pop(0)) if is_far else (near.pop(0), None))
        count = lax.axis_size("mesh")
        z = lax.axis_index("mesh")
        x, y = lax.axis_index("band"), lax.axis_index("groups")
        quarters = [2 * y + x, 2 * y + 1 - x, 2 * (1 - y) + x, 2 * (1 - y) + 1 - x]
        each = len(sources) // self.sides

        def place(kind):
            for wanted in (False, True):
                for i, (src, wait) in enumerate(sources):
                    if self.far[i] != wanted:
                        continue
                    if wait is not None and kind == "e":
                        wait.wait()
                    spot = i % each
                    if spot == 0:
                        put(src, [z], 0, i // each, kind, weights)
                    else:
                        put(src, [z ^ k for k in range(1, count)], quarters[spot - 1], i // each, kind, weights)

        return weights, place


class Whole:
    def __init__(self, arrays, kind="en"):
        self.near_operands, self.far_operands, self.kind = arrays, [], kind

    def scratch(self, hidden, depth):
        return []

    def load(self, near, far, scratch):
        return named(self.kind, near), lambda kind: None


def join_body(*refs):
    blocks = [ref for ref in refs if len(ref.shape) == 4]
    for k, ref in enumerate(refs[: -len(blocks)]):
        for i, block in enumerate(blocks):
            block[k] = ref[i * block.shape[1] : (i + 1) * block.shape[1]]


def join(arrays, blocks, cost=0.5):
    count, rows, cols = arrays[0].shape
    return call(join_body, [(len(arrays), count // blocks, rows, cols)] * blocks, [], arrays, cost=cost)


class Copies:
    def __init__(self, sems, at, *plans):
        self.each = []
        for src, dst, pieces in plans:
            rows = src.shape[0] // pieces
            cuts = [slice(i * rows, (i + 1) * rows) for i in range(pieces)]
            self.each.append([pltpu.make_async_copy(src.at[cut], dst.at[cut], sems.at[at + i]) for i, cut in enumerate(cuts)])
            at += pieces
        for copy in sum(self.each, []):
            copy.start()

    def wait(self, *which):
        for i in which:
            for copy in self.each[i]:
                copy.wait()


def lend_body(grid_in, down_in, up_in, low, high, grid, down, up, sems):
    copies = Copies(sems, 0, (down_in, down, 1), (up_in, up, 1), (grid_in, grid, 1))
    copies.wait(0, 1, 2)
    low[...] = dot(one_hot(down[...], grid.shape[0]), grid[...]).astype(BF)
    high[...] = dot(one_hot(up[...], grid.shape[0]), grid[...]).astype(BF)


def gather_body(grid, low, high, nodes, slots, targets, edges, out, sem):
    depth = grid.shape[1]
    beside = pltpu.make_async_copy(edges, out.at[:, 2 * depth :], sem)
    beside.start()
    table = jnp.concatenate([grid[...], low[...], high[...]], axis=0)
    for at in range(0, out.shape[0], ROWS):
        rows = slice(at, at + ROWS)
        out[rows, 0:depth] = dot(one_hot(slots[:, rows], table.shape[0]), table).astype(BF)
        out[rows, depth : 2 * depth] = dot(one_hot(targets[:, rows], nodes.shape[0]), nodes[...]).astype(BF)
    beside.wait()


def edges_to_nodes(weights, inputs, table, edge_buffer, targets, message, keep):
    for at in range(0, message.shape[0], ROWS):
        rows = slice(at, at + ROWS)
        pre = dot(inputs(rows), table[...])
        normed = normalize(dot(silu(pre).astype(BF), weights["eb"][...]))
        message[rows, :] = normed.astype(BF)
        if keep:
            edge_buffer[rows, :] = (edge_buffer[rows, :].astype(F32) + normed).astype(BF)


def nodes_after(weights, nodes, incoming):
    pre = dot(jnp.concatenate([nodes, incoming], axis=1), weights["nm"][...])
    return (nodes.astype(F32) + normalize(dot(silu(pre).astype(BF), weights["nb"][...]))).astype(BF)


def sum_of(terms, rows=slice(None)):
    total = terms[0][rows, :].astype(F32)
    for term in terms[1:]:
        total = total + term[rows, :].astype(F32)
    return total


def half_edges_body(pack, gathered, *refs):
    count = len(pack.near_operands)
    operands, out, refs = refs[:count], refs[count], refs[count + 1 :]
    saved, refs = (refs[:2], refs[2:]) if len(pack.kind) == 2 else ((), refs)
    sems, *scratch = refs
    weights, place = pack.load(operands, (), scratch)
    saves = []
    if saved:
        place("n")
        saves = [pltpu.make_async_copy(weights[n], to, sems.at[i]) for i, (n, to) in enumerate(zip(("nm", "nb"), saved))]
    for save in saves:
        save.start()
    place("e")
    pre = dot(gathered[...], weights["em"][...])
    out[...] = dot(silu(pre).astype(BF), weights["eb"][...]).astype(BF)
    for save in saves:
        save.wait()


def half_nodes_body(targets, mine, other, nodes_in, nm_in, nb_in, out, message, nodes, nm, nb, sems):
    pairs = ((nodes_in, nodes), (nm_in, nm), (nb_in, nb))
    fetches = [pltpu.make_async_copy(src, dst, sems.at[i]) for i, (src, dst) in enumerate(pairs)]
    for fetch in fetches:
        fetch.start()
    for at in range(0, message.shape[0], ROWS):
        rows = slice(at, at + ROWS)
        message[rows, :] = normalize(sum_of((mine, other), rows)).astype(BF)
    incoming = dot(one_hot_rows(targets[...], nodes.shape[0]), message[...]).astype(BF)
    for fetch in fetches:
        fetch.wait()
    pre = dot(jnp.concatenate([nodes[...], incoming], axis=1), nm[...])
    out[...] = dot(silu(pre).astype(BF), nb[...]).astype(BF)


def mark_body(source, out):
    out[...] = source[0 : out.shape[0], 0 : out.shape[1]]


def mark(source, cost):
    return call(mark_body, (16, 128), [], [source], cost=cost)


def first_next_body(nodes, lists, mine, other, piece, packed, out, buffer, sem):
    buffer[...] = (nodes[...].astype(F32) + normalize(sum_of((mine, other)))).astype(BF)
    save = pltpu.make_async_copy(buffer, out, sem)
    save.start()
    packed[...] = dot(one_hot(lists[...], nodes.shape[0]), buffer[...]).astype(BF)
    save.wait()


def block_body(pack, last, sent, slots, targets, lists, *refs):
    near, far = len(pack.near_operands), len(pack.far_operands)
    near, refs = refs[:near], refs[near:]
    nodes, edges, far, refs = refs[0], refs[1], refs[2 : 2 + far], refs[2 + far :]
    if last:
        (out, *refs) = refs
    else:
        (packed, saved, edges_saved, *refs) = refs
    message, table, node_buffer, edge_buffer, sems, *scratch = refs
    get_nodes = pltpu.make_async_copy(nodes, node_buffer, sems.at[0])
    get_edges = pltpu.make_async_copy(edges, edge_buffer, sems.at[1])
    get_nodes.start()
    get_edges.start()
    weights, place = pack.load(near, far, scratch)
    place("e")
    em, depth, count = weights["em"], sent.shape[1], nodes.shape[0]
    table[0:depth, :] = em[2 * depth :, :]
    get_nodes.wait()
    table[depth : depth + count, :] = dot(node_buffer[...], em[depth : 2 * depth, :]).astype(BF)
    table[depth + count :, :] = dot(sent[...], em[0:depth, :]).astype(BF)
    get_edges.wait()

    def inputs(rows):
        picks = [one_hot(targets[:, rows], count), one_hot(slots[:, rows], sent.shape[0])]
        return jnp.concatenate([edge_buffer[rows, :]] + picks, axis=1)

    edges_to_nodes(weights, inputs, table, edge_buffer, targets, message, not last)
    if not last:
        save_edges = pltpu.make_async_copy(edge_buffer, edges_saved, sems.at[2])
        save_edges.start()
    place("n")
    incoming = dot(one_hot_rows(targets[...], count), message[...]).astype(BF)
    new = nodes_after(weights, node_buffer[...], incoming)
    if last:
        out[...] = new
        return
    node_buffer[...] = new
    save_nodes = pltpu.make_async_copy(node_buffer, saved, sems.at[3])
    save_nodes.start()
    packed[...] = dot(one_hot(lists[...], count), new).astype(BF)
    save_edges.wait()
    save_nodes.wait()


def picks_of(targets, slots, rows, count, room):
    return [one_hot(targets[:, rows], count), one_hot(slots[:, rows], room)]


def fill_table(table, weights, nodes, sent):
    em, depth, count = weights["em"], sent.shape[1], nodes.shape[0]
    table[0:depth, :] = em[2 * depth :, :]
    table[depth : depth + count, :] = dot(nodes[...], em[depth : 2 * depth, :]).astype(BF)
    table[depth + count :, :] = dot(sent[...], em[0:depth, :]).astype(BF)


def own_half_body(pack, sent, slots, targets, nodes_in, edges_in, *refs):
    far, refs = refs[:7], refs[7:]
    total, nm, nb, own_there, joined_there, nodes, edges, table, sems, *scratch = refs
    pairs = ((nodes_in, nodes), (edges_in, edges), (far[5], own_there), (far[6], joined_there))
    copies = [pltpu.make_async_copy(src, dst, sems.at[i]) for i, (src, dst) in enumerate(pairs)]
    weights, place = pack.load((), far[:5], scratch)
    for copy in copies:
        copy.start()
    place("e")
    copies[0].wait()
    fill_table(table, weights, nodes, sent)
    copies[1].wait()
    for at in range(0, edges.shape[0], edges.shape[0]):
        rows = slice(at, at + edges.shape[0])
        picks = picks_of(targets, slots, rows, nodes.shape[0], sent.shape[0])
        pre = dot(jnp.concatenate([edges[rows, :]] + picks, axis=1), table[...])
        total[rows, :] = dot(silu(pre).astype(BF), weights["eb"][...])
    place("n")
    nm[...] = weights["nm"][...]
    nb[...] = weights["nb"][...]
    copies[2].wait()
    copies[3].wait()


def other_half_body(pack, sent, slots, targets, total, nm, nb, nodes, edges, *refs):
    near, out, message, table, scratch = refs[:5], refs[5], refs[6], refs[7], refs[8:]
    weights, place = pack.load(near, (), scratch)
    place("e")
    fill_table(table, weights, nodes, sent)
    for at in range(0, edges.shape[0], edges.shape[0]):
        rows = slice(at, at + edges.shape[0])
        picks = picks_of(targets, slots, rows, nodes.shape[0], sent.shape[0])
        pre = dot(jnp.concatenate([edges[rows, :]] + picks, axis=1), table[...])
        sums = total[rows, :] + dot(silu(pre).astype(BF), weights["eb"][...])
        message[rows, :] = normalize(sums).astype(BF)
    place("n")
    incoming = dot(one_hot_rows(targets[...], nodes.shape[0]), message[...]).astype(BF)
    both = jnp.concatenate([nodes[...], incoming], axis=1)
    sums = dot(silu(dot(both, nm[...])).astype(BF), nb[...])
    sums = sums + dot(silu(dot(both, weights["nm"][...])).astype(BF), weights["nb"][...])
    out[...] = (nodes[...].astype(F32) + normalize(sums)).astype(BF)


def over_slices(chunk):
    count = lax.axis_size("mesh")
    return [lax.ppermute(chunk, "mesh", [(i, i ^ k) for i in range(count)]) for k in range(1, count)]


def over_plane(own):
    across = lax.ppermute(own, ("groups", "band"), DIAGONAL)
    along_y = lax.ppermute(own, "groups", SWAP)
    along_x = lax.ppermute(own, "band", SWAP)
    return [along_x, along_y, across]


def swap_width(array):
    return lax.ppermute(array, "width", SWAP)


def weights_whole(edge_mats, node_mats, edge_back, node_back):
    def joined(array, rows, cols):
        axis = {rows: array.ndim - 2, cols: array.ndim - 1}
        for name in ("mesh", "width"):
            array = lax.all_gather(array, name, axis=axis[name], tiled=True)
        return array

    em, nm = joined(edge_mats, "mesh", "width"), joined(node_mats, "mesh", "width")
    eb, nb = joined(edge_back, "width", "mesh"), joined(node_back, "width", "mesh")
    em = em.reshape(em.shape[0], -1, em.shape[3])
    nm = nm.reshape(nm.shape[0], -1, nm.shape[3])
    cols = edge_mats.shape[3]
    at = lax.axis_index("width") * cols
    found = []
    for kind, mats, back in (("e", em[0], eb[0]), ("n", nm[0], nb[0])):
        found.append(Whole([lax.dynamic_slice_in_dim(mats, at, cols, 1), lax.dynamic_slice_in_dim(back, at, cols, 0)], kind))
    return found + [Whole([em[block], eb[block], nm[block], nb[block]]) for block in range(1, em.shape[0])]


def on_device(
    grid_latent,
    mesh_latent,
    grid_edge,
    mesh_edge,
    encoder_slot,
    encoder_target,
    halo_down,
    halo_up,
    send_lists,
    mesh_slot,
    mesh_target,
    edge_mats,
    node_mats,
    edge_back,
    node_back,
):
    depth = grid_latent.shape[1]
    nodes = mesh_latent.shape[0]
    grid_edges, mesh_edges = grid_edge.shape[0], mesh_edge.shape[0]
    sizes = [lax.axis_size(name) for name in ("groups", "mesh", "band", "width")]
    by_parts = sizes == [2, 4, 2, 2] and edge_mats.shape[0] == 3
    halo = halo_down.shape[0]
    line = sizes[1] * sizes[2]
    sent_rows = send_lists.shape[1] * send_lists.shape[2]
    hidden = edge_mats.shape[3] * sizes[3]
    lists = send_lists.reshape(1, -1)
    lists_back = send_lists[:, ::-1].reshape(1, -1)
    node_buffer, edge_buffer = pltpu.VMEM((nodes, depth), BF), pltpu.VMEM((mesh_edges, depth), BF)

    lent_down, lent_up = call(
        lend_body,
        [(halo, depth), (halo, depth)],
        [pltpu.VMEM(grid_latent.shape, BF)] + [pltpu.VMEM((1, halo), jnp.int32)] * 2 + [pltpu.SemaphoreType.DMA((3,))],
        [],
        [grid_latent, halo_down[None, :], halo_up[None, :]],
    )
    if by_parts:
        raws = [edge_mats, edge_back, node_mats, node_back]
        slab = edge_mats.shape[2]
        quarter = slab // 4
        [cut0] = cut([((0,), "quarter", quarter)], raws)
        cut12, own0, own1, own2 = cut([((1, 2), "quarter", quarter)] + [((block,), "whole", slab) for block in range(3)], raws)
        turned0 = over_slices(cut0)
        lent_down, lent_up = after(lent_down, cut0), after(lent_up, cut0)
    from_upper = lax.ppermute(lent_down, ("mesh", "band"), [(i + 1, i) for i in range(line - 1)])
    from_lower = lax.ppermute(lent_up, ("mesh", "band"), [(i, i + 1) for i in range(line - 1)])
    if by_parts:
        [joined0] = join(turned0[:-1] + [after(turned0[-1], from_upper, from_lower, cut12)], 1)
        plane0 = over_plane(joined0)
        side0 = [own0, joined0] + plane0
        joined1, joined2 = join(over_slices(after(cut12, joined0)), 2, 3.0)
    else:
        packs = weights_whole(edge_mats, node_mats, edge_back, node_back)
    gathered = call(
        gather_body,
        (grid_edges, 3 * depth),
        [pltpu.SemaphoreType.DMA(())],
        [grid_latent, from_lower, from_upper, mesh_latent, encoder_slot[None, :], encoder_target[None, :]],
        [grid_edge],
        cost=1.2,
    )
    if by_parts:
        packs = [Parts([[after(own0, joined1)] + side0[1:]], [])]
    pack = packs[0]
    term, *node_weights = call(
        functools.partial(half_edges_body, pack),
        [((grid_edges, depth), BF)] + [(shape, BF) for shape in (weight_shapes("n", hidden // 2, depth) if by_parts else [])],
        [pltpu.SemaphoreType.DMA((2,))] + pack.scratch(hidden // 2, depth),
        [gathered] + pack.near_operands,
        cost=3.0,
        far=2 if by_parts else 0,
    )
    if by_parts:
        plane1 = over_plane(after(joined1, term))
    else:
        node_weights = packs[1].near_operands
    before = gathered
    term = call(
        half_nodes_body,
        (nodes, depth),
        [pltpu.VMEM((grid_edges, depth), BF), node_buffer]
        + [pltpu.VMEM(shape, BF) for shape in weight_shapes("n", hidden // 2, depth)]
        + [pltpu.SemaphoreType.DMA((3,))],
        [encoder_target[None, :], term, swap_width(term)],
        [mesh_latent] + node_weights,
        cost=1.6,
    )
    packed, rows = call(
        first_next_body,
        [(sent_rows, depth), (nodes, depth)],
        [node_buffer, pltpu.SemaphoreType.DMA(())],
        [mesh_latent, lists_back, term, swap_width(term), mark(term, 5.0)],
        cost=1.6,
        far=1,
    )
    edges = mesh_edge
    slots, targets = mesh_slot[None, :], mesh_target[None, :]
    room = send_lists.shape[2]
    slots_back = ((line - 1 - mesh_slot // room) * room + mesh_slot % room)[None, :]
    for block in range(1, edge_mats.shape[0]):
        last = block == edge_mats.shape[0] - 1
        cut_rows = packed.reshape(send_lists.shape[1:] + (depth,))
        order = [list(reversed(range(line)))]
        sent = lax.all_to_all(
            cut_rows, ("mesh", "band"), split_axis=0, concat_axis=0, axis_index_groups=order, tiled=True
        ).reshape(-1, depth)
        if by_parts:
            if not last:
                plane2 = over_plane(after(joined2, sent))
                side = [own1, joined1] + plane1
            else:
                side = [own2, joined2] + plane2
            other = [swap_width(after(a, before)) for a in side[:2]] + [swap_width(after(a, sent)) for a in side[2:]]
            pack = Parts([side, other], range(7))
            before = sent
        else:
            pack = packs[block + 1]
        if by_parts and last:
            half = hidden // 2
            mine, there = Parts([side], range(5)), Parts([other], [])
            table = pltpu.VMEM((depth + nodes + sent_rows, half), BF)
            total, *kept = call(
                functools.partial(own_half_body, mine),
                [((mesh_edges, depth), F32)]
                + [(shape, BF) for shape in weight_shapes("n", half, depth) + [other[0].shape, other[1].shape]]
                + [((nodes, depth), BF), ((mesh_edges, depth), BF)],
                [table, pltpu.SemaphoreType.DMA((4,))] + mine.scratch(half, depth),
                [sent, slots_back, targets],
                [rows, edges],
                side + other[:2],
                cost=3.5,
            )
            nm, nb, own_there, joined_there, node_rows, edge_rows = kept
            return call(
                functools.partial(other_half_body, there),
                (nodes, depth),
                [edge_buffer, table] + there.scratch(half, depth),
                [sent, slots_back, targets, total, nm, nb, node_rows, edge_rows, own_there, joined_there] + other[2:],
                cost=3.5,
                keep=False,
            )
        table = pltpu.VMEM((depth + nodes + sent_rows, hidden), BF)
        got = call(
            functools.partial(block_body, pack, last),
            (nodes, depth) if last else [(sent_rows, depth), (nodes, depth), (mesh_edges, depth)],
            [edge_buffer, table, node_buffer, edge_buffer, pltpu.SemaphoreType.DMA((4,))] + pack.scratch(hidden, depth),
            [sent, slots_back, targets, lists_back] + pack.near_operands,
            [rows, edges] + pack.far_operands,
            cost=6.5,
            far=0 if last else 2,
            keep=not last,
        )
        if last:
            rows = got
        else:
            packed, rows, edges = got
    return rows


def solution(mesh):
    return jax.shard_map(
        on_device,
        mesh=mesh,
        in_specs=(
            P(("groups", "mesh", "band"), None),
            P(("groups", "mesh", "band"), None),
            P(("groups", "mesh", "band"), None),
            P(("groups", "mesh", "band"), None),
            P(("groups", "mesh", "band")),
            P(("groups", "mesh", "band")),
            P(("groups", "mesh", "band")),
            P(("groups", "mesh", "band")),
            P(("groups", "mesh", "band"), None, None),
            P(("groups", "mesh", "band")),
            P(("groups", "mesh", "band")),
            P(None, None, "mesh", "width"),
            P(None, None, "mesh", "width"),
            P(None, "width", "mesh"),
            P(None, "width", "mesh"),
        ),
        out_specs=P(("groups", "mesh", "band"), None),
        check_vma=False,
    )
```

```python
import functools

import jax
import jax.numpy as jnp
from jax import lax
from jax.experimental import pallas as pl
from jax.experimental.pallas import tpu as pltpu
from jax.sharding import PartitionSpec as P

BF = jnp.bfloat16
F32 = jnp.float32
ROWS = 384
SWAP = [(0, 1), (1, 0)]
DIAGONAL = [(0, 3), (3, 0), (1, 2), (2, 1)]
LIMIT = 28 * 2**20


def dot(a, b):
    return jnp.dot(a, b, preferred_element_type=F32)


def silu(v):
    return v * (0.5 * jnp.tanh(0.5 * v) + 0.5)


def normalize(total):
    mean = jnp.mean(total, axis=1, keepdims=True)
    meansq = jnp.mean(total * total, axis=1, keepdims=True)
    return (total - mean) * lax.rsqrt(meansq - mean * mean + 1e-05)


def columns_of(ids):
    return jnp.broadcast_to(ids, (128, ids.shape[1])).T


def one_hot(ids, count):
    spread_ids = columns_of(ids)
    pieces = []
    for at in range(0, count, 128):
        width = min(128, count - at)
        spots = lax.broadcasted_iota(jnp.int32, (ids.shape[1], width), 1) + at
        pieces.append(jnp.where(spots == spread_ids[:, :width], 1.0, 0.0).astype(BF))
    return jnp.concatenate(pieces, axis=1) if len(pieces) > 1 else pieces[0]


def one_hot_rows(ids, count):
    spots = lax.broadcasted_iota(jnp.int32, (count, ids.shape[1]), 0)
    return jnp.where(spots == ids, 1.0, 0.0).astype(BF)


def call(body, outs, scratch, fast, slow=(), free=(), cost=0.5, far=0, keep=True):
    many = isinstance(outs, list)
    full = [(o if isinstance(o[1], tuple) or not isinstance(o[0], int) else (o, BF)) for o in (outs if many else [outs])]
    places = [pltpu.VMEM] * (len(full) - far) + [pltpu.HBM] * far
    shapes = [(place if keep else jax.ShapeDtypeStruct)(shape, dtype) for place, (shape, dtype) in zip(places, full)]
    operands = [pltpu.with_memory_space_constraint(a, pltpu.VMEM) for a in fast]
    operands += [pltpu.with_memory_space_constraint(a, pltpu.HBM) for a in slow]
    operands += list(free)
    specs = [pl.BlockSpec(memory_space=pltpu.VMEM)] * len(fast) + [pl.BlockSpec(memory_space=pltpu.HBM)] * len(slow)
    specs += [pl.BlockSpec(memory_space=pl.ANY)] * len(free)
    return pl.pallas_call(
        body,
        out_shape=shapes if many else shapes[0],
        in_specs=specs,
        out_specs=[pl.BlockSpec(memory_space=place) for place in places] if many else pl.BlockSpec(memory_space=places[0]),
        scratch_shapes=scratch,
        compiler_params=pltpu.CompilerParams(vmem_limit_bytes=LIMIT),
        cost_estimate=pl.CostEstimate(flops=int(cost * 1e9), bytes_accessed=0, transcendentals=0),
    )(*operands)


def after(array, *others):
    return lax.optimization_barrier((array,) + others)[0]


MATS = {"e": 3, "n": 2}


def arrays_in(kind):
    return sum(MATS[letter] + 1 for letter in kind)


def weight_shapes(kind, hidden, depth):
    found = []
    for letter in kind:
        found += [(MATS[letter] * depth, hidden), (hidden, depth)]
    return found


def named(kind, refs):
    return dict(zip([letter + name for letter in kind for name in "mb"], refs))


def cut_body(plan, *refs):
    raws = (refs[0], refs[1]), (refs[2], refs[3])
    outs, sem = refs[4:-1], refs[-1]
    part = {"quarter": 2 * lax.axis_index("groups") + lax.axis_index("band"), "whole": 0}
    copies = []
    for (blocks, split, rows), out in zip(plan, outs):
        spot = 0
        for block in blocks:
            for mats, back in raws:
                lanes, count = back.shape[2], mats.shape[1]
                first = pl.ds(pl.multiple_of(part[split] * rows, rows), rows)
                copies.append((mats.at[block, :, first, :], out.at[spot : spot + count]))
                spot += count
                for j in range(2):
                    at = pl.ds(pl.multiple_of(part[split] * 2 * rows + j * rows, rows), rows)
                    copies.append((back.at[block, at, :], out.at[spot, :, j * lanes : (j + 1) * lanes]))
                spot += 1
    started = [pltpu.make_async_copy(src, dst, sem.at[i]) for i, (src, dst) in enumerate(copies)]
    for copy in started:
        copy.start()
    for copy in started:
        copy.wait()


def cut(plan, raws):
    shapes = [(arrays_in("en") * len(blocks), rows, raws[0].shape[3]) for blocks, _, rows in plan]
    copies = sum(6 * len(blocks) for blocks, _, _ in plan)
    return call(functools.partial(cut_body, plan), shapes, [pltpu.SemaphoreType.DMA((copies,))], [], raws)


def put(src, zs, part, half, kind, weights):
    def piece(k, spot):
        return src.at[spot] if len(src.shape) == 3 else src.at[k, spot]

    rows, cols = src.shape[-2:]
    lanes = cols // 2
    spot = 0
    for letter in "en":
        if letter in kind:
            mats, back = weights[letter + "m"], weights[letter + "b"]
            depth = back.shape[1]
            for k, z in enumerate(zs):
                for m in range(MATS[letter]):
                    at = pl.multiple_of(m * depth + z * lanes + part * rows, rows)
                    mats[pl.ds(at, rows), half * cols : (half + 1) * cols] = piece(k, spot + m)[...]
                for j in range(2):
                    at = pl.multiple_of(half * cols + part * 2 * rows + j * rows, rows)
                    into = pl.ds(pl.multiple_of(z * lanes, lanes), lanes)
                    back[pl.ds(at, rows), into] = piece(k, spot + MATS[letter])[:, j * lanes : (j + 1) * lanes]
        spot += MATS[letter] + 1


class Parts:
    def __init__(self, sides, far, kind="en"):
        arrays = [array for side in sides for array in side]
        self.kind, self.sides = kind, len(sides)
        self.far = [i in far for i in range(len(arrays))]
        self.near_operands = [array for array, far in zip(arrays, self.far) if not far]
        self.far_operands = [array for array, far in zip(arrays, self.far) if far]

    def scratch(self, hidden, depth):
        found = [pltpu.VMEM(shape, BF) for shape in weight_shapes(self.kind, hidden, depth)]
        found += [pltpu.VMEM(array.shape, BF) for array in self.far_operands]
        return found + [pltpu.SemaphoreType.DMA((max(len(self.far_operands), 1),))]

    def load(self, near, far, scratch):
        weights, sems = named(self.kind, scratch), scratch[-1]
        staged = scratch[2 * len(self.kind) : -1]
        copies = [pltpu.make_async_copy(src, dst, sems.at[i]) for i, (src, dst) in enumerate(zip(far, staged))]
        for copy in copies:
            copy.start()
        sources, near, staged, waits = [], list(near), list(staged), list(copies)
        for is_far in self.far:
            sources.append((staged.pop(0), waits.pop(0)) if is_far else (near.pop(0), None))
        count = lax.axis_size("mesh")
        z = lax.axis_index("mesh")
        x, y = lax.axis_index("band"), lax.axis_index("groups")
        quarters = [2 * y + x, 2 * y + 1 - x, 2 * (1 - y) + x, 2 * (1 - y) + 1 - x]
        each = len(sources) // self.sides

        def place(kind):
            for wanted in (False, True):
                for i, (src, wait) in enumerate(sources):
                    if self.far[i] != wanted:
                        continue
                    if wait is not None and kind == "e":
                        wait.wait()
                    spot = i % each
                    if spot == 0:
                        put(src, [z], 0, i // each, kind, weights)
                    else:
                        put(src, [z ^ k for k in range(1, count)], quarters[spot - 1], i // each, kind, weights)

        return weights, place


class Whole:
    def __init__(self, arrays, kind="en"):
        self.near_operands, self.far_operands, self.kind = arrays, [], kind

    def scratch(self, hidden, depth):
        return []

    def load(self, near, far, scratch):
        return named(self.kind, near), lambda kind: None


def join_body(*refs):
    blocks = [ref for ref in refs if len(ref.shape) == 4]
    for k, ref in enumerate(refs[: -len(blocks)]):
        for i, block in enumerate(blocks):
            block[k] = ref[i * block.shape[1] : (i + 1) * block.shape[1]]


def join(arrays, blocks, cost=0.5):
    count, rows, cols = arrays[0].shape
    return call(join_body, [(len(arrays), count // blocks, rows, cols)] * blocks, [], arrays, cost=cost)


class Copies:
    def __init__(self, sems, at, *plans):
        self.each = []
        for src, dst, pieces in plans:
            rows = src.shape[0] // pieces
            cuts = [slice(i * rows, (i + 1) * rows) for i in range(pieces)]
            self.each.append([pltpu.make_async_copy(src.at[cut], dst.at[cut], sems.at[at + i]) for i, cut in enumerate(cuts)])
            at += pieces
        for copy in sum(self.each, []):
            copy.start()

    def wait(self, *which):
        for i in which:
            for copy in self.each[i]:
                copy.wait()


def lend_body(grid_in, down_in, up_in, low, high, grid, down, up, sems):
    copies = Copies(sems, 0, (down_in, down, 1), (up_in, up, 1), (grid_in, grid, 1))
    copies.wait(0, 1, 2)
    low[...] = dot(one_hot(down[...], grid.shape[0]), grid[...]).astype(BF)
    high[...] = dot(one_hot(up[...], grid.shape[0]), grid[...]).astype(BF)


def gather_body(grid, low, high, nodes, slots, targets, edges, out, sem):
    depth = grid.shape[1]
    beside = pltpu.make_async_copy(edges, out.at[:, 2 * depth :], sem)
    beside.start()
    table = jnp.concatenate([grid[...], low[...], high[...]], axis=0)
    for at in range(0, out.shape[0], ROWS):
        rows = slice(at, at + ROWS)
        out[rows, 0:depth] = dot(one_hot(slots[:, rows], table.shape[0]), table).astype(BF)
        out[rows, depth : 2 * depth] = dot(one_hot(targets[:, rows], nodes.shape[0]), nodes[...]).astype(BF)
    beside.wait()


def edges_to_nodes(weights, inputs, table, edge_buffer, targets, message, keep):
    for at in range(0, message.shape[0], ROWS):
        rows = slice(at, at + ROWS)
        pre = dot(inputs(rows), table[...])
        normed = normalize(dot(silu(pre).astype(BF), weights["eb"][...]))
        message[rows, :] = normed.astype(BF)
        if keep:
            edge_buffer[rows, :] = (edge_buffer[rows, :].astype(F32) + normed).astype(BF)


def nodes_after(weights, nodes, incoming):
    pre = dot(jnp.concatenate([nodes, incoming], axis=1), weights["nm"][...])
    return (nodes.astype(F32) + normalize(dot(silu(pre).astype(BF), weights["nb"][...]))).astype(BF)


def sum_of(terms, rows=slice(None)):
    total = terms[0][rows, :].astype(F32)
    for term in terms[1:]:
        total = total + term[rows, :].astype(F32)
    return total


def half_edges_body(pack, gathered, *refs):
    count = len(pack.near_operands)
    operands, out, refs = refs[:count], refs[count], refs[count + 1 :]
    saved, refs = (refs[:2], refs[2:]) if len(pack.kind) == 2 else ((), refs)
    sems, *scratch = refs
    weights, place = pack.load(operands, (), scratch)
    saves = []
    if saved:
        place("n")
        saves = [pltpu.make_async_copy(weights[n], to, sems.at[i]) for i, (n, to) in enumerate(zip(("nm", "nb"), saved))]
    for save in saves:
        save.start()
    place("e")
    pre = dot(gathered[...], weights["em"][...])
    out[...] = dot(silu(pre).astype(BF), weights["eb"][...]).astype(BF)
    for save in saves:
        save.wait()


def half_nodes_body(targets, mine, other, nodes_in, nm_in, nb_in, out, message, nodes, nm, nb, sems):
    pairs = ((nodes_in, nodes), (nm_in, nm), (nb_in, nb))
    fetches = [pltpu.make_async_copy(src, dst, sems.at[i]) for i, (src, dst) in enumerate(pairs)]
    for fetch in fetches:
        fetch.start()
    for at in range(0, message.shape[0], ROWS):
        rows = slice(at, at + ROWS)
        message[rows, :] = normalize(sum_of((mine, other), rows)).astype(BF)
    incoming = dot(one_hot_rows(targets[...], nodes.shape[0]), message[...]).astype(BF)
    for fetch in fetches:
        fetch.wait()
    pre = dot(jnp.concatenate([nodes[...], incoming], axis=1), nm[...])
    out[...] = dot(silu(pre).astype(BF), nb[...]).astype(BF)


def mark_body(source, out):
    out[...] = source[0 : out.shape[0], 0 : out.shape[1]]


def mark(source, cost):
    return call(mark_body, (16, 128), [], [source], cost=cost)


def first_next_body(nodes, lists, mine, other, piece, packed, out, buffer, sem):
    buffer[...] = (nodes[...].astype(F32) + normalize(sum_of((mine, other)))).astype(BF)
    save = pltpu.make_async_copy(buffer, out, sem)
    save.start()
    packed[...] = dot(one_hot(lists[...], nodes.shape[0]), buffer[...]).astype(BF)
    save.wait()


def block_body(pack, last, sent, slots, targets, lists, piece, *refs):
    near, far = len(pack.near_operands), len(pack.far_operands)
    near, refs = refs[:near], refs[near:]
    nodes, edges, far, refs = refs[0], refs[1], refs[2 : 2 + far], refs[2 + far :]
    if last:
        (out, *refs) = refs
    else:
        (packed, saved, edges_saved, *refs) = refs
    message, table, node_buffer, edge_buffer, sems, *scratch = refs
    get_nodes = pltpu.make_async_copy(nodes, node_buffer, sems.at[0])
    get_edges = pltpu.make_async_copy(edges, edge_buffer, sems.at[1])
    get_nodes.start()
    get_edges.start()
    weights, place = pack.load(near, far, scratch)
    place("e")
    em, depth, count = weights["em"], sent.shape[1], nodes.shape[0]
    table[0:depth, :] = em[2 * depth :, :]
    get_nodes.wait()
    table[depth : depth + count, :] = dot(node_buffer[...], em[depth : 2 * depth, :]).astype(BF)
    table[depth + count :, :] = dot(sent[...], em[0:depth, :]).astype(BF)
    get_edges.wait()

    def inputs(rows):
        picks = [one_hot(targets[:, rows], count), one_hot(slots[:, rows], sent.shape[0])]
        return jnp.concatenate([edge_buffer[rows, :]] + picks, axis=1)

    edges_to_nodes(weights, inputs, table, edge_buffer, targets, message, not last)
    if not last:
        save_edges = pltpu.make_async_copy(edge_buffer, edges_saved, sems.at[2])
        save_edges.start()
    place("n")
    incoming = dot(one_hot_rows(targets[...], count), message[...]).astype(BF)
    new = nodes_after(weights, node_buffer[...], incoming)
    if last:
        out[...] = new
        return
    node_buffer[...] = new
    save_nodes = pltpu.make_async_copy(node_buffer, saved, sems.at[3])
    save_nodes.start()
    packed[...] = dot(one_hot(lists[...], count), new).astype(BF)
    save_edges.wait()
    save_nodes.wait()


def picks_of(targets, slots, rows, count, room):
    return [one_hot(targets[:, rows], count), one_hot(slots[:, rows], room)]


def fill_table(table, weights, nodes, sent):
    em, depth, count = weights["em"], sent.shape[1], nodes.shape[0]
    table[0:depth, :] = em[2 * depth :, :]
    table[depth : depth + count, :] = dot(nodes[...], em[depth : 2 * depth, :]).astype(BF)
    table[depth + count :, :] = dot(sent[...], em[0:depth, :]).astype(BF)


def own_half_body(pack, sent, slots, targets, nodes_in, edges_in, *refs):
    far, refs = refs[:7], refs[7:]
    total, nm, nb, own_there, joined_there, nodes, edges, table, sems, *scratch = refs
    pairs = ((nodes_in, nodes), (edges_in, edges), (far[5], own_there), (far[6], joined_there))
    copies = [pltpu.make_async_copy(src, dst, sems.at[i]) for i, (src, dst) in enumerate(pairs)]
    weights, place = pack.load((), far[:5], scratch)
    for copy in copies:
        copy.start()
    place("e")
    copies[0].wait()
    fill_table(table, weights, nodes, sent)
    copies[1].wait()
    for at in range(0, edges.shape[0], edges.shape[0]):
        rows = slice(at, at + edges.shape[0])
        picks = picks_of(targets, slots, rows, nodes.shape[0], sent.shape[0])
        pre = dot(jnp.concatenate([edges[rows, :]] + picks, axis=1), table[...])
        total[rows, :] = dot(silu(pre).astype(BF), weights["eb"][...])
    place("n")
    nm[...] = weights["nm"][...]
    nb[...] = weights["nb"][...]
    copies[2].wait()
    copies[3].wait()


def other_half_body(pack, sent, slots, targets, total, nm, nb, nodes, edges, *refs):
    near, out, message, table, scratch = refs[:5], refs[5], refs[6], refs[7], refs[8:]
    weights, place = pack.load(near, (), scratch)
    place("e")
    fill_table(table, weights, nodes, sent)
    for at in range(0, edges.shape[0], edges.shape[0]):
        rows = slice(at, at + edges.shape[0])
        picks = picks_of(targets, slots, rows, nodes.shape[0], sent.shape[0])
        pre = dot(jnp.concatenate([edges[rows, :]] + picks, axis=1), table[...])
        sums = total[rows, :] + dot(silu(pre).astype(BF), weights["eb"][...])
        message[rows, :] = normalize(sums).astype(BF)
    place("n")
    incoming = dot(one_hot_rows(targets[...], nodes.shape[0]), message[...]).astype(BF)
    both = jnp.concatenate([nodes[...], incoming], axis=1)
    sums = dot(silu(dot(both, nm[...])).astype(BF), nb[...])
    sums = sums + dot(silu(dot(both, weights["nm"][...])).astype(BF), weights["nb"][...])
    out[...] = (nodes[...].astype(F32) + normalize(sums)).astype(BF)


def over_slices(chunk):
    count = lax.axis_size("mesh")
    return [lax.ppermute(chunk, "mesh", [(i, i ^ k) for i in range(count)]) for k in range(1, count)]


def over_plane(own):
    across = lax.ppermute(own, ("groups", "band"), DIAGONAL)
    along_y = lax.ppermute(own, "groups", SWAP)
    along_x = lax.ppermute(own, "band", SWAP)
    return [along_x, along_y, across]


def swap_width(array):
    return lax.ppermute(array, "width", SWAP)


def weights_whole(edge_mats, node_mats, edge_back, node_back):
    def joined(array, rows, cols):
        axis = {rows: array.ndim - 2, cols: array.ndim - 1}
        for name in ("mesh", "width"):
            array = lax.all_gather(array, name, axis=axis[name], tiled=True)
        return array

    em, nm = joined(edge_mats, "mesh", "width"), joined(node_mats, "mesh", "width")
    eb, nb = joined(edge_back, "width", "mesh"), joined(node_back, "width", "mesh")
    em = em.reshape(em.shape[0], -1, em.shape[3])
    nm = nm.reshape(nm.shape[0], -1, nm.shape[3])
    cols = edge_mats.shape[3]
    at = lax.axis_index("width") * cols
    found = []
    for kind, mats, back in (("e", em[0], eb[0]), ("n", nm[0], nb[0])):
        found.append(Whole([lax.dynamic_slice_in_dim(mats, at, cols, 1), lax.dynamic_slice_in_dim(back, at, cols, 0)], kind))
    return found + [Whole([em[block], eb[block], nm[block], nb[block]]) for block in range(1, em.shape[0])]


def on_device(
    grid_latent,
    mesh_latent,
    grid_edge,
    mesh_edge,
    encoder_slot,
    encoder_target,
    halo_down,
    halo_up,
    send_lists,
    mesh_slot,
    mesh_target,
    edge_mats,
    node_mats,
    edge_back,
    node_back,
):
    depth = grid_latent.shape[1]
    nodes = mesh_latent.shape[0]
    grid_edges, mesh_edges = grid_edge.shape[0], mesh_edge.shape[0]
    sizes = [lax.axis_size(name) for name in ("groups", "mesh", "band", "width")]
    by_parts = sizes == [2, 4, 2, 2] and edge_mats.shape[0] == 3
    halo = halo_down.shape[0]
    line = sizes[1] * sizes[2]
    sent_rows = send_lists.shape[1] * send_lists.shape[2]
    hidden = edge_mats.shape[3] * sizes[3]
    lists = send_lists.reshape(1, -1)
    lists_back = send_lists[:, ::-1].reshape(1, -1)
    node_buffer, edge_buffer = pltpu.VMEM((nodes, depth), BF), pltpu.VMEM((mesh_edges, depth), BF)

    lent_down, lent_up = call(
        lend_body,
        [(halo, depth), (halo, depth)],
        [pltpu.VMEM(grid_latent.shape, BF)] + [pltpu.VMEM((1, halo), jnp.int32)] * 2 + [pltpu.SemaphoreType.DMA((3,))],
        [],
        [grid_latent, halo_down[None, :], halo_up[None, :]],
    )
    if by_parts:
        raws = [edge_mats, edge_back, node_mats, node_back]
        slab = edge_mats.shape[2]
        quarter = slab // 4
        [cut0] = cut([((0,), "quarter", quarter)], raws)
        cut12, own0, own1, own2 = cut([((1, 2), "quarter", quarter)] + [((block,), "whole", slab) for block in range(3)], raws)
        turned0 = over_slices(cut0)
        lent_down, lent_up = after(lent_down, cut0), after(lent_up, cut0)
    from_upper = lax.ppermute(lent_down, ("mesh", "band"), [(i + 1, i) for i in range(line - 1)])
    from_lower = lax.ppermute(lent_up, ("mesh", "band"), [(i, i + 1) for i in range(line - 1)])
    if by_parts:
        [joined0] = join(turned0[:-1] + [after(turned0[-1], from_upper, from_lower, cut12)], 1)
        plane0 = over_plane(joined0)
        side0 = [own0, joined0] + plane0
        joined1, joined2 = join(over_slices(after(cut12, joined0)), 2, 3.0)
    else:
        packs = weights_whole(edge_mats, node_mats, edge_back, node_back)
    gathered = call(
        gather_body,
        (grid_edges, 3 * depth),
        [pltpu.SemaphoreType.DMA(())],
        [grid_latent, from_lower, from_upper, mesh_latent, encoder_slot[None, :], encoder_target[None, :]],
        [grid_edge],
        cost=1.2,
    )
    if by_parts:
        packs = [Parts([[after(own0, joined1)] + side0[1:]], [])]
    pack = packs[0]
    term, *node_weights = call(
        functools.partial(half_edges_body, pack),
        [((grid_edges, depth), BF)] + [(shape, BF) for shape in (weight_shapes("n", hidden // 2, depth) if by_parts else [])],
        [pltpu.SemaphoreType.DMA((2,))] + pack.scratch(hidden // 2, depth),
        [gathered] + pack.near_operands,
        cost=3.0,
        far=2 if by_parts else 0,
    )
    if by_parts:
        plane1 = over_plane(after(joined1, term))
    else:
        node_weights = packs[1].near_operands
    before = term
    term = call(
        half_nodes_body,
        (nodes, depth),
        [pltpu.VMEM((grid_edges, depth), BF), node_buffer]
        + [pltpu.VMEM(shape, BF) for shape in weight_shapes("n", hidden // 2, depth)]
        + [pltpu.SemaphoreType.DMA((3,))],
        [encoder_target[None, :], term, swap_width(term)],
        [mesh_latent] + node_weights,
        cost=1.6,
    )
    packed, rows = call(
        first_next_body,
        [(sent_rows, depth), (nodes, depth)],
        [node_buffer, pltpu.SemaphoreType.DMA(())],
        [mesh_latent, lists_back, term, swap_width(term), mark(term, 5.0)],
        cost=1.6,
        far=1,
    )
    edges = mesh_edge
    slots, targets = mesh_slot[None, :], mesh_target[None, :]
    room = send_lists.shape[2]
    slots_back = ((line - 1 - mesh_slot // room) * room + mesh_slot % room)[None, :]
    for block in range(1, edge_mats.shape[0]):
        last = block == edge_mats.shape[0] - 1
        cut_rows = packed.reshape(send_lists.shape[1:] + (depth,))
        order = [list(reversed(range(line)))]
        sent = lax.all_to_all(
            cut_rows, ("mesh", "band"), split_axis=0, concat_axis=0, axis_index_groups=order, tiled=True
        ).reshape(-1, depth)
        if by_parts:
            if not last:
                plane2 = over_plane(after(joined2, packed))
                side = [own1, joined1] + plane1
            else:
                side = [own2, joined2] + plane2
            other = [swap_width(after(a, before)) for a in side[:2]] + [swap_width(after(a, sent)) for a in side[2:]]
            pack = Parts([side, other], range(7))
            before = sent
        else:
            pack = packs[block + 1]
        if by_parts and last:
            half = hidden // 2
            mine, there = Parts([side], range(5)), Parts([other], [])
            table = pltpu.VMEM((depth + nodes + sent_rows, half), BF)
            total, *kept = call(
                functools.partial(own_half_body, mine),
                [((mesh_edges, depth), F32)]
                + [(shape, BF) for shape in weight_shapes("n", half, depth) + [other[0].shape, other[1].shape]]
                + [((nodes, depth), BF), ((mesh_edges, depth), BF)],
                [table, pltpu.SemaphoreType.DMA((4,))] + mine.scratch(half, depth),
                [sent, slots_back, targets],
                [rows, edges],
                side + other[:2],
                cost=3.5,
            )
            nm, nb, own_there, joined_there, node_rows, edge_rows = kept
            return call(
                functools.partial(other_half_body, there),
                (nodes, depth),
                [edge_buffer, table] + there.scratch(half, depth),
                [sent, slots_back, targets, total, nm, nb, node_rows, edge_rows, own_there, joined_there] + other[2:],
                cost=3.5,
                keep=False,
            )
        table = pltpu.VMEM((depth + nodes + sent_rows, hidden), BF)
        got = call(
            functools.partial(block_body, pack, last),
            (nodes, depth) if last else [(sent_rows, depth), (nodes, depth), (mesh_edges, depth)],
            [edge_buffer, table, node_buffer, edge_buffer, pltpu.SemaphoreType.DMA((4,))] + pack.scratch(hidden, depth),
            [sent, slots_back, targets, lists_back, mark(sent, 8.0)] + pack.near_operands,
            [rows, edges] + pack.far_operands,
            cost=6.5,
            far=0 if last else 2,
            keep=not last,
        )
        if last:
            rows = got
        else:
            packed, rows, edges = got
    return rows


def solution(mesh):
    return jax.shard_map(
        on_device,
        mesh=mesh,
        in_specs=(
            P(("groups", "mesh", "band"), None),
            P(("groups", "mesh", "band"), None),
            P(("groups", "mesh", "band"), None),
            P(("groups", "mesh", "band"), None),
            P(("groups", "mesh", "band")),
            P(("groups", "mesh", "band")),
            P(("groups", "mesh", "band")),
            P(("groups", "mesh", "band")),
            P(("groups", "mesh", "band"), None, None),
            P(("groups", "mesh", "band")),
            P(("groups", "mesh", "band")),
            P(None, None, "mesh", "width"),
            P(None, None, "mesh", "width"),
            P(None, "width", "mesh"),
            P(None, "width", "mesh"),
        ),
        out_specs=P(("groups", "mesh", "band"), None),
        check_vma=False,
    )
```
